256 devices in a mesh: batch: 2 (over x_lo), ctx: 16 (over z, x_hi), tp: 8 (over y, core).
Axes of the slice: x: 4 (x_hi: 2, x_lo: 2; x = x_hi * 2 + x_lo), y: 4, z: 8, core: 2. Of those that a mesh axis runs over, the one named last changes fastest.
Arguments:
- tokens: bfloat16 [2, 4096, 1024], P('batch', 'ctx'), may hold values from -10.5 to 10.5
- query_weight: bfloat16 [1024, 1024], P(None, 'tp'), may hold values from -0.1875 to 0.1875
- key_weight: bfloat16 [1024, 1024], P(None, 'tp'), may hold values from -0.1875 to 0.1875
- value_weight: bfloat16 [1024, 1024], P(None, 'tp'), may hold values from -0.1875 to 0.1875
- cotangent: bfloat16 [2, 4096, 1024], P('batch', 'ctx', 'tp'), may hold values from -6 to 6
- doc_lengths: int32 [2, 8], P('batch'), may hold values from 1 to 3072, 4096 in all within a row
- global_positions: int32 [2, 256], P('batch'), may hold values from 0 to 4095, as said below
Outputs:
- attended: bfloat16 [2, 4096, 1024], P('batch', 'ctx', 'tp')
- grad_tokens: bfloat16 [2, 4096, 1024], P('batch', ('ctx', 'tp'))
- grad_query_weight: float32 [1024, 1024], P(None, 'tp')
- grad_key_weight: float32 [1024, 1024], P(None, 'tp')
- grad_value_weight: float32 [1024, 1024], P(None, 'tp')
The draws below stay inside these ranges and needn't reach their ends.
Inputs may be any that keep to these rules, and one draw needn't show every extreme that they name: `global_positions`: distinct positions of the sequence in ascending order; the first position 0 and the last position 4095 are always among them.
All inputs are finite; a program needn't handle non-finite values.
Results may differ from the reference program's by a relative error of at most 0.022.
The reference program's roundings to bfloat16 on the way count: a program that leaves them out, or rounds other values in their place, can miss the bound.
Values may be sent and summed in bfloat16 or wider, within the bound.
No kernel may reach another device: no remote copies, remote signals or barrier semaphores. Data moves between devices by JAX's collectives and lax.ppermute only.
A program may use at most 64 MiB of HBM per device.

```python
import math
import jax
import jax.numpy as jnp
import numpy as np
from jax import lax

D = 1024
H = 16
WINDOW = 512
HD = 64
TOK_DEV = 256
G = 256
NDOC = 8
SEQ = 4096
SEQS = 2


def draw_tokens(key, part):
    first_key = jax.random.fold_in(key, 0)
    drawn = jnp.clip(jax.random.normal(first_key, (SEQS, SEQ, D), jnp.float32), -6.0, 6.0)
    return drawn.astype(jnp.bfloat16)


def global_row(row_key):
    first_key, second_key = jax.random.split(row_key)
    hot_blocks = jax.random.randint(first_key, (SEQ // TOK_DEV,), 0, 3) == 0
    positions = jnp.arange(SEQ, dtype=jnp.int32)
    ranking = jax.random.randint(second_key, (SEQ,), 0, 1024) + jnp.where(hot_blocks[positions // TOK_DEV], 1024, 0)
    ranking = ranking * SEQ + (SEQ - 1 - positions)
    ranking = jnp.where(positions == 0, 4096 * SEQ, ranking)
    ranking = jnp.where(positions == SEQ - 1, 4096 * SEQ + 1, ranking).astype(jnp.int32)
    chosen = lax.top_k(ranking, G)[1]
    return jnp.sort(chosen).astype(jnp.int32)


def draw_global_positions(key, part):
    return jax.vmap(global_row)(jax.random.split(key, SEQS))


def steps_of(rng, shape, pieces, least, top_value):
    gain = 1.0
    for position, parts in pieces:
        steps = jax.random.uniform(jax.random.fold_in(jax.random.fold_in(rng, 6), position), (parts,), jnp.float32, least / len(pieces), top_value / len(pieces))
        gain = gain * jnp.repeat(jnp.exp(steps), shape[position] // parts).reshape((-1,) + (1,) * (len(shape) - 1 - position))
    return gain


def profile(count, total, reach, skew):
    weights = [(1 << 20) // math.isqrt(rank ** skew) + 1 for rank in range(2, count + 1)]
    spare, holding = total - reach - (count - 1), [1] * (count - 1)
    while spare > 0:
        candidates = [i for i in range(count - 1) if holding[i] < reach]
        pool, remaining = sum([weights[i] for i in candidates]), spare
        for i in candidates:
            addition = min(reach - holding[i], max(1, remaining * weights[i] // pool), spare)
            holding[i] = holding[i] + addition
            spare = spare - addition
    return np.array([reach] + holding)


def uneven_parts(stream_key, amount, total, most, slope):
    if amount == 2:
        one = jax.random.randint(stream_key, (), max(1, total - most), min(most, total - 1) + 1)
        return jnp.stack([one, total - one])
    tallies = jnp.asarray(profile(amount, total, most, slope), jnp.int32)
    couples = (amount - 1) // 2
    giver, receiver = tallies[1:1 + 2 * couples:2], tallies[2:2 + 2 * couples:2]
    room = jnp.minimum(giver - 1, most - receiver)
    moved = jax.random.randint(jax.random.fold_in(stream_key, 1), (couples,), 0, 1 << 20) % (room + 1)
    tallies = tallies.at[1:1 + 2 * couples:2].set(giver - moved).at[2:2 + 2 * couples:2].set(receiver + moved)
    return tallies[jax.random.permutation(jax.random.fold_in(stream_key, 2), amount)]


def normal_values(stream_key, extent, deviation, most, cuts=(), kind=jnp.bfloat16):
    values = jax.random.normal(stream_key, extent, jnp.float32) * deviation
    if len(cuts) > 0:
        values = steps_of(stream_key, extent, cuts, -0.22, 0.18) * values
    return jnp.clip(values, min=-most, max=most).astype(kind)


def setup_inputs(seed: int = 0) -> dict:
    streams_of = jax.random.split(jax.random.key(seed), 8)
    return {
        "tokens": draw_tokens(jax.random.fold_in(streams_of[7], 71), 0),
        "query_weight": normal_values(streams_of[1], (D, H * HD), D ** -0.5, 0.1875, ((1, 8),)),
        "key_weight": normal_values(streams_of[2], (D, H * HD), D ** -0.5, 0.1875, ((1, 8),)),
        "value_weight": normal_values(streams_of[3], (D, H * HD), D ** -0.5, 0.1875, ((1, 8),)),
        "cotangent": normal_values(streams_of[4], (SEQS, SEQ, H * HD), 1.0, 6.0, ((0, 2), (1, 16), (2, 8))),
        "doc_lengths": jax.vmap(lambda own: uneven_parts(own, NDOC, SEQ, 3 * SEQ // 4, 2))(jax.random.split(streams_of[5], SEQS)).reshape((SEQS, NDOC)).astype(jnp.int32),
        "global_positions": draw_global_positions(jax.random.fold_in(streams_of[7], 71), 0),
    }


NEGATIVE = -1e+30

def rounded(values):
    return lax.optimization_barrier(values.astype(jnp.bfloat16)).astype(jnp.float32)

def document_of(positions, lengths):
    ends = jnp.cumsum(lengths).astype(jnp.int32)
    return lax.optimization_barrier(jnp.sum((positions[:, None] >= ends[None, :]).astype(jnp.int32), axis=1)).astype(jnp.int32)

def combine(earlier, latter):
    row_peak = jnp.maximum(earlier[0], latter[0])
    scale_first = jnp.exp(earlier[0] - row_peak)
    scale_second = jnp.exp(latter[0] - row_peak)
    row_total = scale_first * earlier[1] + scale_second * latter[1]
    weighted = scale_first[..., None] * earlier[2] + scale_second[..., None] * latter[2]
    return (row_peak, row_total, weighted)

def group_stats(scores, allowed, value_rows):
    masked = jnp.where(allowed[:, None, :], scores, NEGATIVE)
    row_peak = lax.optimization_barrier(jnp.max(masked, axis=2))
    expon_terms = jnp.where(allowed[:, None, :], jnp.exp(masked - row_peak[:, :, None]), 0.0)
    row_total = lax.optimization_barrier(jnp.sum(expon_terms, axis=2))
    weighted = jnp.einsum('qhk,khd->qhd', rounded(expon_terms), value_rows.astype(jnp.float32))
    return (row_peak, row_total, weighted)

def group_grads(scores, allowed, log_total, row_delta, out_grad, queries, key_rows, value_rows, score_scale):
    prob_terms = jnp.where(allowed[:, None, :], jnp.exp(scores - log_total[:, :, None]), 0.0)
    value_grad = jnp.einsum('qhk,qhd->khd', rounded(prob_terms), out_grad.astype(jnp.float32))
    prob_grad = jnp.einsum('qhd,khd->qhk', out_grad.astype(jnp.float32), value_rows.astype(jnp.float32))
    score_grad = rounded(prob_terms * (prob_grad - row_delta[:, :, None]))
    query_grad = score_scale * jnp.einsum('qhk,khd->qhd', score_grad, key_rows.astype(jnp.float32))
    key_grad = score_scale * jnp.einsum('qhk,qhd->khd', score_grad, queries.astype(jnp.float32))
    return (query_grad, key_grad, value_grad)

def one_sequence(tokens, query_weight, key_weight, value_weight, cotangent, lengths, global_spots):
    length = tokens.shape[0]
    half_span = WINDOW // 2
    block_len = min(TOK_DEV, 512)
    key_span = block_len + 2 * half_span
    score_scale = 1.0 / math.sqrt(HD)
    query_proj = jnp.dot(tokens, query_weight, preferred_element_type=jnp.float32).astype(jnp.bfloat16)
    key_proj = jnp.dot(tokens, key_weight, preferred_element_type=jnp.float32).astype(jnp.bfloat16)
    value_proj = jnp.dot(tokens, value_weight, preferred_element_type=jnp.float32).astype(jnp.bfloat16)
    queries3 = query_proj.reshape(length, H, HD)
    keys3 = key_proj.reshape(length, H, HD)
    values3 = value_proj.reshape(length, H, HD)
    cot3 = cotangent.reshape(length, H, HD)
    positions = jnp.arange(length, dtype=jnp.int32)
    doc_ids = document_of(positions, lengths)
    global_docs = document_of(global_spots, lengths)
    is_global = jnp.any(positions[:, None] == global_spots[None, :], axis=1)
    global_queries = queries3[global_spots]
    global_keys = keys3[global_spots]
    global_values = values3[global_spots]
    global_cotangent = cot3[global_spots]
    padded_keys = jnp.pad(keys3, ((half_span, half_span), (0, 0), (0, 0)))
    padded_values = jnp.pad(values3, ((half_span, half_span), (0, 0), (0, 0)))
    padded_docs = jnp.pad(doc_ids, (half_span, half_span), constant_values=-1)
    padded_global = jnp.pad(is_global, (half_span, half_span))
    offsets = jnp.arange(key_span)[None, :] - half_span - jnp.arange(block_len)[:, None]
    near_mask = jnp.abs(offsets) <= half_span
    block_ids = jnp.arange(length // block_len, dtype=jnp.int32)
    run_ids = jnp.arange(length // TOK_DEV, dtype=jnp.int32)

    def block_parts(offset):
        query_block = lax.dynamic_slice_in_dim(queries3, offset, block_len, 0)
        key_block = lax.dynamic_slice_in_dim(padded_keys, offset, key_span, 0)
        value_block = lax.dynamic_slice_in_dim(padded_values, offset, key_span, 0)
        query_docs = lax.dynamic_slice_in_dim(doc_ids, offset, block_len, 0)
        query_global = lax.dynamic_slice_in_dim(is_global, offset, block_len, 0)
        key_docs = lax.dynamic_slice_in_dim(padded_docs, offset, key_span, 0)
        key_global = lax.dynamic_slice_in_dim(padded_global, offset, key_span, 0)
        band_mask = (key_docs[None, :] == query_docs[:, None]) & near_mask & jnp.logical_not(key_global)[None, :] & jnp.logical_not(query_global)[:, None]
        global_mask = (global_docs[None, :] == query_docs[:, None]) & jnp.logical_not(query_global)[:, None]
        band_scores = jnp.einsum('qhd,khd->qhk', query_block.astype(jnp.float32), key_block.astype(jnp.float32)) * score_scale
        global_scores = jnp.einsum('qhd,khd->qhk', query_block.astype(jnp.float32), global_keys.astype(jnp.float32)) * score_scale
        return (query_block, key_block, value_block, query_global, band_mask, global_mask, band_scores, global_scores)

    def forward_block(block_index):
        offset = (block_index * block_len).astype(jnp.int32)
        query_block, key_block, value_block, query_global, band_mask, global_mask, band_scores, global_scores = block_parts(offset)
        row_peak, row_total, weighted = combine(group_stats(band_scores, band_mask, value_block), group_stats(global_scores, global_mask, global_values))
        safe_total = jnp.where(query_global[:, None], 1.0, row_total)
        return (weighted / safe_total[:, :, None], row_peak + jnp.log(safe_total))
    block_outputs, block_totals = lax.map(forward_block, block_ids)
    local_out = block_outputs.reshape(length, H, HD)
    log_total = block_totals.reshape(length, H)

    def run_scores(offset):
        key_block = lax.dynamic_slice_in_dim(keys3, offset, TOK_DEV, 0)
        value_block = lax.dynamic_slice_in_dim(values3, offset, TOK_DEV, 0)
        key_docs = lax.dynamic_slice_in_dim(doc_ids, offset, TOK_DEV, 0)
        allowed = global_docs[:, None] == key_docs[None, :]
        scores = jnp.einsum('ghd,khd->ghk', global_queries.astype(jnp.float32), key_block.astype(jnp.float32)) * score_scale
        return (key_block, value_block, allowed, scores)

    def global_forward(running, run_index):
        offset = (run_index * TOK_DEV).astype(jnp.int32)
        key_block, value_block, allowed, scores = run_scores(offset)
        return (combine(running, group_stats(scores, allowed, value_block)), None)
    initial = (jnp.full((G, H), NEGATIVE, jnp.float32), jnp.zeros((G, H), jnp.float32), jnp.zeros((G, H, HD), jnp.float32))
    (global_peak, global_total, global_weighted), _ = lax.scan(global_forward, initial, run_ids)
    global_out = (global_weighted / global_total[:, :, None]).astype(jnp.bfloat16)
    global_log_total = global_peak + jnp.log(global_total)
    attended3 = local_out.astype(jnp.bfloat16).at[global_spots].set(global_out)
    row_delta = lax.optimization_barrier(jnp.sum(cot3.astype(jnp.float32) * attended3.astype(jnp.float32), axis=2))
    global_delta = lax.optimization_barrier(jnp.sum(global_cotangent.astype(jnp.float32) * global_out.astype(jnp.float32), axis=2))

    def backward_block(running, block_index):
        key_grads, value_grads, gkey_grads, gvalue_grads = running
        offset = (block_index * block_len).astype(jnp.int32)
        query_block, key_block, value_block, query_global, band_mask, global_mask, band_scores, global_scores = block_parts(offset)
        total_block = lax.dynamic_slice_in_dim(log_total, offset, block_len, 0)
        delta_block = lax.dynamic_slice_in_dim(row_delta, offset, block_len, 0)
        cot_block = lax.dynamic_slice_in_dim(cot3, offset, block_len, 0)
        band_q, band_k, band_v = group_grads(band_scores, band_mask, total_block, delta_block, cot_block, query_block, key_block, value_block, score_scale)
        glob_q, glob_k, glob_v = group_grads(global_scores, global_mask, total_block, delta_block, cot_block, query_block, global_keys, global_values, score_scale)
        key_grads = lax.dynamic_update_slice_in_dim(key_grads, lax.dynamic_slice_in_dim(key_grads, offset, key_span, 0) + band_k, offset, 0)
        value_grads = lax.dynamic_update_slice_in_dim(value_grads, lax.dynamic_slice_in_dim(value_grads, offset, key_span, 0) + band_v, offset, 0)
        return ((key_grads, value_grads, gkey_grads + glob_k, gvalue_grads + glob_v), band_q + glob_q)
    zero_padded = jnp.zeros((length + 2 * half_span, H, HD), jnp.float32)
    zero_global = jnp.zeros((G, H, HD), jnp.float32)
    (key_grads, value_grads, gkey_grads, gvalue_grads), query_blocks = lax.scan(backward_block, (zero_padded, zero_padded, zero_global, zero_global), block_ids)

    def global_backward(running, run_index):
        offset = (run_index * TOK_DEV).astype(jnp.int32)
        key_block, value_block, allowed, scores = run_scores(offset)
        glob_q, glob_k, glob_v = group_grads(scores, allowed, global_log_total, global_delta, global_cotangent, global_queries, key_block, value_block, score_scale)
        return (running + glob_q, (glob_k, glob_v))
    gquery_grads, (from_key, from_value) = lax.scan(global_backward, zero_global, run_ids)
    key_total = key_grads[half_span:half_span + length] + from_key.reshape(length, H, HD)
    value_total = value_grads[half_span:half_span + length] + from_value.reshape(length, H, HD)
    key_total = key_total.at[global_spots].add(gkey_grads)
    value_total = value_total.at[global_spots].add(gvalue_grads)
    query_total = query_blocks.reshape(length, H, HD).at[global_spots].add(gquery_grads)
    query_bf = query_total.reshape(length, H * HD).astype(jnp.bfloat16)
    key_bf = key_total.reshape(length, H * HD).astype(jnp.bfloat16)
    value_bf = value_total.reshape(length, H * HD).astype(jnp.bfloat16)
    grad_query = jnp.dot(tokens.T, query_bf, preferred_element_type=jnp.float32)
    grad_key = jnp.dot(tokens.T, key_bf, preferred_element_type=jnp.float32)
    grad_value = jnp.dot(tokens.T, value_bf, preferred_element_type=jnp.float32)
    grad_input = jnp.dot(query_bf, query_weight.T, preferred_element_type=jnp.float32)
    grad_input = grad_input + jnp.dot(key_bf, key_weight.T, preferred_element_type=jnp.float32)
    grad_input = grad_input + jnp.dot(value_bf, value_weight.T, preferred_element_type=jnp.float32)
    attended = attended3.reshape(length, H * HD)
    return (attended, grad_input.astype(jnp.bfloat16), grad_query, grad_key, grad_value)

def reference(tokens, query_weight, key_weight, value_weight, cotangent, doc_lengths, global_positions):
    results = [one_sequence(tokens[sequence], query_weight, key_weight, value_weight, cotangent[sequence], doc_lengths[sequence], global_positions[sequence]) for sequence in range(SEQS)]
    attended = jnp.stack([result[0] for result in results])
    grad_tokens = jnp.stack([result[1] for result in results])
    grad_query = results[0][2]
    grad_key = results[0][3]
    grad_value = results[0][4]
    for result in results[1:]:
        grad_query = grad_query + result[2]
        grad_key = grad_key + result[3]
        grad_value = grad_value + result[4]
    return (attended, grad_tokens, grad_query, grad_key, grad_value)
```

```python
import functools
import math

import jax
import jax.numpy as jnp
from jax import lax
from jax.experimental import pallas as pl
from jax.experimental.pallas import tpu as pltpu
from jax.sharding import Mesh
from jax.sharding import PartitionSpec as P

HALF = 256
HD = 64
RUN = 256
SEC = 512
NSEC = 8
NEG = -1e30
BF = jnp.bfloat16
F32 = jnp.float32

Z = ("z2", "z1", "z0")
CTX = Z + ("xh",)
TP = ("y", "core")

OFFSETS = (0, -1, 1, -2, 2, -3, 3, 4)

NN = (((1,), (0,)), ((), ()))
NT = (((1,), (1,)), ((), ()))
TN = (((0,), (0,)), ((), ()))


def dot(a, b, dims=NN):
    return lax.dot_general(a, b, dims, preferred_element_type=F32)


def full_spec(memory_space=pltpu.VMEM):
    return pl.BlockSpec(memory_space=memory_space)


def call(kernel, outs, args, scratch=(), flops=0, transcendentals=0, smem=1, limit=48 << 20):
    specs = [full_spec(pltpu.SMEM)] * smem + [full_spec()] * (len(args) - smem)
    moved = sum(a.size * a.dtype.itemsize for a in args)
    return pl.pallas_call(
        kernel,
        out_shape=outs,
        in_specs=specs,
        out_specs=jax.tree.map(lambda _: full_spec(), outs),
        scratch_shapes=list(scratch),
        compiler_params=pltpu.CompilerParams(vmem_limit_bytes=limit),
        cost_estimate=pl.CostEstimate(
            flops=flops, bytes_accessed=moved, transcendentals=transcendentals
        ),
    )(*args)


def low_lanes(rows):
    return lax.broadcasted_iota(jnp.int32, (rows, 128), 1) < HD


def project_kernel(place, tok, wq, wk, wv, cot, mine, theirs):
    first = place[0] == 0
    t = tok[...]
    q = dot(t, wq[...]).astype(BF)
    k = dot(t, wk[...]).astype(BF)
    v = dot(t, wv[...]).astype(BF)
    c = cot[...]
    kv0 = jnp.concatenate([k[:, :HD], v[:, :HD]], axis=1)
    kv1 = jnp.concatenate([k[:, HD:], v[:, HD:]], axis=1)
    qc0 = jnp.concatenate([q[:, :HD], c[:, :HD]], axis=1)
    qc1 = jnp.concatenate([q[:, HD:], c[:, HD:]], axis=1)

    @pl.when(first)
    def _():
        mine[:RUN] = kv0
        mine[RUN:] = qc0
        theirs[:RUN] = kv1
        theirs[RUN:] = qc1

    @pl.when(jnp.logical_not(first))
    def _():
        mine[:RUN] = kv1
        mine[RUN:] = qc1
        theirs[:RUN] = kv0
        theirs[RUN:] = qc0


def feature_kernel(place, spots, starts, ends, key_feat, row_feat):
    flip = place[0]
    lane = lax.broadcasted_iota(jnp.int32, (RUN, 128), 1)
    inside = (lane >= HD) & (lane < HD + 8)
    last = lane == HD + 8

    def one(block, carry):
        half = lax.rem(block, 2)
        run = (block - half) + jnp.where(half == flip, 0, 1)
        pos = run * RUN + lax.broadcasted_iota(jnp.int32, (RUN, RUN), 0)
        hit = jnp.max(jnp.where(pos == spots[...], 1.0, 0.0), axis=1, keepdims=True)
        other = 1.0 - hit
        pos128 = run * RUN + lax.broadcasted_iota(jnp.int32, (RUN, 128), 0)
        member = (pos128 >= starts[...]) & (pos128 < ends[...])
        row = jnp.where(last, other, jnp.where(member, 1.0, 0.0))
        key = jnp.where(last, other, jnp.where(inside & jnp.logical_not(member), 1.0, 0.0))
        at = pl.ds(pl.multiple_of(block * RUN, RUN), RUN)
        row_feat[at, :] = row.astype(BF)
        key_feat[at, :] = (key * NEG).astype(BF)
        return carry

    lax.fori_loop(0, 2 * NSEC, one, 0)


def places(section, flip, along):
    shape = (1, SEC) if along == 1 else (SEC, 1)
    i = lax.broadcasted_iota(jnp.int32, shape, along)
    half = jnp.where(i >= RUN, 1 - flip, flip)
    return section * SEC + half * RUN + lax.bitwise_and(i, RUN - 1)


def rows_kernel(chunk, place, *refs):
    pieces, rest = refs[: 2 * NSEC], refs[2 * NSEC :]
    key_feat, row_feat, packed, stats, kv_s, kp_s, q_s, qn_s, c_s = rest
    flip, own = place[0], place[1]
    low = low_lanes(RUN)
    lane = lax.broadcasted_iota(jnp.int32, (RUN, 128), 1)
    for r in range(NSEC):
        section = lax.rem(own + OFFSETS[r] + NSEC, NSEC)
        for half in range(2):
            kv = pieces[2 * r + half][:RUN]
            at = r * SEC + half * RUN
            kv_s[at : at + RUN] = kv
            feat = key_feat[pl.ds(pl.multiple_of(section * SEC + half * RUN, RUN), RUN), :]
            kp_s[at : at + RUN] = jnp.where(low, kv, feat)
    for half in range(2):
        qc = pieces[half][RUN:]
        feat = row_feat[pl.ds(pl.multiple_of(own * SEC + half * RUN, RUN), RUN), :]
        at = half * RUN
        scaled = qc * jnp.asarray(1.0 / math.sqrt(HD), BF)
        joined = jnp.where(low, scaled, feat)
        zero = jnp.zeros_like(qc)
        q_s[at : at + RUN] = joined
        qn_s[at : at + RUN] = jnp.where(lane == HD + 8, zero, joined)
        c_s[at : at + RUN] = jnp.where(low, zero, qc)
    row_places = places(own, flip, 0)
    for c in range(SEC // chunk):
        rows = slice(c * chunk, (c + 1) * chunk)
        q, qn, cot = q_s[rows], qn_s[rows], c_s[rows]

        def scores(r, at, q=q, qn=qn, rows=rows):
            s = dot(q, kp_s[at, :], NT)
            if r is not None:
                section = lax.rem(own + OFFSETS[r] + NSEC, NSEC)
                away = row_places[rows] - places(section, flip, 1)
                s = jnp.where(jnp.abs(away) <= HALF, dot(qn, kp_s[at, :], NT), s)
            return s

        def forward(r, at, state, scores=scores):
            peak, total, acc = state
            s = scores(r, at)
            new_peak = jnp.maximum(peak, jnp.max(s, axis=1, keepdims=True))
            keep = jnp.exp(peak - new_peak)
            e = jnp.exp(s - new_peak)
            total = keep * total + jnp.sum(e, axis=1, keepdims=True)
            acc = keep * acc + dot(e.astype(BF), kv_s[at, :])
            return new_peak, total, acc

        state = (
            jnp.full((chunk, 1), NEG, F32),
            jnp.zeros((chunk, 1), F32),
            jnp.zeros((chunk, 128), F32),
        )
        for r in range(3):
            state = forward(r, slice(r * SEC, (r + 1) * SEC), state)
        state = lax.fori_loop(
            3,
            NSEC,
            lambda r, st, forward=forward: forward(
                None, pl.ds(pl.multiple_of(r * SEC, SEC), SEC), st
            ),
            state,
        )
        peak, total, acc = state
        att = (acc / total).astype(BF)
        log_total = peak + jnp.log(total)
        delta = jnp.sum(att.astype(F32) * cot.astype(F32), axis=1, keepdims=True)

        def backward(r, at, acc, scores=scores, log_total=log_total, delta=delta, cot=cot):
            p = jnp.exp(scores(r, at) - log_total)
            kv = kv_s[at, :]
            ds = p * (dot(cot, kv, NT) - delta)
            return acc + dot(ds.astype(BF), kv)

        grad = jnp.zeros((chunk, 128), F32)
        for r in range(3):
            grad = backward(r, slice(r * SEC, (r + 1) * SEC), grad)
        grad = lax.fori_loop(
            3,
            NSEC,
            lambda r, acc, backward=backward: backward(
                None, pl.ds(pl.multiple_of(r * SEC, SEC), SEC), acc
            ),
            grad,
        )
        grad = (grad * (1.0 / math.sqrt(HD))).astype(BF)
        packed[rows] = jnp.where(low_lanes(chunk), grad, att)
        lanes = lax.broadcasted_iota(jnp.int32, (chunk, 128), 1)
        turned = jnp.where(lanes == 0, log_total, delta).T
        for k in range(chunk // 128):
            at = c * (chunk // 128) + k
            stats[at : at + 1] = turned[0:1, k * 128 : (k + 1) * 128]
            stats[4 + at : 5 + at] = turned[1:2, k * 128 : (k + 1) * 128]


def keys_kernel(chunk, place, *refs):
    pieces, rest = refs[: 2 * NSEC], refs[2 * NSEC :]
    own_a, own_b, key_feat, row_feat, stats, packed, qc_s, q_s, k_s, kn_s, v_s = rest
    flip, own = place[0], place[1]
    low = low_lanes(RUN)
    lane = lax.broadcasted_iota(jnp.int32, (RUN, 128), 1)
    for r in range(NSEC):
        section = lax.rem(own + OFFSETS[r] + NSEC, NSEC)
        for half in range(2):
            piece = pieces[2 * r + half]
            qc = piece[piece.shape[0] - RUN :]
            at = r * SEC + half * RUN
            qc_s[at : at + RUN] = qc
            feat = row_feat[pl.ds(pl.multiple_of(section * SEC + half * RUN, RUN), RUN), :]
            q_s[at : at + RUN] = jnp.where(low, qc * jnp.asarray(1.0 / math.sqrt(HD), BF), feat)
    for half, piece in enumerate((own_a, own_b)):
        kv = piece[:RUN]
        feat = key_feat[pl.ds(pl.multiple_of(own * SEC + half * RUN, RUN), RUN), :]
        at = half * RUN
        joined = jnp.where(low, kv, feat)
        zero = jnp.zeros_like(kv)
        k_s[at : at + RUN] = joined
        kn_s[at : at + RUN] = jnp.where(lane == HD + 8, zero, joined)
        v_s[at : at + RUN] = jnp.where(low, zero, kv)
    key_places = places(own, flip, 0)
    for c in range(SEC // chunk):
        rows = slice(c * chunk, (c + 1) * chunk)
        k, kn, v = k_s[rows], kn_s[rows], v_s[rows]

        def backward(band, r, section, at, state):
            key_acc, value_acc = state
            st = stats[pl.ds(pl.multiple_of(section * 8, 8), 8), :]
            log_total = jnp.concatenate([st[i : i + 1] for i in range(4)], axis=1)
            delta = jnp.concatenate([st[i : i + 1] for i in range(4, 8)], axis=1)
            qc = qc_s[at, :]
            s = dot(k, q_s[at, :], NT)
            if band:
                away = key_places[rows] - places(section, flip, 1)
                s = jnp.where(jnp.abs(away) <= HALF, dot(kn, q_s[at, :], NT), s)
            p = jnp.exp(s - log_total)
            ds = p * (dot(v, qc, NT) - delta)
            key_acc = key_acc + dot(ds.astype(BF), qc)
            value_acc = value_acc + dot(p.astype(BF), qc)
            return key_acc, value_acc

        state = (jnp.zeros((chunk, 128), F32), jnp.zeros((chunk, 128), F32))
        for r in range(3):
            section = lax.rem(own + OFFSETS[r] + NSEC, NSEC)
            state = backward(True, r, section, slice(r * SEC, (r + 1) * SEC), state)

        def far(r, st):
            size = lax.div(r + 1, 2)
            offset = jnp.where(lax.rem(r, 2) == 1, jnp.where(r == 7, size, -size), size)
            section = lax.rem(own + offset + NSEC, NSEC)
            return backward(False, r, section, pl.ds(pl.multiple_of(r * SEC, SEC), SEC), st)

        key_acc, value_acc = lax.fori_loop(3, NSEC, far, state)
        joined = jnp.where(low_lanes(chunk), key_acc * (1.0 / math.sqrt(HD)), value_acc)
        packed[rows] = joined.astype(BF)


def weights_kernel(tok, tok_other, first, second, out):
    qa = dot(tok[...], first[:RUN], TN) + dot(tok_other[...], first[RUN:], TN)
    kv = dot(tok[...], second[:RUN], TN) + dot(tok_other[...], second[RUN:], TN)
    for p in range(16):
        out[p, :64] = kv[p * 64 : (p + 1) * 64].astype(BF)
        upper = qa[p * 32 : (p + 1) * 32, :HD]
        lower = qa[512 + p * 32 : 512 + (p + 1) * 32, :HD]
        out[p, 64:96] = jnp.concatenate([upper, lower], axis=1).astype(BF)


def sum_kernel(parts, out):
    total = parts[0].astype(F32)
    for p in range(1, 16):
        total = total + parts[p].astype(F32)
    total = total.astype(BF)
    for p in range(32):
        out[p] = total


def input_kernel(place, first, first_other, second, second_other, wq, wk, wv, att, keep, send):
    swap = place[0] != 0
    core = place[2]
    a, b, c, d = first[:RUN], first_other[...], second[:RUN], second_other[...]
    a, b = jnp.where(swap, b, a), jnp.where(swap, a, b)
    c, d = jnp.where(swap, d, c), jnp.where(swap, c, d)
    dq = jnp.concatenate([a[:, :HD], b[:, :HD]], axis=1)
    att[...] = jnp.concatenate([a[:, HD:], b[:, HD:]], axis=1)
    dk = jnp.concatenate([c[:, :HD], d[:, :HD]], axis=1)
    dv = jnp.concatenate([c[:, HD:], d[:, HD:]], axis=1)
    grad = dot(dq, wq[...], NT) + dot(dk, wk[...], NT) + dot(dv, wv[...], NT)
    for y in range(4):
        low, high = grad[y * 64 : y * 64 + 32], grad[y * 64 + 32 : y * 64 + 64]
        keep[y] = jnp.where(core == 0, low, high)
        send[y] = jnp.where(core == 0, high, low).astype(BF)


def assemble_kernel(parts, gq, gk, gv):
    for p in range(16):
        a, b = parts[2 * p].astype(F32), parts[2 * p + 1].astype(F32)
        low = jnp.concatenate([a[:, :HD], b[:, :HD]], axis=1)
        high = jnp.concatenate([a[:, HD:], b[:, HD:]], axis=1)
        gk[p * 64 : (p + 1) * 64] = low[:64]
        gv[p * 64 : (p + 1) * 64] = high[:64]
        gq[p * 32 : (p + 1) * 32] = low[64:]
        gq[512 + p * 32 : 512 + (p + 1) * 32] = high[64:]


def shift(a, step):
    return lax.ppermute(a, Z, [(i, (i + step) % NSEC) for i in range(NSEC)])


def swap(a):
    return lax.ppermute(a, "xh", [(0, 1), (1, 0)])


def ring(block):
    lower, upper = [block], [block]
    for _ in range(3):
        lower.append(shift(lower[-1], 1))
        upper.append(shift(upper[-1], -1))
    far_kv = shift(lower[3][:RUN], 1)
    far_qc = shift(upper[3][RUN:], -1)
    near = [block, lower[1], upper[1], lower[2], upper[2], lower[3], upper[3]]
    return near + [far_kv], near + [far_qc]


def on_device(tokens, wq, wk, wv, cotangent, doc_lengths, global_positions):
    shape = jax.ShapeDtypeStruct
    tok, cot = tokens[0], cotangent[0]
    xh, z, y, core = (lax.axis_index(a) for a in ("xh", Z, "y", "core"))
    place = jnp.stack([xh, z, core]).astype(jnp.int32)
    ends = jnp.cumsum(doc_lengths[0])
    starts_row = jnp.zeros((1, 128), jnp.int32).at[0, HD : HD + 8].set(ends - doc_lengths[0])
    ends_row = jnp.zeros((1, 128), jnp.int32).at[0, HD : HD + 8].set(ends)
    mine, theirs = call(
        project_kernel,
        (shape((SEC, 128), BF),) * 2,
        (place, tok, wq, wk, wv, cot),
        flops=6 * 256 * 1024 * 128,
    )
    other = swap(theirs)
    tok_other = swap(tok)
    key_feat, row_feat = call(
        feature_kernel,
        (shape((NSEC * SEC, 128), BF),) * 2,
        (place, global_positions, starts_row, ends_row),
    )
    kv_a, qc_a = ring(mine)
    kv_b, qc_b = ring(other)
    kv = [x for pair in zip(kv_a, kv_b) for x in pair]
    qc = [x for pair in zip(qc_a, qc_b) for x in pair]
    whole, part = pltpu.VMEM((NSEC * SEC, 128), BF), pltpu.VMEM((SEC, 128), BF)
    pairs = SEC * NSEC * SEC
    first, stats = call(
        functools.partial(rows_kernel, 256),
        (shape((SEC, 128), BF), shape((8, 128), F32)),
        (place, *kv, key_feat, row_feat),
        scratch=(whole, whole, part, part, part),
        flops=2 * 128 * 5 * pairs,
        transcendentals=2 * pairs,
    )
    first_other = swap(first[RUN:])
    all_stats = lax.all_to_all(
        jnp.broadcast_to(stats[None], (NSEC, 8, 128)), Z, 0, 0, tiled=True
    ).reshape(NSEC * 8, 128)
    second = call(
        functools.partial(keys_kernel, 256),
        shape((SEC, 128), BF),
        (place, *qc, mine, other, key_feat, row_feat, all_stats),
        scratch=(whole, whole, part, part, part),
        flops=2 * 128 * 4 * pairs,
        transcendentals=pairs,
    )
    second_other = swap(second[RUN:])
    partial = call(
        weights_kernel,
        shape((16, 96, 128), BF),
        (tok, tok_other, first, second),
        flops=2 * 512 * 1024 * 256,
        smem=0,
    )
    partial = lax.all_to_all(partial, ("b",) + Z, 0, 0, tiled=True)
    total = call(sum_kernel, shape((32, 96, 128), BF), (partial,), smem=0)
    att, keep, send = call(
        input_kernel,
        (shape((RUN, 128), BF), shape((4, 32, 1024), F32), shape((4, 32, 1024), BF)),
        (place, first, first_other, second, second_other, wq, wk, wv),
        flops=6 * 256 * 1024 * 128,
    )
    arrived = lax.ppermute(send, "core", [(0, 1), (1, 0)])
    both = keep + arrived.astype(F32)
    share = lax.dynamic_index_in_dim(both, y, 0, False)
    both_bf = both.astype(BF)
    for k in (1, 2, 3):
        out = lax.dynamic_index_in_dim(both_bf, lax.bitwise_xor(y, k), 0, False)
        share = share + lax.ppermute(out, "y", [(i, i ^ k) for i in range(4)]).astype(F32)
    total = lax.all_to_all(total, ("b",) + CTX, 0, 0, tiled=True)
    gq, gk, gv = call(assemble_kernel, (shape((1024, 128), F32),) * 3, (total,), smem=0)
    return att[None], share.astype(BF)[None], gq, gk, gv


def solution(mesh):
    devices = mesh.devices.reshape(2, 2, 2, 2, 2, 4, 2)
    fine = Mesh(devices, ("b",) + CTX + TP)
    in_specs = (
        P("b", CTX, None),
        P(None, TP),
        P(None, TP),
        P(None, TP),
        P("b", CTX, TP),
        P("b", None),
        P("b", None),
    )
    out_specs = (
        P("b", CTX, TP),
        P("b", CTX + TP, None),
        P(None, TP),
        P(None, TP),
        P(None, TP),
    )
    return jax.shard_map(
        on_device, mesh=fine, in_specs=in_specs, out_specs=out_specs, check_vma=False
    )
```

```python
import functools
import math

import jax
import jax.numpy as jnp
from jax import lax
from jax.experimental import pallas as pl
from jax.experimental.pallas import tpu as pltpu
from jax.sharding import Mesh
from jax.sharding import PartitionSpec as P

HALF = 256
HD = 64
RUN = 256
SEC = 512
NSEC = 8
NEG = -1e30
LIMIT = 64 << 20
BF = jnp.bfloat16
F32 = jnp.float32

Z = ("z2", "z1", "z0")
CTX = Z + ("xh",)
TP = ("y", "core")

OFFSETS = (0, -1, 1, -2, 2, -3, 3, 4)

NN = (((1,), (0,)), ((), ()))
NT = (((1,), (1,)), ((), ()))
TN = (((0,), (0,)), ((), ()))


def dot(a, b, dims=NN):
    return lax.dot_general(a, b, dims, preferred_element_type=F32)


def call(kernel, outs, args, scratch=(), flops=0, transcendentals=0, smem=1, manual=0):
    specs = [pl.BlockSpec(memory_space=pltpu.SMEM)] * smem
    specs += [pl.BlockSpec(memory_space=pl.ANY)] * manual
    specs += [pl.BlockSpec(memory_space=pltpu.VMEM)] * (len(args) - smem - manual)
    moved = sum(a.size * a.dtype.itemsize for a in args)
    return pl.pallas_call(
        kernel,
        out_shape=outs,
        in_specs=specs,
        out_specs=jax.tree.map(lambda _: pl.BlockSpec(memory_space=pltpu.VMEM), outs),
        scratch_shapes=list(scratch),
        compiler_params=pltpu.CompilerParams(vmem_limit_bytes=LIMIT),
        cost_estimate=pl.CostEstimate(
            flops=flops, bytes_accessed=moved, transcendentals=transcendentals
        ),
    )(*args)


def low_lanes(rows):
    return lax.broadcasted_iota(jnp.int32, (rows, 128), 1) < HD


def project_kernel(place, tok, wq, wk, wv, cot, mine, theirs, tok_v, wk_v, wv_v, wq_v, cot_v, sems):
    pairs = ((tok, tok_v), (wk, wk_v), (wv, wv_v), (wq, wq_v), (cot, cot_v))
    copies = [pltpu.make_async_copy(a, b, sems.at[i]) for i, (a, b) in enumerate(pairs)]
    for copy in copies:
        copy.start()
    first = place[0] == 0
    copies[0].wait()
    t = tok_v[...]
    copies[1].wait()
    k = dot(t, wk_v[...]).astype(BF)
    copies[2].wait()
    v = dot(t, wv_v[...]).astype(BF)
    copies[3].wait()
    q = dot(t, wq_v[...]).astype(BF)
    copies[4].wait()
    c = cot_v[...]
    kv0 = jnp.concatenate([k[:, :HD], v[:, :HD]], axis=1)
    kv1 = jnp.concatenate([k[:, HD:], v[:, HD:]], axis=1)
    qc0 = jnp.concatenate([q[:, :HD], c[:, :HD]], axis=1)
    qc1 = jnp.concatenate([q[:, HD:], c[:, HD:]], axis=1)

    @pl.when(first)
    def _():
        mine[:RUN] = kv0
        mine[RUN:] = qc0
        theirs[:RUN] = kv1
        theirs[RUN:] = qc1

    @pl.when(jnp.logical_not(first))
    def _():
        mine[:RUN] = kv1
        mine[RUN:] = qc1
        theirs[:RUN] = kv0
        theirs[RUN:] = qc0


def feature_kernel(place, lengths, spots, key_feat, row_feat):
    flip = place[0]
    lane = lax.broadcasted_iota(jnp.int32, (RUN, 128), 1)
    inside = (lane >= HD) & (lane < HD + 8)
    last = lane == HD + 8
    lane_row = lax.broadcasted_iota(jnp.int32, (1, 128), 1)
    starts, ends = jnp.zeros((1, 128), jnp.int32), jnp.zeros((1, 128), jnp.int32)
    start = jnp.int32(0)
    for d in range(8):
        end = start + lengths[0, d]
        starts = jnp.where(lane_row == HD + d, start, starts)
        ends = jnp.where(lane_row == HD + d, end, ends)
        start = end

    def one(block, carry):
        half = lax.rem(block, 2)
        run = (block - half) + jnp.where(half == flip, 0, 1)
        pos = run * RUN + lax.broadcasted_iota(jnp.int32, (RUN, RUN), 0)
        hit = jnp.max(jnp.where(pos == spots[...], 1.0, 0.0), axis=1, keepdims=True)
        other = 1.0 - hit
        pos128 = run * RUN + lax.broadcasted_iota(jnp.int32, (RUN, 128), 0)
        member = (pos128 >= starts) & (pos128 < ends)
        row = jnp.where(last, other, jnp.where(member, 1.0, 0.0))
        key = jnp.where(last, other, jnp.where(inside & jnp.logical_not(member), 1.0, 0.0))
        at = pl.ds(pl.multiple_of(block * RUN, RUN), RUN)
        row_feat[at, :] = row.astype(BF)
        key_feat[at, :] = (key * NEG).astype(BF)
        return carry

    lax.fori_loop(0, 2 * NSEC, one, 0)


def places(section, flip, along):
    shape = (1, SEC) if along == 1 else (SEC, 1)
    i = lax.broadcasted_iota(jnp.int32, shape, along)
    half = jnp.where(i >= RUN, 1 - flip, flip)
    return section * SEC + half * RUN + lax.bitwise_and(i, RUN - 1)


def section_at(own, offset):
    return lax.rem(own + offset + NSEC, NSEC)


def bring(own, offsets, pieces, part, feat, rows, joined, sems):
    copies = []
    for r, offset in enumerate(offsets):
        for half in range(2):
            to = rows.at[pl.ds(r * SEC + half * RUN, RUN)]
            copies.append((pieces[2 * r + half].at[pl.ds(part * RUN, RUN)], to))
        at = pl.multiple_of(section_at(own, offset) * SEC, SEC)
        copies.append((feat.at[pl.ds(at, SEC)], joined.at[pl.ds(r * SEC, SEC)]))
    copies = [pltpu.make_async_copy(a, b, sems.at[i]) for i, (a, b) in enumerate(copies)]
    for copy in copies:
        copy.start()
    return copies


def join_keys(count, kv_s, kp_s):
    low = low_lanes(SEC)
    for r in range(count):
        at = slice(r * SEC, (r + 1) * SEC)
        kp_s[at] = jnp.where(low, kv_s[at], kp_s[at])


def join_queries(count, qc_s, q_s):
    low = low_lanes(SEC)
    for r in range(count):
        at = slice(r * SEC, (r + 1) * SEC)
        scaled = qc_s[at] * jnp.asarray(1.0 / math.sqrt(HD), BF)
        q_s[at] = jnp.where(low, scaled, q_s[at])


def upper_only(rows_s, joined_s, near_s):
    rows = rows_s[...]
    rows_s[...] = jnp.where(low_lanes(SEC), jnp.zeros_like(rows), rows)
    lane = lax.broadcasted_iota(jnp.int32, (SEC, 128), 1)
    joined = joined_s[...]
    near_s[...] = jnp.where(lane == HD + 8, jnp.zeros_like(joined), joined)


def bring_both(own, offsets, pieces, mine, other, key_feat, row_feat, scratch):
    kv_s, kp_s, q_s, qn_s, c_s, sems, own_sems = scratch
    copies = bring(own, offsets, pieces, 0, key_feat, kv_s, kp_s, sems)
    copies += bring(own, (0,), (mine, other), 1, row_feat, c_s, q_s, own_sems)
    for copy in copies:
        copy.wait()
    join_keys(len(offsets), kv_s, kp_s)
    join_queries(1, c_s, q_s)
    upper_only(c_s, q_s, qn_s)


def scores_of(own, flip, chunk, c, offset, at, row_places, q_s, qn_s, kp_s):
    rows = slice(c * chunk, (c + 1) * chunk)
    s = dot(q_s[rows], kp_s[at, :], NT)
    if offset in (0, -1, 1):
        away = row_places[rows] - places(section_at(own, offset), flip, 1)
        s = jnp.where(jnp.abs(away) <= HALF, dot(qn_s[rows], kp_s[at, :], NT), s)
    return s


def forward_kernel(chunk, offsets, first, last, place, mine, other, key_feat, row_feat, *refs):
    pieces, rest = refs[: 2 * len(offsets)], list(refs[2 * len(offsets) :])
    acc_in, peak_in = (None, None) if first else (rest.pop(0), rest.pop(0))
    if last:
        att_out, column_out, stats, *scratch = rest
    else:
        acc_out, peak_out, *scratch = rest
    kv_s, kp_s, q_s, qn_s, c_s = scratch[:5]
    flip, own = place[0], place[1]
    bring_both(own, offsets, pieces, mine, other, key_feat, row_feat, scratch)
    row_places = places(own, flip, 0)
    for c in range(SEC // chunk):
        rows = slice(c * chunk, (c + 1) * chunk)
        if first:
            peak = jnp.full((chunk, 1), NEG, F32)
            total = jnp.zeros((chunk, 1), F32)
            acc = jnp.zeros((chunk, 128), F32)
        else:
            peak, total, acc = peak_in[rows, 0:1], peak_in[rows, 1:2], acc_in[rows]
        for r, offset in enumerate(offsets):
            at = slice(r * SEC, (r + 1) * SEC)
            s = scores_of(own, flip, chunk, c, offset, at, row_places, q_s, qn_s, kp_s)
            new_peak = jnp.maximum(peak, jnp.max(s, axis=1, keepdims=True))
            keep = jnp.exp(peak - new_peak)
            e = jnp.exp(s - new_peak)
            total = keep * total + jnp.sum(e, axis=1, keepdims=True)
            acc = keep * acc + dot(e.astype(BF), kv_s[at, :])
            peak = new_peak
        lanes = lax.broadcasted_iota(jnp.int32, (chunk, 128), 1)
        if not last:
            acc_out[rows] = acc
            peak_out[rows] = jnp.where(lanes == 0, peak, total)
            continue
        att = (acc / total).astype(BF)
        att_out[rows] = att
        log_total = peak + jnp.log(total)
        cot = c_s[rows].astype(F32)
        delta = jnp.sum(att.astype(F32) * cot, axis=1, keepdims=True)
        column = jnp.where(lanes == 0, log_total, delta)
        column_out[rows] = column
        turned = column.T
        for k in range(chunk // 128):
            at = c * (chunk // 128) + k
            stats[at : at + 1] = turned[0:1, k * 128 : (k + 1) * 128]
            stats[4 + at : 5 + at] = turned[1:2, k * 128 : (k + 1) * 128]


def queries_kernel(chunk, place, *refs):
    pieces, rest = refs[: 2 * NSEC], refs[2 * NSEC :]
    key_feat, row_feat, att, column, packed, packed_other, *scratch = rest
    kv_s, kp_s, q_s, qn_s, c_s = scratch[:5]
    flip, own = place[0], place[1]
    bring_both(own, OFFSETS, pieces, pieces[0], pieces[1], key_feat, row_feat, scratch)
    row_places = places(own, flip, 0)
    for c in range(SEC // chunk):
        rows = slice(c * chunk, (c + 1) * chunk)
        log_total, delta, cot = column[rows, 0:1], column[rows, 1:2], c_s[rows]

        def backward(offset, at, acc, c=c, log_total=log_total, delta=delta, cot=cot):
            s = scores_of(own, flip, chunk, c, offset, at, row_places, q_s, qn_s, kp_s)
            p = jnp.exp(s - log_total)
            kv = kv_s[at, :]
            ds = p * (dot(cot, kv, NT) - delta)
            return acc + dot(ds.astype(BF), kv)

        grad = jnp.zeros((chunk, 128), F32)
        for r in range(3):
            grad = backward(OFFSETS[r], slice(r * SEC, (r + 1) * SEC), grad)
        grad = lax.fori_loop(
            3,
            NSEC,
            lambda r, acc, backward=backward: backward(
                None, pl.ds(pl.multiple_of(r * SEC, SEC), SEC), acc
            ),
            grad,
        )
        grad = (grad * (1.0 / math.sqrt(HD))).astype(BF)
        joined = jnp.where(low_lanes(chunk), grad, att[rows])
        out = packed if c * chunk < RUN else packed_other
        at = (c * chunk) % RUN
        out[at : at + chunk] = joined


def keys_kernel(chunk, place, *refs):
    pieces, rest = refs[: 2 * NSEC], refs[2 * NSEC :]
    key_feat, row_feat, stats, packed, packed_other, *scratch = rest
    qc_s, q_s, k_s, kn_s, v_s, sems, own_sems, stats_s, stats_sems = scratch
    flip, own = place[0], place[1]
    copies = bring(own, OFFSETS, pieces, 1, row_feat, qc_s, q_s, sems)
    copies += bring(own, (0,), pieces[:2], 0, key_feat, v_s, k_s, own_sems)
    for r, offset in enumerate(OFFSETS):
        at = pl.multiple_of(section_at(own, offset) * 8, 8)
        to = stats_s.at[pl.ds(r * 8, 8)]
        copies.append(pltpu.make_async_copy(stats.at[pl.ds(at, 8)], to, stats_sems.at[r]))
        copies[-1].start()
    for copy in copies:
        copy.wait()
    join_queries(NSEC, qc_s, q_s)
    join_keys(1, v_s, k_s)
    upper_only(v_s, k_s, kn_s)
    key_places = places(own, flip, 0)
    for c in range(SEC // chunk):
        rows = slice(c * chunk, (c + 1) * chunk)
        k, kn, v = k_s[rows], kn_s[rows], v_s[rows]

        def backward(near, r, at, state):
            key_acc, value_acc = state
            st = stats_s[pl.ds(pl.multiple_of(r * 8, 8), 8), :]
            log_total = jnp.concatenate([st[i : i + 1] for i in range(4)], axis=1)
            delta = jnp.concatenate([st[i : i + 1] for i in range(4, 8)], axis=1)
            qc = qc_s[at, :]
            s = dot(k, q_s[at, :], NT)
            if near:
                section = section_at(own, OFFSETS[r])
                away = key_places[rows] - places(section, flip, 1)
                s = jnp.where(jnp.abs(away) <= HALF, dot(kn, q_s[at, :], NT), s)
            p = jnp.exp(s - log_total)
            ds = p * (dot(v, qc, NT) - delta)
            key_acc = key_acc + dot(ds.astype(BF), qc)
            value_acc = value_acc + dot(p.astype(BF), qc)
            return key_acc, value_acc

        state = (jnp.zeros((chunk, 128), F32), jnp.zeros((chunk, 128), F32))
        for r in range(3):
            state = backward(True, r, slice(r * SEC, (r + 1) * SEC), state)

        def far(r, st, backward=backward):
            return backward(False, r, pl.ds(pl.multiple_of(r * SEC, SEC), SEC), st)

        key_acc, value_acc = lax.fori_loop(3, NSEC, far, state)
        joined = jnp.where(low_lanes(chunk), key_acc * (1.0 / math.sqrt(HD)), value_acc)
        out = packed if c * chunk < RUN else packed_other
        at = (c * chunk) % RUN
        out[at : at + chunk] = joined.astype(BF)


def weights_kernel(tok, tok_other, first, first_sent, second, second_sent, out):
    qa = dot(tok[...], first[...], TN) + dot(tok_other[...], first_sent[...], TN)
    kv = dot(tok[...], second[...], TN) + dot(tok_other[...], second_sent[...], TN)
    for p in range(16):
        out[p, :64] = kv[p * 64 : (p + 1) * 64].astype(BF)
        upper = qa[p * 32 : (p + 1) * 32, :HD]
        lower = qa[512 + p * 32 : 512 + (p + 1) * 32, :HD]
        out[p, 64:96] = jnp.concatenate([upper, lower], axis=1).astype(BF)


def sum_kernel(parts, out):
    total = parts[0].astype(F32)
    for p in range(1, 16):
        total = total + parts[p].astype(F32)
    total = total.astype(BF)
    for p in range(32):
        out[p] = total


def input_kernel(place, first, first_other, second, second_other, wq, wk, wv, att, keep, send):
    swap = place[0] != 0
    core = place[2]
    a, b, c, d = first[...], first_other[...], second[...], second_other[...]
    a, b = jnp.where(swap, b, a), jnp.where(swap, a, b)
    c, d = jnp.where(swap, d, c), jnp.where(swap, c, d)
    dq = jnp.concatenate([a[:, :HD], b[:, :HD]], axis=1)
    att[...] = jnp.concatenate([a[:, HD:], b[:, HD:]], axis=1)
    dk = jnp.concatenate([c[:, :HD], d[:, :HD]], axis=1)
    dv = jnp.concatenate([c[:, HD:], d[:, HD:]], axis=1)
    grad = dot(dq, wq[...], NT) + dot(dk, wk[...], NT) + dot(dv, wv[...], NT)
    for y in range(4):
        low, high = grad[y * 64 : y * 64 + 32], grad[y * 64 + 32 : y * 64 + 64]
        keep[y] = jnp.where(core == 0, low, high)
        send[y] = jnp.where(core == 0, high, low).astype(BF)


def assemble_kernel(parts, gq, gk, gv):
    for p in range(16):
        a, b = parts[2 * p].astype(F32), parts[2 * p + 1].astype(F32)
        low = jnp.concatenate([a[:, :HD], b[:, :HD]], axis=1)
        high = jnp.concatenate([a[:, HD:], b[:, HD:]], axis=1)
        gk[p * 64 : (p + 1) * 64] = low[:64]
        gv[p * 64 : (p + 1) * 64] = high[:64]
        gq[p * 32 : (p + 1) * 32] = low[64:]
        gq[512 + p * 32 : 512 + (p + 1) * 32] = high[64:]


def shift(a, step):
    return lax.ppermute(a, Z, [(i, (i + step) % NSEC) for i in range(NSEC)])


def swap(a):
    return lax.ppermute(a, "xh", [(0, 1), (1, 0)])


def on_device(tokens, wq, wk, wv, cotangent, doc_lengths, global_positions):
    shape = jax.ShapeDtypeStruct
    tok, cot = tokens[0], cotangent[0]
    xh, z, y, core = (lax.axis_index(a) for a in ("xh", Z, "y", "core"))
    place = jnp.stack([xh, z, core]).astype(jnp.int32)
    weight = pltpu.VMEM((1024, 128), BF)
    mine, theirs = call(
        project_kernel,
        (shape((SEC, 128), BF),) * 2,
        (place, tok, wq, wk, wv, cot),
        scratch=(
            pltpu.VMEM((RUN, 1024), BF),
            weight,
            weight,
            weight,
            pltpu.VMEM((RUN, 128), BF),
            pltpu.SemaphoreType.DMA((5,)),
        ),
        flops=6 * 256 * 1024 * 128,
        manual=5,
    )
    other = swap(theirs)
    tok_other = swap(tok)
    part, own_sems = pltpu.VMEM((SEC, 128), BF), pltpu.SemaphoreType.DMA((3,))
    pairs = SEC * SEC
    wide = shape((SEC, 128), F32)

    def forward(lo, hi, place, pieces, state):
        n, last = hi - lo, hi == NSEC
        outs = (shape((SEC, 128), BF), wide, shape((8, 128), F32)) if last else (wide, wide)
        keys = pltpu.VMEM((n * SEC, 128), BF)
        return call(
            functools.partial(forward_kernel, 256, OFFSETS[lo:hi], lo == 0, last),
            outs,
            (place, mine, other, key_feat, row_feat, *pieces, *state),
            scratch=(keys, keys, part, part, part, pltpu.SemaphoreType.DMA((3 * n,)), own_sems),
            flops=2 * 128 * 2 * n * pairs,
            transcendentals=n * pairs,
            manual=4 + 2 * n,
        )

    tie = lax.optimization_barrier
    lower_a, upper_a = [mine, shift(mine, 1)], [mine, shift(mine, -1)]
    lower_b, upper_b = [other, shift(other, 1)], [other, shift(other, -1)]
    late, upper_a[1] = tie((place, upper_a[1]))
    key_feat, row_feat = call(
        feature_kernel,
        (shape((NSEC * SEC, 128), BF),) * 2,
        (late, doc_lengths, global_positions),
        smem=2,
    )
    lower_b[1], key_feat, row_feat = tie((lower_b[1], key_feat, row_feat))
    for x, step in ((lower_a, 1), (upper_a, -1), (lower_b, 1), (upper_b, -1)):
        x.append(shift(x[1], step))
    late, upper_a[2] = tie((place, upper_a[2]))
    state = forward(0, 1, late, (mine, other), ())
    lower_b[2], *state = tie((lower_b[2], *state))
    for x, step in ((lower_a, 1), (upper_a, -1), (lower_b, 1), (upper_b, -1)):
        x.append(shift(x[2], step))
    late, upper_a[3] = tie((place, upper_a[3]))
    near = (lower_a[1], lower_b[1], upper_a[1], upper_b[1])
    state = forward(1, 3, late, near, state)
    upper_b[3], *state = tie((upper_b[3], *state))
    far = (shift(lower_a[3], 1), shift(upper_b[3], -1))
    near2 = (lower_a[2], lower_b[2], upper_a[2], upper_b[2])
    state = forward(3, 5, place, near2, state)
    rest = (lower_a[3], lower_b[3], upper_a[3], upper_b[3]) + far
    pieces = (mine, other) + near + near2 + rest
    att_rows, column, stats = forward(5, 8, place, rest, state)
    all_stats = lax.all_to_all(
        jnp.broadcast_to(stats[None], (NSEC, 8, 128)), Z, 0, 0, tiled=True
    ).reshape(NSEC * 8, 128)
    whole = pltpu.VMEM((NSEC * SEC, 128), BF)
    half = shape((RUN, 128), BF)
    first, first_sent = call(
        functools.partial(queries_kernel, 256),
        (half, half),
        (place, *pieces, key_feat, row_feat, att_rows, column),
        scratch=(whole, whole, part, part, part, pltpu.SemaphoreType.DMA((24,)), own_sems),
        flops=2 * 128 * 3 * NSEC * pairs,
        manual=18,
        transcendentals=NSEC * pairs,
    )
    all_stats, first, first_sent = lax.optimization_barrier((all_stats, first, first_sent))
    first_other = swap(first_sent)
    stats_scratch = (pltpu.VMEM((NSEC * 8, 128), F32), pltpu.SemaphoreType.DMA((NSEC,)))
    second, second_sent = call(
        functools.partial(keys_kernel, 256),
        (half, half),
        (place, *pieces, key_feat, row_feat, all_stats),
        scratch=(whole, whole, part, part, part, pltpu.SemaphoreType.DMA((24,)), own_sems) + stats_scratch,
        flops=2 * 128 * 4 * NSEC * pairs,
        manual=19,
        transcendentals=NSEC * pairs,
    )
    second, second_sent, first_other = lax.optimization_barrier((second, second_sent, first_other))
    second_other = swap(second_sent)
    partial = call(
        weights_kernel,
        shape((16, 96, 128), BF),
        (tok, tok_other, first, first_sent, second, second_sent),
        flops=2 * 512 * 1024 * 256,
        smem=0,
    )
    partial = lax.all_to_all(partial, ("b",) + Z, 0, 0, tiled=True)
    att, keep, send = call(
        input_kernel,
        (half, shape((4, 32, 1024), F32), shape((4, 32, 1024), BF)),
        (place, first, first_other, second, second_other, wq, wk, wv),
        flops=6 * 256 * 1024 * 128,
    )
    arrived = lax.ppermute(send, "core", [(0, 1), (1, 0)])
    partial, arrived = lax.optimization_barrier((partial, arrived))
    total = call(sum_kernel, shape((32, 96, 128), BF), (partial,), smem=0)
    both = keep + arrived.astype(F32)
    share = lax.dynamic_index_in_dim(both, y, 0, False)
    both_bf = both.astype(BF)
    for k in (1, 2, 3):
        out = lax.dynamic_index_in_dim(both_bf, lax.bitwise_xor(y, k), 0, False)
        share = share + lax.ppermute(out, "y", [(i, i ^ k) for i in range(4)]).astype(F32)
    total = lax.all_to_all(total, ("b",) + CTX, 0, 0, tiled=True)
    gq, gk, gv = call(assemble_kernel, (shape((1024, 128), F32),) * 3, (total,), smem=0)
    return att[None], share.astype(BF)[None], gq, gk, gv


def solution(mesh):
    devices = mesh.devices.reshape(2, 2, 2, 2, 2, 4, 2)
    fine = Mesh(devices, ("b",) + CTX + TP)
    in_specs = (
        P("b", CTX, None),
        P(None, TP),
        P(None, TP),
        P(None, TP),
        P("b", CTX, TP),
        P("b", None),
        P("b", None),
    )
    out_specs = (
        P("b", CTX, TP),
        P("b", CTX + TP, None),
        P(None, TP),
        P(None, TP),
        P(None, TP),
    )
    return jax.shard_map(
        on_device, mesh=fine, in_specs=in_specs, out_specs=out_specs, check_vma=False
    )
```

```python
import functools
import math

import jax
import jax.numpy as jnp
from jax import lax
from jax.experimental import pallas as pl
from jax.experimental.pallas import tpu as pltpu
from jax.sharding import Mesh
from jax.sharding import PartitionSpec as P

HALF = 256
HD = 64
RUN = 256
SEC = 512
NSEC = 8
NEG = -1e30
LIMIT = 51 << 20
CALLS = ((0, 8),)
BF = jnp.bfloat16
F32 = jnp.float32

Z = ("z2", "z1", "z0")
CTX = Z + ("xh",)
TP = ("y", "core")

OFFSETS = (0, -1, 1, -2, 2, -3, 3, 4)

NN = (((1,), (0,)), ((), ()))
NT = (((1,), (1,)), ((), ()))
TN = (((0,), (0,)), ((), ()))


def dot(a, b, dims=NN):
    return lax.dot_general(a, b, dims, preferred_element_type=F32)


def call(kernel, outs, args, scratch=(), flops=0, transcendentals=0, smem=1, manual=0, limit=None):
    specs = [pl.BlockSpec(memory_space=pltpu.SMEM)] * smem
    specs += [pl.BlockSpec(memory_space=pl.ANY)] * manual
    specs += [pl.BlockSpec(memory_space=pltpu.VMEM)] * (len(args) - smem - manual)
    moved = sum(a.size * a.dtype.itemsize for a in args)
    return pl.pallas_call(
        kernel,
        out_shape=outs,
        in_specs=specs,
        out_specs=jax.tree.map(lambda _: pl.BlockSpec(memory_space=pltpu.VMEM), outs),
        scratch_shapes=list(scratch),
        compiler_params=pltpu.CompilerParams(vmem_limit_bytes=limit or LIMIT),
        cost_estimate=pl.CostEstimate(
            flops=flops, bytes_accessed=moved, transcendentals=transcendentals
        ),
    )(*args)


def low_lanes(rows):
    return lax.broadcasted_iota(jnp.int32, (rows, 128), 1) < HD


def document_features(place, lengths, spots, feat):
    flip = place[0]
    lane = lax.broadcasted_iota(jnp.int32, (RUN, 128), 1)
    last = lane == HD + 8
    lane_row = lax.broadcasted_iota(jnp.int32, (1, 128), 1)
    starts, ends = jnp.zeros((1, 128), jnp.int32), jnp.zeros((1, 128), jnp.int32)
    start = jnp.int32(0)
    for d in range(8):
        end = start + lengths[0, d]
        starts = jnp.where(lane_row == HD + d, start, starts)
        ends = jnp.where(lane_row == HD + d, end, ends)
        start = end

    def one(block, carry):
        half = lax.rem(block, 2)
        run = (block - half) + jnp.where(half == flip, 0, 1)
        pos = run * RUN + lax.broadcasted_iota(jnp.int32, (RUN, RUN), 0)
        hit = jnp.max(jnp.where(pos == spots[...], 1.0, 0.0), axis=1, keepdims=True)
        other = 1.0 - hit
        pos128 = run * RUN + lax.broadcasted_iota(jnp.int32, (RUN, 128), 0)
        member = (pos128 >= starts) & (pos128 < ends)
        row = jnp.where(last, other, jnp.where(member, 1.0, 0.0))
        at = pl.ds(pl.multiple_of(block * RUN, RUN), RUN)
        feat[at, :] = row.astype(BF)
        return carry

    lax.fori_loop(0, 2 * NSEC, one, 0)


def project_kernel(place, lengths, tok, wq, wk, wv, cot, spots, mine, theirs, feat, *scratch):
    tok_v, wk_v, wv_v, wq_v, cot_v, sems = scratch
    pairs = ((tok, tok_v), (wk, wk_v), (wv, wv_v), (wq, wq_v), (cot, cot_v))
    copies = [pltpu.make_async_copy(a, b, sems.at[i]) for i, (a, b) in enumerate(pairs)]
    for copy in copies:
        copy.start()
    document_features(place, lengths, spots, feat)
    first = place[0] == 0
    copies[0].wait()
    t = tok_v[...]
    copies[1].wait()
    k = dot(t, wk_v[...]).astype(BF)
    copies[2].wait()
    v = dot(t, wv_v[...]).astype(BF)
    copies[3].wait()
    q = dot(t, wq_v[...]).astype(BF)
    copies[4].wait()
    c = cot_v[...]
    kv0 = jnp.concatenate([k[:, :HD], v[:, :HD]], axis=1)
    kv1 = jnp.concatenate([k[:, HD:], v[:, HD:]], axis=1)
    qc0 = jnp.concatenate([q[:, :HD], c[:, :HD]], axis=1)
    qc1 = jnp.concatenate([q[:, HD:], c[:, HD:]], axis=1)

    @pl.when(first)
    def _():
        mine[:RUN] = kv0
        mine[RUN:] = qc0
        theirs[:RUN] = kv1
        theirs[RUN:] = qc1

    @pl.when(jnp.logical_not(first))
    def _():
        mine[:RUN] = kv1
        mine[RUN:] = qc1
        theirs[:RUN] = kv0
        theirs[RUN:] = qc0


def places(section, flip, along):
    shape = (1, SEC) if along == 1 else (SEC, 1)
    i = lax.broadcasted_iota(jnp.int32, shape, along)
    half = jnp.where(i >= RUN, 1 - flip, flip)
    return section * SEC + half * RUN + lax.bitwise_and(i, RUN - 1)


def section_at(own, offset):
    return lax.rem(own + offset + NSEC, NSEC)


def bring(own, offsets, pieces, part, feat, rows, joined, sems):
    copies = []
    for r, offset in enumerate(offsets):
        for half in range(2):
            to = rows.at[pl.ds(r * SEC + half * RUN, RUN)]
            copies.append((pieces[2 * r + half].at[pl.ds(part * RUN, RUN)], to))
        at = pl.multiple_of(section_at(own, offset) * SEC, SEC)
        copies.append((feat.at[pl.ds(at, SEC)], joined.at[pl.ds(r * SEC, SEC)]))
    copies = [pltpu.make_async_copy(a, b, sems.at[i]) for i, (a, b) in enumerate(copies)]
    for copy in copies:
        copy.start()
    return copies


def join_keys(count, kv_s, kp_s):
    lane = lax.broadcasted_iota(jnp.int32, (SEC, 128), 1)
    low, last = lane < HD, lane == HD + 8
    base = jnp.where(lane < HD + 8, 1.0, 0.0).astype(BF)
    sign = jnp.where(last, 1.0, jnp.where(lane < HD + 8, -1.0, 0.0)).astype(BF)
    for r in range(count):
        at = slice(r * SEC, (r + 1) * SEC)
        feat = (base + sign * kp_s[at]) * jnp.asarray(NEG, BF)
        kp_s[at] = jnp.where(low, kv_s[at], feat)


def join_queries(count, qc_s, q_s):
    low = low_lanes(SEC)
    for r in range(count):
        at = slice(r * SEC, (r + 1) * SEC)
        scaled = qc_s[at] * jnp.asarray(1.0 / math.sqrt(HD), BF)
        q_s[at] = jnp.where(low, scaled, q_s[at])


def upper_only(rows_s, joined_s, near_s):
    rows = rows_s[...]
    rows_s[...] = jnp.where(low_lanes(SEC), jnp.zeros_like(rows), rows)
    lane = lax.broadcasted_iota(jnp.int32, (SEC, 128), 1)
    joined = joined_s[...]
    near_s[...] = jnp.where(lane == HD + 8, jnp.zeros_like(joined), joined)


def bring_both(own, offsets, pieces, mine, other, feat, scratch):
    kv_s, kp_s, q_s, qn_s, c_s, sems, own_sems = scratch
    copies = bring(own, offsets, pieces, 0, feat, kv_s, kp_s, sems)
    copies += bring(own, (0,), (mine, other), 1, feat, c_s, q_s, own_sems)
    for copy in copies:
        copy.wait()
    join_keys(len(offsets), kv_s, kp_s)
    join_queries(1, c_s, q_s)
    upper_only(c_s, q_s, qn_s)


def scores_of(own, flip, chunk, c, offset, at, row_places, q_s, qn_s, kp_s):
    rows = slice(c * chunk, (c + 1) * chunk)
    s = dot(q_s[rows], kp_s[at, :], NT)
    if offset in (0, -1, 1):
        away = row_places[rows] - places(section_at(own, offset), flip, 1)
        s = jnp.where(jnp.abs(away) <= HALF, dot(qn_s[rows], kp_s[at, :], NT), s)
    return s


def forward_kernel(chunk, offsets, first, last, place, mine, other, feat, *refs):
    pieces, rest = refs[: 2 * len(offsets)], list(refs[2 * len(offsets) :])
    acc_in, peak_in = (None, None) if first else (rest.pop(0), rest.pop(0))
    if last:
        att_out, column_out, stats, *scratch = rest
    else:
        acc_out, peak_out, *scratch = rest
    kv_s, kp_s, q_s, qn_s, c_s = scratch[:5]
    flip, own = place[0], place[1]
    bring_both(own, offsets, pieces, mine, other, feat, scratch)
    row_places = places(own, flip, 0)
    for c in range(SEC // chunk):
        rows = slice(c * chunk, (c + 1) * chunk)
        if first:
            peak = jnp.full((chunk, 1), NEG, F32)
            total = jnp.zeros((chunk, 1), F32)
            acc = jnp.zeros((chunk, 128), F32)
        else:
            peak, total, acc = peak_in[rows, 0:1], peak_in[rows, 1:2], acc_in[rows]
        for r, offset in enumerate(offsets):
            at = slice(r * SEC, (r + 1) * SEC)
            s = scores_of(own, flip, chunk, c, offset, at, row_places, q_s, qn_s, kp_s)
            new_peak = jnp.maximum(peak, jnp.max(s, axis=1, keepdims=True))
            keep = jnp.exp(peak - new_peak)
            e = jnp.exp(s - new_peak)
            total = keep * total + jnp.sum(e, axis=1, keepdims=True)
            acc = keep * acc + dot(e.astype(BF), kv_s[at, :])
            peak = new_peak
        lanes = lax.broadcasted_iota(jnp.int32, (chunk, 128), 1)
        if not last:
            acc_out[rows] = acc
            peak_out[rows] = jnp.where(lanes == 0, peak, total)
            continue
        att = (acc / total).astype(BF)
        att_out[rows] = att
        log_total = peak + jnp.log(total)
        cot = c_s[rows].astype(F32)
        delta = jnp.sum(att.astype(F32) * cot, axis=1, keepdims=True)
        column = jnp.where(lanes == 0, log_total, delta)
        column_out[rows] = column
        turned = column.T
        for k in range(chunk // 128):
            at = c * (chunk // 128) + k
            stats[at : at + 1] = turned[0:1, k * 128 : (k + 1) * 128]
            stats[4 + at : 5 + at] = turned[1:2, k * 128 : (k + 1) * 128]


def queries_kernel(chunk, place, *refs):
    pieces, rest = refs[: 2 * NSEC], refs[2 * NSEC :]
    feat, att, column, packed, packed_other, *scratch = rest
    kv_s, kp_s, q_s, qn_s, c_s = scratch[:5]
    flip, own = place[0], place[1]
    bring_both(own, OFFSETS, pieces, pieces[0], pieces[1], feat, scratch)
    row_places = places(own, flip, 0)
    for c in range(SEC // chunk):
        rows = slice(c * chunk, (c + 1) * chunk)
        log_total, delta, cot = column[rows, 0:1], column[rows, 1:2], c_s[rows]

        def backward(offset, at, acc, c=c, log_total=log_total, delta=delta, cot=cot):
            s = scores_of(own, flip, chunk, c, offset, at, row_places, q_s, qn_s, kp_s)
            p = jnp.exp(s - log_total)
            kv = kv_s[at, :]
            ds = p * (dot(cot, kv, NT) - delta)
            return acc + dot(ds.astype(BF), kv)

        grad = jnp.zeros((chunk, 128), F32)
        for r in range(3):
            grad = backward(OFFSETS[r], slice(r * SEC, (r + 1) * SEC), grad)
        grad = lax.fori_loop(
            3,
            NSEC,
            lambda r, acc, backward=backward: backward(
                None, pl.ds(pl.multiple_of(r * SEC, SEC), SEC), acc
            ),
            grad,
        )
        grad = (grad * (1.0 / math.sqrt(HD))).astype(BF)
        joined = jnp.where(low_lanes(chunk), grad, att[rows])
        out = packed if c * chunk < RUN else packed_other
        at = (c * chunk) % RUN
        out[at : at + chunk] = joined


def keys_kernel(chunk, place, *refs):
    pieces, rest = refs[: 2 * NSEC], refs[2 * NSEC :]
    feat, stats, packed, packed_other, *scratch = rest
    qc_s, q_s, k_s, kn_s, v_s, sems, own_sems, stats_s, stats_sems = scratch
    flip, own = place[0], place[1]
    copies = bring(own, OFFSETS, pieces, 1, feat, qc_s, q_s, sems)
    copies += bring(own, (0,), pieces[:2], 0, feat, v_s, k_s, own_sems)
    for r, offset in enumerate(OFFSETS):
        at = pl.multiple_of(section_at(own, offset) * 8, 8)
        to = stats_s.at[pl.ds(r * 8, 8)]
        copies.append(pltpu.make_async_copy(stats.at[pl.ds(at, 8)], to, stats_sems.at[r]))
        copies[-1].start()
    for copy in copies:
        copy.wait()
    join_queries(NSEC, qc_s, q_s)
    join_keys(1, v_s, k_s)
    upper_only(v_s, k_s, kn_s)
    key_places = places(own, flip, 0)
    for c in range(SEC // chunk):
        rows = slice(c * chunk, (c + 1) * chunk)
        k, kn, v = k_s[rows], kn_s[rows], v_s[rows]

        def backward(near, r, at, state):
            key_acc, value_acc = state
            st = stats_s[pl.ds(pl.multiple_of(r * 8, 8), 8), :]
            log_total = jnp.concatenate([st[i : i + 1] for i in range(4)], axis=1)
            delta = jnp.concatenate([st[i : i + 1] for i in range(4, 8)], axis=1)
            qc = qc_s[at, :]
            s = dot(k, q_s[at, :], NT)
            if near:
                section = section_at(own, OFFSETS[r])
                away = key_places[rows] - places(section, flip, 1)
                s = jnp.where(jnp.abs(away) <= HALF, dot(kn, q_s[at, :], NT), s)
            p = jnp.exp(s - log_total)
            ds = p * (dot(v, qc, NT) - delta)
            key_acc = key_acc + dot(ds.astype(BF), qc)
            value_acc = value_acc + dot(p.astype(BF), qc)
            return key_acc, value_acc

        state = (jnp.zeros((chunk, 128), F32), jnp.zeros((chunk, 128), F32))
        for r in range(3):
            state = backward(True, r, slice(r * SEC, (r + 1) * SEC), state)

        def far(r, st, backward=backward):
            return backward(False, r, pl.ds(pl.multiple_of(r * SEC, SEC), SEC), st)

        key_acc, value_acc = lax.fori_loop(3, NSEC, far, state)
        joined = jnp.where(low_lanes(chunk), key_acc * (1.0 / math.sqrt(HD)), value_acc)
        out = packed if c * chunk < RUN else packed_other
        at = (c * chunk) % RUN
        out[at : at + chunk] = joined.astype(BF)


def weights_kernel(tok, tok_other, first, first_sent, second, second_sent, out):
    qa = dot(tok[...], first[...], TN) + dot(tok_other[...], first_sent[...], TN)
    kv = dot(tok[...], second[...], TN) + dot(tok_other[...], second_sent[...], TN)
    for p in range(16):
        out[p, :64] = kv[p * 64 : (p + 1) * 64].astype(BF)
        upper = qa[p * 32 : (p + 1) * 32, :HD]
        lower = qa[512 + p * 32 : 512 + (p + 1) * 32, :HD]
        out[p, 64:96] = jnp.concatenate([upper, lower], axis=1).astype(BF)


def sum_kernel(parts, out):
    total = parts[0].astype(F32)
    for p in range(1, 16):
        total = total + parts[p].astype(F32)
    total = total.astype(BF)
    for p in range(32):
        out[p] = total


def input_kernel(place, first, first_other, second, second_other, wq, wk, wv, att, keep, send):
    swap = place[0] != 0
    core = place[2]
    a, b, c, d = first[...], first_other[...], second[...], second_other[...]
    a, b = jnp.where(swap, b, a), jnp.where(swap, a, b)
    c, d = jnp.where(swap, d, c), jnp.where(swap, c, d)
    dq = jnp.concatenate([a[:, :HD], b[:, :HD]], axis=1)
    att[...] = jnp.concatenate([a[:, HD:], b[:, HD:]], axis=1)
    dk = jnp.concatenate([c[:, :HD], d[:, :HD]], axis=1)
    dv = jnp.concatenate([c[:, HD:], d[:, HD:]], axis=1)
    grad = dot(dq, wq[...], NT) + dot(dk, wk[...], NT) + dot(dv, wv[...], NT)
    for y in range(4):
        low, high = grad[y * 64 : y * 64 + 32], grad[y * 64 + 32 : y * 64 + 64]
        keep[y] = jnp.where(core == 0, low, high)
        send[y] = jnp.where(core == 0, high, low).astype(BF)


def assemble_kernel(parts, gq, gk, gv):
    for p in range(16):
        a, b = parts[2 * p].astype(F32), parts[2 * p + 1].astype(F32)
        low = jnp.concatenate([a[:, :HD], b[:, :HD]], axis=1)
        high = jnp.concatenate([a[:, HD:], b[:, HD:]], axis=1)
        gk[p * 64 : (p + 1) * 64] = low[:64]
        gv[p * 64 : (p + 1) * 64] = high[:64]
        gq[p * 32 : (p + 1) * 32] = low[64:]
        gq[512 + p * 32 : 512 + (p + 1) * 32] = high[64:]


def shift(a, step):
    return lax.ppermute(a, Z, [(i, (i + step) % NSEC) for i in range(NSEC)])


def swap(a):
    return lax.ppermute(a, "xh", [(0, 1), (1, 0)])


def on_device(tokens, wq, wk, wv, cotangent, doc_lengths, global_positions):
    shape = jax.ShapeDtypeStruct
    tok, cot = tokens[0], cotangent[0]
    xh, z, y, core = (lax.axis_index(a) for a in ("xh", Z, "y", "core"))
    place = jnp.stack([xh, z, core]).astype(jnp.int32)
    weight = pltpu.VMEM((1024, 128), BF)
    mine, theirs, feat = call(
        project_kernel,
        (shape((SEC, 128), BF),) * 2 + (shape((NSEC * SEC, 128), BF),),
        (place, doc_lengths, tok, wq, wk, wv, cot, global_positions),
        scratch=(
            pltpu.VMEM((RUN, 1024), BF),
            weight,
            weight,
            weight,
            pltpu.VMEM((RUN, 128), BF),
            pltpu.SemaphoreType.DMA((5,)),
        ),
        flops=6 * 256 * 1024 * 128,
        smem=2,
        manual=5,
        limit=64 << 20,
    )
    other = swap(theirs)
    tok_other = swap(tok)
    part, own_sems = pltpu.VMEM((SEC, 128), BF), pltpu.SemaphoreType.DMA((3,))
    pairs = SEC * SEC
    wide = shape((SEC, 128), F32)

    def forward(lo, hi, place, pieces, state):
        n, last = hi - lo, hi == NSEC
        outs = (shape((SEC, 128), BF), wide, shape((8, 128), F32)) if last else (wide, wide)
        keys = pltpu.VMEM((n * SEC, 128), BF)
        return call(
            functools.partial(forward_kernel, 256, OFFSETS[lo:hi], lo == 0, last),
            outs,
            (place, mine, other, feat, *pieces, *state),
            scratch=(keys, keys, part, part, part, pltpu.SemaphoreType.DMA((3 * n,)), own_sems),
            flops=2 * 128 * 2 * n * pairs,
            transcendentals=n * pairs,
            manual=3 + 2 * n,
        )

    tie = lax.optimization_barrier
    lower_a, upper_a = [mine, shift(mine, 1)], [mine, shift(mine, -1)]
    lower_b, upper_b = [other, shift(other, 1)], [other, shift(other, -1)]
    for x, step in ((lower_a, 1), (upper_a, -1), (lower_b, 1), (upper_b, -1)):
        x.append(shift(x[1], step))
    for x, step in ((lower_a, 1), (upper_a, -1), (lower_b, 1), (upper_b, -1)):
        x.append(shift(x[2], step))
    far = (shift(lower_a[3], 1), shift(upper_b[3], -1))
    pieces = (mine, other)
    for i in (1, 2, 3):
        pieces += (lower_a[i], lower_b[i], upper_a[i], upper_b[i])
    pieces += far
    state = ()
    for lo, hi in CALLS:
        state = forward(lo, hi, place, pieces[2 * lo : 2 * hi], state)
    att_rows, column, stats = state
    all_stats = lax.all_to_all(
        jnp.broadcast_to(stats[None], (NSEC, 8, 128)), Z, 0, 0, tiled=True
    ).reshape(NSEC * 8, 128)
    whole = pltpu.VMEM((NSEC * SEC, 128), BF)
    half = shape((RUN, 128), BF)
    first, first_sent = call(
        functools.partial(queries_kernel, 256),
        (half, half),
        (place, *pieces, feat, att_rows, column),
        scratch=(whole, whole, part, part, part, pltpu.SemaphoreType.DMA((24,)), own_sems),
        flops=2 * 128 * 3 * NSEC * pairs,
        manual=17,
        transcendentals=NSEC * pairs,
    )
    all_stats, first, first_sent = lax.optimization_barrier((all_stats, first, first_sent))
    first_other = swap(first_sent)
    stats_scratch = (pltpu.VMEM((NSEC * 8, 128), F32), pltpu.SemaphoreType.DMA((NSEC,)))
    second, second_sent = call(
        functools.partial(keys_kernel, 256),
        (half, half),
        (place, *pieces, feat, all_stats),
        scratch=(whole, whole, part, part, part, pltpu.SemaphoreType.DMA((24,)), own_sems) + stats_scratch,
        flops=2 * 128 * 4 * NSEC * pairs,
        manual=18,
        transcendentals=NSEC * pairs,
    )
    second, second_sent, first_other = lax.optimization_barrier((second, second_sent, first_other))
    second_other = swap(second_sent)
    partial = call(
        weights_kernel,
        shape((16, 96, 128), BF),
        (tok, tok_other, first, first_sent, second, second_sent),
        flops=2 * 512 * 1024 * 256,
        smem=0,
    )
    partial = lax.all_to_all(partial, ("b",) + Z, 0, 0, tiled=True)
    partial, second_other = tie((partial, second_other))
    total = call(sum_kernel, shape((32, 96, 128), BF), (partial,), smem=0)
    att, keep, send = call(
        input_kernel,
        (half, shape((4, 32, 1024), F32), shape((4, 32, 1024), BF)),
        (place, first, first_other, second, second_other, wq, wk, wv),
        flops=6 * 256 * 1024 * 128,
    )
    arrived = lax.ppermute(send, "core", [(0, 1), (1, 0)])
    both = keep + arrived.astype(F32)
    share = lax.dynamic_index_in_dim(both, y, 0, False)
    both_bf = both.astype(BF)
    for k in (1, 2, 3):
        out = lax.dynamic_index_in_dim(both_bf, lax.bitwise_xor(y, k), 0, False)
        share = share + lax.ppermute(out, "y", [(i, i ^ k) for i in range(4)]).astype(F32)
    total = lax.all_to_all(total, ("b",) + CTX, 0, 0, tiled=True)
    gq, gk, gv = call(assemble_kernel, (shape((1024, 128), F32),) * 3, (total,), smem=0)
    return att[None], share.astype(BF)[None], gq, gk, gv


def solution(mesh):
    devices = mesh.devices.reshape(2, 2, 2, 2, 2, 4, 2)
    fine = Mesh(devices, ("b",) + CTX + TP)
    in_specs = (
        P("b", CTX, None),
        P(None, TP),
        P(None, TP),
        P(None, TP),
        P("b", CTX, TP),
        P("b", None),
        P("b", None),
    )
    out_specs = (
        P("b", CTX, TP),
        P("b", CTX + TP, None),
        P(None, TP),
        P(None, TP),
        P(None, TP),
    )
    return jax.shard_map(
        on_device, mesh=fine, in_specs=in_specs, out_specs=out_specs, check_vma=False
    )
```

```python
import functools
import math

import jax
import jax.numpy as jnp
from jax import lax
from jax.experimental import pallas as pl
from jax.experimental.pallas import tpu as pltpu
from jax.sharding import Mesh
from jax.sharding import PartitionSpec as P

HALF = 256
HD = 64
RUN = 256
SEC = 512
NSEC = 8
NEG = -1e30
LIMIT = 51 << 20
CHUNK = 512
BF = jnp.bfloat16
F32 = jnp.float32

Z = ("z2", "z1", "z0")
CTX = Z + ("xh",)
TP = ("y", "core")

OFFSETS = (0, -1, 1, -2, 2, -3, 3, 4)

NN = (((1,), (0,)), ((), ()))
NT = (((1,), (1,)), ((), ()))
TN = (((0,), (0,)), ((), ()))


def dot(a, b, dims=NN):
    return lax.dot_general(a, b, dims, preferred_element_type=F32)


def call(kernel, outs, args, scratch=(), flops=0, transcendentals=0, smem=1, manual=0, limit=None):
    specs = [pl.BlockSpec(memory_space=pltpu.SMEM)] * smem
    specs += [pl.BlockSpec(memory_space=pl.ANY)] * manual
    specs += [pl.BlockSpec(memory_space=pltpu.VMEM)] * (len(args) - smem - manual)
    moved = sum(a.size * a.dtype.itemsize for a in args)
    return pl.pallas_call(
        kernel,
        out_shape=outs,
        in_specs=specs,
        out_specs=jax.tree.map(lambda _: pl.BlockSpec(memory_space=pltpu.VMEM), outs),
        scratch_shapes=list(scratch),
        compiler_params=pltpu.CompilerParams(vmem_limit_bytes=limit or LIMIT),
        cost_estimate=pl.CostEstimate(
            flops=flops, bytes_accessed=moved, transcendentals=transcendentals
        ),
    )(*args)


def low_lanes(rows):
    return lax.broadcasted_iota(jnp.int32, (rows, 128), 1) < HD


def document_features(place, lengths, spots, feat):
    flip = place[0]
    lane = lax.broadcasted_iota(jnp.int32, (RUN, 128), 1)
    last = lane == HD + 8
    lane_row = lax.broadcasted_iota(jnp.int32, (1, 128), 1)
    starts, ends = jnp.zeros((1, 128), jnp.int32), jnp.zeros((1, 128), jnp.int32)
    start = jnp.int32(0)
    for d in range(8):
        end = start + lengths[0, d]
        starts = jnp.where(lane_row == HD + d, start, starts)
        ends = jnp.where(lane_row == HD + d, end, ends)
        start = end

    def one(block, carry):
        half = lax.rem(block, 2)
        run = (block - half) + jnp.where(half == flip, 0, 1)
        pos = run * RUN + lax.broadcasted_iota(jnp.int32, (RUN, RUN), 0)
        hit = jnp.where(pos == spots[...], 1.0, 0.0).astype(BF)
        other = 1.0 - dot(hit, jnp.ones((RUN, 128), BF))
        pos128 = run * RUN + lax.broadcasted_iota(jnp.int32, (RUN, 128), 0)
        member = (pos128 >= starts) & (pos128 < ends)
        row = jnp.where(last, other, jnp.where(member, 1.0, 0.0))
        at = pl.ds(pl.multiple_of(block * RUN, RUN), RUN)
        feat[at, :] = row.astype(BF)
        return carry

    lax.fori_loop(0, 2 * NSEC, one, 0)


def project_kernel(place, lengths, tok, wq, wk, wv, cot, spots, mine, theirs, feat, *scratch):
    tok_v, wk_v, wv_v, wq_v, cot_v, sems = scratch
    pairs = ((tok, tok_v), (wk, wk_v), (wv, wv_v), (wq, wq_v), (cot, cot_v))
    copies = [pltpu.make_async_copy(a, b, sems.at[i]) for i, (a, b) in enumerate(pairs)]
    for copy in copies:
        copy.start()
    document_features(place, lengths, spots, feat)
    first = place[0] == 0
    copies[0].wait()
    t = tok_v[...]
    copies[1].wait()
    k = dot(t, wk_v[...]).astype(BF)
    copies[2].wait()
    v = dot(t, wv_v[...]).astype(BF)
    copies[3].wait()
    q = dot(t, wq_v[...]).astype(BF)
    copies[4].wait()
    c = cot_v[...]
    kv0 = jnp.concatenate([k[:, :HD], v[:, :HD]], axis=1)
    kv1 = jnp.concatenate([k[:, HD:], v[:, HD:]], axis=1)
    qc0 = jnp.concatenate([q[:, :HD], c[:, :HD]], axis=1)
    qc1 = jnp.concatenate([q[:, HD:], c[:, HD:]], axis=1)

    @pl.when(first)
    def _():
        mine[:RUN] = kv0
        mine[RUN:] = qc0
        theirs[:RUN] = kv1
        theirs[RUN:] = qc1

    @pl.when(jnp.logical_not(first))
    def _():
        mine[:RUN] = kv1
        mine[RUN:] = qc1
        theirs[:RUN] = kv0
        theirs[RUN:] = qc0


def places(section, flip, along):
    shape = (1, SEC) if along == 1 else (SEC, 1)
    i = lax.broadcasted_iota(jnp.int32, shape, along)
    half = jnp.where(i >= RUN, 1 - flip, flip)
    return section * SEC + half * RUN + lax.bitwise_and(i, RUN - 1)


def section_at(own, offset):
    return lax.rem(own + offset + NSEC, NSEC)


def part_of(pieces, r, part):
    at = slice(part * RUN, (part + 1) * RUN)
    return jnp.concatenate([pieces[2 * r][at], pieces[2 * r + 1][at]], axis=0)


def features_at(feat, section):
    return feat[pl.ds(pl.multiple_of(section * SEC, SEC), SEC), :]


def join_key(kv, feat):
    lane = lax.broadcasted_iota(jnp.int32, kv.shape, 1)
    base = jnp.where(lane < HD + 8, 1.0, 0.0).astype(BF)
    sign = jnp.where(lane == HD + 8, 1.0, jnp.where(lane < HD + 8, -1.0, 0.0)).astype(BF)
    return jnp.where(lane < HD, kv, (base + sign * feat) * jnp.asarray(NEG, BF))


def join_query(qc, feat):
    low = lax.broadcasted_iota(jnp.int32, qc.shape, 1) < HD
    return jnp.where(low, qc * jnp.asarray(1.0 / math.sqrt(HD), BF), feat)


def less_global(joined):
    lane = lax.broadcasted_iota(jnp.int32, joined.shape, 1)
    return jnp.where(lane == HD + 8, jnp.zeros_like(joined), joined)


def right_half(rows):
    low = lax.broadcasted_iota(jnp.int32, rows.shape, 1) < HD
    return jnp.where(low, jnp.zeros_like(rows), rows)


def forward_kernel(chunk, place, *refs):
    pieces, (feat, att_out, column_out, stats) = refs[: 2 * NSEC], refs[2 * NSEC :]
    flip, own = place[0], place[1]
    own_qc = part_of(pieces, 0, 1)
    joined = join_query(own_qc, features_at(feat, own))
    near_rows = less_global(joined)
    row_places = places(own, flip, 0)
    count = SEC // chunk
    state = [None] * count
    for r, offset in enumerate(OFFSETS):
        section = section_at(own, offset)
        kv = part_of(pieces, r, 0)
        kp = join_key(kv, features_at(feat, section))
        for c in range(count):
            rows = slice(c * chunk, (c + 1) * chunk)
            s = dot(joined[rows], kp, NT)
            if r < 3:
                away = row_places[rows] - places(section, flip, 1)
                s = jnp.where(jnp.abs(away) <= HALF, dot(near_rows[rows], kp, NT), s)
            new_peak = jnp.max(s, axis=1, keepdims=True)
            if r > 0:
                peak, total, acc = state[c]
                new_peak = jnp.maximum(peak, new_peak)
                keep = jnp.exp(peak - new_peak)
            e = jnp.exp(s - new_peak)
            new_total = jnp.sum(e, axis=1, keepdims=True)
            new_acc = dot(e.astype(BF), kv)
            if r > 0:
                new_total, new_acc = keep * total + new_total, keep * acc + new_acc
            state[c] = new_peak, new_total, new_acc
    for c in range(count):
        rows = slice(c * chunk, (c + 1) * chunk)
        peak, total, acc = state[c]
        att = (acc / total).astype(BF)
        att_out[rows] = att
        log_total = peak + jnp.log(total)
        cot = right_half(own_qc[rows]).astype(F32)
        delta = jnp.sum(att.astype(F32) * cot, axis=1, keepdims=True)
        lanes = lax.broadcasted_iota(jnp.int32, (chunk, 128), 1)
        column = jnp.where(lanes == 0, log_total, delta)
        column_out[rows] = column
        turned = column.T
        for k in range(chunk // 128):
            at = c * (chunk // 128) + k
            for copy in range(NSEC):
                stats[copy, at : at + 1] = turned[0:1, k * 128 : (k + 1) * 128]
                stats[copy, 4 + at : 5 + at] = turned[1:2, k * 128 : (k + 1) * 128]


def queries_kernel(chunk, place, *refs):
    pieces, (feat, att, column, packed, packed_other) = refs[: 2 * NSEC], refs[2 * NSEC :]
    flip, own = place[0], place[1]
    own_qc = part_of(pieces, 0, 1)
    joined = join_query(own_qc, features_at(feat, own))
    near_rows, cot = less_global(joined), right_half(own_qc)
    row_places = places(own, flip, 0)
    count = SEC // chunk
    grads = [None] * count
    for r, offset in enumerate(OFFSETS):
        section = section_at(own, offset)
        kv = part_of(pieces, r, 0)
        kp = join_key(kv, features_at(feat, section))
        for c in range(count):
            rows = slice(c * chunk, (c + 1) * chunk)
            s = dot(joined[rows], kp, NT)
            if r < 3:
                away = row_places[rows] - places(section, flip, 1)
                s = jnp.where(jnp.abs(away) <= HALF, dot(near_rows[rows], kp, NT), s)
            p = jnp.exp(s - column[rows, 0:1])
            ds = p * (dot(cot[rows], kv, NT) - column[rows, 1:2])
            grad = dot(ds.astype(BF), kv)
            grads[c] = grad if r == 0 else grads[c] + grad
    grad = jnp.concatenate(grads, axis=0) if count > 1 else grads[0]
    grad = (grad * (1.0 / math.sqrt(HD))).astype(BF)
    out = jnp.where(low_lanes(SEC), grad, att[...])
    packed[...] = out[:RUN]
    packed_other[...] = out[RUN:]


def keys_kernel(chunk, place, *refs):
    pieces, (feat, stats, packed, packed_other, stats_s, sems) = refs[: 2 * NSEC], refs[2 * NSEC :]
    flip, own = place[0], place[1]
    copies = []
    for r, offset in enumerate(OFFSETS):
        at = pl.multiple_of(section_at(own, offset) * 8, 8)
        to = stats_s.at[pl.ds(r * 8, 8)]
        copies.append(pltpu.make_async_copy(stats.at[pl.ds(at, 8)], to, sems.at[r]))
        copies[-1].start()
    own_kv = part_of(pieces, 0, 0)
    joined = join_key(own_kv, features_at(feat, own))
    near_keys, value = less_global(joined), right_half(own_kv)
    key_places = places(own, flip, 0)
    count = SEC // chunk
    state = [None] * count
    for copy in copies:
        copy.wait()
    for r, offset in enumerate(OFFSETS):
        section = section_at(own, offset)
        qc = part_of(pieces, r, 1)
        qp = join_query(qc, features_at(feat, section))
        st = stats_s[r * 8 : r * 8 + 8]
        log_total = jnp.concatenate([st[i : i + 1] for i in range(4)], axis=1)
        delta = jnp.concatenate([st[i : i + 1] for i in range(4, 8)], axis=1)
        for c in range(count):
            rows = slice(c * chunk, (c + 1) * chunk)
            s = dot(joined[rows], qp, NT)
            if r < 3:
                away = key_places[rows] - places(section, flip, 1)
                s = jnp.where(jnp.abs(away) <= HALF, dot(near_keys[rows], qp, NT), s)
            p = jnp.exp(s - log_total)
            ds = p * (dot(value[rows], qc, NT) - delta)
            both = dot(ds.astype(BF), qc), dot(p.astype(BF), qc)
            state[c] = both if r == 0 else (state[c][0] + both[0], state[c][1] + both[1])
    key_acc = jnp.concatenate([x[0] for x in state], axis=0) if count > 1 else state[0][0]
    value_acc = jnp.concatenate([x[1] for x in state], axis=0) if count > 1 else state[0][1]
    out = jnp.where(low_lanes(SEC), key_acc * (1.0 / math.sqrt(HD)), value_acc).astype(BF)
    packed[...] = out[:RUN]
    packed_other[...] = out[RUN:]


def weights_kernel(tok, tok_other, first, first_sent, second, second_sent, out):
    qa = dot(tok[...], first[...], TN) + dot(tok_other[...], first_sent[...], TN)
    kv = dot(tok[...], second[...], TN) + dot(tok_other[...], second_sent[...], TN)
    for p in range(16):
        out[p, :64] = kv[p * 64 : (p + 1) * 64].astype(BF)
        upper = qa[p * 32 : (p + 1) * 32, :HD]
        lower = qa[512 + p * 32 : 512 + (p + 1) * 32, :HD]
        out[p, 64:96] = jnp.concatenate([upper, lower], axis=1).astype(BF)


def sum_kernel(parts, out):
    total = parts[0].astype(F32)
    for p in range(1, 16):
        total = total + parts[p].astype(F32)
    total = total.astype(BF)
    for p in range(32):
        out[p] = total


def input_kernel(place, first, first_other, second, second_other, wq, wk, wv, att, keep, send):
    swap = place[0] != 0
    core = place[2]
    a, b, c, d = first[...], first_other[...], second[...], second_other[...]
    a, b = jnp.where(swap, b, a), jnp.where(swap, a, b)
    c, d = jnp.where(swap, d, c), jnp.where(swap, c, d)
    dq = jnp.concatenate([a[:, :HD], b[:, :HD]], axis=1)
    att[...] = jnp.concatenate([a[:, HD:], b[:, HD:]], axis=1)
    dk = jnp.concatenate([c[:, :HD], d[:, :HD]], axis=1)
    dv = jnp.concatenate([c[:, HD:], d[:, HD:]], axis=1)
    grad = dot(dq, wq[...], NT) + dot(dk, wk[...], NT) + dot(dv, wv[...], NT)
    for y in range(4):
        low, high = grad[y * 64 : y * 64 + 32], grad[y * 64 + 32 : y * 64 + 64]
        keep[y] = jnp.where(core == 0, low, high)
        send[y] = jnp.where(core == 0, high, low).astype(BF)


def assemble_kernel(parts, gq, gk, gv):
    for p in range(16):
        a, b = parts[2 * p].astype(F32), parts[2 * p + 1].astype(F32)
        low = jnp.concatenate([a[:, :HD], b[:, :HD]], axis=1)
        high = jnp.concatenate([a[:, HD:], b[:, HD:]], axis=1)
        gk[p * 64 : (p + 1) * 64] = low[:64]
        gv[p * 64 : (p + 1) * 64] = high[:64]
        gq[p * 32 : (p + 1) * 32] = low[64:]
        gq[512 + p * 32 : 512 + (p + 1) * 32] = high[64:]


def shift(a, step):
    return lax.ppermute(a, Z, [(i, (i + step) % NSEC) for i in range(NSEC)])


def swap(a):
    return lax.ppermute(a, "xh", [(0, 1), (1, 0)])


def on_device(tokens, wq, wk, wv, cotangent, doc_lengths, global_positions):
    shape = jax.ShapeDtypeStruct
    tok, cot = tokens[0], cotangent[0]
    xh, z, y, core = (lax.axis_index(a) for a in ("xh", Z, "y", "core"))
    place = jnp.stack([xh, z, core]).astype(jnp.int32)
    weight = pltpu.VMEM((1024, 128), BF)
    mine, theirs, feat = call(
        project_kernel,
        (shape((SEC, 128), BF),) * 2 + (shape((NSEC * SEC, 128), BF),),
        (place, doc_lengths, tok, wq, wk, wv, cot, global_positions),
        scratch=(
            pltpu.VMEM((RUN, 1024), BF),
            weight,
            weight,
            weight,
            pltpu.VMEM((RUN, 128), BF),
            pltpu.SemaphoreType.DMA((5,)),
        ),
        flops=6 * 256 * 1024 * 128,
        smem=2,
        manual=5,
        limit=64 << 20,
    )
    other = swap(theirs)
    tok_other = swap(tok)
    pairs = SEC * SEC * NSEC
    wide = shape((SEC, 128), F32)

    tie = lax.optimization_barrier
    lower_a, upper_a = [mine, shift(mine, 1)], [mine, shift(mine, -1)]
    lower_b, upper_b = [other, shift(other, 1)], [other, shift(other, -1)]
    for x, step in ((lower_a, 1), (upper_a, -1), (lower_b, 1), (upper_b, -1)):
        x.append(shift(x[1], step))
    for x, step in ((lower_a, 1), (upper_a, -1), (lower_b, 1), (upper_b, -1)):
        x.append(shift(x[2], step))
    far = (shift(lower_a[3], 1), shift(upper_b[3], -1))
    pieces = (mine, other)
    for i in (1, 2, 3):
        pieces += (lower_a[i], lower_b[i], upper_a[i], upper_b[i])
    pieces += far
    att_rows, column, stats = call(
        functools.partial(forward_kernel, CHUNK),
        (shape((SEC, 128), BF), wide, shape((NSEC, 8, 128), F32)),
        (place, *pieces, feat),
        flops=2 * 128 * 2 * pairs,
        transcendentals=pairs,
    )
    all_stats = lax.all_to_all(stats, Z, 0, 0, tiled=True).reshape(NSEC * 8, 128)
    half = shape((RUN, 128), BF)
    first, first_sent = call(
        functools.partial(queries_kernel, CHUNK),
        (half, half),
        (place, *pieces, feat, att_rows, column),
        flops=2 * 128 * 3 * pairs,
        transcendentals=pairs,
    )
    all_stats, first, first_sent = lax.optimization_barrier((all_stats, first, first_sent))
    first_other = swap(first_sent)
    second, second_sent = call(
        functools.partial(keys_kernel, CHUNK),
        (half, half),
        (place, *pieces, feat, all_stats),
        scratch=(pltpu.VMEM((NSEC * 8, 128), F32), pltpu.SemaphoreType.DMA((NSEC,))),
        flops=2 * 128 * 4 * pairs,
        transcendentals=pairs,
    )
    second, second_sent, first_other = lax.optimization_barrier((second, second_sent, first_other))
    second_other = swap(second_sent)
    partial = call(
        weights_kernel,
        shape((16, 96, 128), BF),
        (tok, tok_other, first, first_sent, second, second_sent),
        flops=2 * 512 * 1024 * 256,
        smem=0,
    )
    partial = lax.all_to_all(partial, ("b",) + Z, 0, 0, tiled=True)
    partial, second_other = tie((partial, second_other))
    total = call(sum_kernel, shape((32, 96, 128), BF), (partial,), smem=0)
    att, keep, send = call(
        input_kernel,
        (half, shape((4, 32, 1024), F32), shape((4, 32, 1024), BF)),
        (place, first, first_other, second, second_other, wq, wk, wv),
        flops=6 * 256 * 1024 * 128,
    )
    arrived = lax.ppermute(send, "core", [(0, 1), (1, 0)])
    both = keep + arrived.astype(F32)
    share = lax.dynamic_index_in_dim(both, y, 0, False)
    both_bf = both.astype(BF)
    for k in (1, 2, 3):
        out = lax.dynamic_index_in_dim(both_bf, lax.bitwise_xor(y, k), 0, False)
        share = share + lax.ppermute(out, "y", [(i, i ^ k) for i in range(4)]).astype(F32)
    total = lax.all_to_all(total, ("b",) + CTX, 0, 0, tiled=True)
    gq, gk, gv = call(assemble_kernel, (shape((1024, 128), F32),) * 3, (total,), smem=0)
    return att[None], share.astype(BF)[None], gq, gk, gv


def solution(mesh):
    devices = mesh.devices.reshape(2, 2, 2, 2, 2, 4, 2)
    fine = Mesh(devices, ("b",) + CTX + TP)
    in_specs = (
        P("b", CTX, None),
        P(None, TP),
        P(None, TP),
        P(None, TP),
        P("b", CTX, TP),
        P("b", None),
        P("b", None),
    )
    out_specs = (
        P("b", CTX, TP),
        P("b", CTX + TP, None),
        P(None, TP),
        P(None, TP),
        P(None, TP),
    )
    return jax.shard_map(
        on_device, mesh=fine, in_specs=in_specs, out_specs=out_specs, check_vma=False
    )
```

```python
import functools
import math

import jax
import jax.numpy as jnp
from jax import lax
from jax.experimental import pallas as pl
from jax.experimental.pallas import tpu as pltpu
from jax.sharding import Mesh
from jax.sharding import PartitionSpec as P

HALF = 256
HD = 64
RUN = 256
SEC = 512
NSEC = 8
NEG = -1e30
LIMIT = 51 << 20
CHUNK = 512
FEATURE_LIMIT = 64 << 20
BF = jnp.bfloat16
F32 = jnp.float32

Z = ("z2", "z1", "z0")
CTX = Z + ("xh",)
TP = ("y", "core")

OFFSETS = (0, -1, 1, -2, 2, -3, 3, 4)

NN = (((1,), (0,)), ((), ()))
NT = (((1,), (1,)), ((), ()))
TN = (((0,), (0,)), ((), ()))


def dot(a, b, dims=NN):
    return lax.dot_general(a, b, dims, preferred_element_type=F32)


def call(kernel, outs, args, scratch=(), flops=0, transcendentals=0, smem=1, manual=0, limit=None):
    specs = [pl.BlockSpec(memory_space=pltpu.SMEM)] * smem
    specs += [pl.BlockSpec(memory_space=pl.ANY)] * manual
    specs += [pl.BlockSpec(memory_space=pltpu.VMEM)] * (len(args) - smem - manual)
    moved = sum(a.size * a.dtype.itemsize for a in args)
    return pl.pallas_call(
        kernel,
        out_shape=outs,
        in_specs=specs,
        out_specs=jax.tree.map(lambda _: pl.BlockSpec(memory_space=pltpu.VMEM), outs),
        scratch_shapes=list(scratch),
        compiler_params=pltpu.CompilerParams(vmem_limit_bytes=limit or LIMIT),
        cost_estimate=pl.CostEstimate(
            flops=flops, bytes_accessed=moved, transcendentals=transcendentals
        ),
    )(*args)


def low_lanes(rows):
    return lax.broadcasted_iota(jnp.int32, (rows, 128), 1) < HD


def feature_kernel(place, lengths, spots, feat):
    flip = place[0]
    lane = lax.broadcasted_iota(jnp.int32, (RUN, 128), 1)
    last = lane == HD + 8
    lane_row = lax.broadcasted_iota(jnp.int32, (1, 128), 1)
    starts, ends = jnp.zeros((1, 128), jnp.int32), jnp.zeros((1, 128), jnp.int32)
    start = jnp.int32(0)
    for d in range(8):
        end = start + lengths[0, d]
        starts = jnp.where(lane_row == HD + d, start, starts)
        ends = jnp.where(lane_row == HD + d, end, ends)
        start = end

    def one(block, carry):
        half = lax.rem(block, 2)
        run = (block - half) + jnp.where(half == flip, 0, 1)
        pos = run * RUN + lax.broadcasted_iota(jnp.int32, (RUN, RUN), 0)
        hit = jnp.max(jnp.where(pos == spots[...], 1.0, 0.0), axis=1, keepdims=True)
        other = 1.0 - hit
        pos128 = run * RUN + lax.broadcasted_iota(jnp.int32, (RUN, 128), 0)
        member = (pos128 >= starts) & (pos128 < ends)
        row = jnp.where(last, other, jnp.where(member, 1.0, 0.0))
        at = pl.ds(pl.multiple_of(block * RUN, RUN), RUN)
        feat[at, :] = row.astype(BF)
        return carry

    lax.fori_loop(0, 2 * NSEC, one, 0)


def project_kernel(place, tok, wq, wk, wv, cot, mine, theirs, *scratch):
    tok_v, wk_v, wv_v, wq_v, cot_v, sems = scratch
    pairs = ((tok, tok_v), (wk, wk_v), (wv, wv_v), (wq, wq_v), (cot, cot_v))
    copies = [pltpu.make_async_copy(a, b, sems.at[i]) for i, (a, b) in enumerate(pairs)]
    for copy in copies:
        copy.start()
    first = place[0] == 0
    copies[0].wait()
    t = tok_v[...]
    copies[1].wait()
    k = dot(t, wk_v[...]).astype(BF)
    copies[2].wait()
    v = dot(t, wv_v[...]).astype(BF)
    copies[3].wait()
    q = dot(t, wq_v[...]).astype(BF)
    copies[4].wait()
    c = cot_v[...]
    kv0 = jnp.concatenate([k[:, :HD], v[:, :HD]], axis=1)
    kv1 = jnp.concatenate([k[:, HD:], v[:, HD:]], axis=1)
    qc0 = jnp.concatenate([q[:, :HD], c[:, :HD]], axis=1)
    qc1 = jnp.concatenate([q[:, HD:], c[:, HD:]], axis=1)

    @pl.when(first)
    def _():
        mine[:RUN] = kv0
        mine[RUN:] = qc0
        theirs[:RUN] = kv1
        theirs[RUN:] = qc1

    @pl.when(jnp.logical_not(first))
    def _():
        mine[:RUN] = kv1
        mine[RUN:] = qc1
        theirs[:RUN] = kv0
        theirs[RUN:] = qc0


def places(section, flip, along):
    shape = (1, SEC) if along == 1 else (SEC, 1)
    i = lax.broadcasted_iota(jnp.int32, shape, along)
    half = jnp.where(i >= RUN, 1 - flip, flip)
    return section * SEC + half * RUN + lax.bitwise_and(i, RUN - 1)


def section_at(own, offset):
    return lax.rem(own + offset + NSEC, NSEC)


def part_of(pieces, r, part):
    at = slice(part * RUN, (part + 1) * RUN)
    return jnp.concatenate([pieces[2 * r][at], pieces[2 * r + 1][at]], axis=0)


def features_at(feat, section):
    return feat[pl.ds(pl.multiple_of(section * SEC, SEC), SEC), :]


def join_key(kv, feat):
    lane = lax.broadcasted_iota(jnp.int32, kv.shape, 1)
    base = jnp.where(lane < HD + 8, 1.0, 0.0).astype(BF)
    sign = jnp.where(lane == HD + 8, 1.0, jnp.where(lane < HD + 8, -1.0, 0.0)).astype(BF)
    return jnp.where(lane < HD, kv, (base + sign * feat) * jnp.asarray(NEG, BF))


def join_query(qc, feat):
    low = lax.broadcasted_iota(jnp.int32, qc.shape, 1) < HD
    return jnp.where(low, qc * jnp.asarray(1.0 / math.sqrt(HD), BF), feat)


def less_global(joined):
    lane = lax.broadcasted_iota(jnp.int32, joined.shape, 1)
    return jnp.where(lane == HD + 8, jnp.zeros_like(joined), joined)


def right_half(rows):
    low = lax.broadcasted_iota(jnp.int32, rows.shape, 1) < HD
    return jnp.where(low, jnp.zeros_like(rows), rows)


def forward_kernel(chunk, place, *refs):
    pieces, (feat, att_out, column_out, stats) = refs[: 2 * NSEC], refs[2 * NSEC :]
    flip, own = place[0], place[1]
    own_qc = part_of(pieces, 0, 1)
    joined = join_query(own_qc, features_at(feat, own))
    near_rows = less_global(joined)
    row_places = places(own, flip, 0)
    count = SEC // chunk
    state = [None] * count
    for r, offset in enumerate(OFFSETS):
        section = section_at(own, offset)
        kv = part_of(pieces, r, 0)
        kp = join_key(kv, features_at(feat, section))
        for c in range(count):
            rows = slice(c * chunk, (c + 1) * chunk)
            s = dot(joined[rows], kp, NT)
            if r < 3:
                away = row_places[rows] - places(section, flip, 1)
                s = jnp.where(jnp.abs(away) <= HALF, dot(near_rows[rows], kp, NT), s)
            new_peak = jnp.max(s, axis=1, keepdims=True)
            if r > 0:
                peak, total, acc = state[c]
                new_peak = jnp.maximum(peak, new_peak)
                keep = jnp.exp(peak - new_peak)
            e = jnp.exp(s - new_peak)
            new_total = jnp.sum(e, axis=1, keepdims=True)
            new_acc = dot(e.astype(BF), kv)
            if r > 0:
                new_total, new_acc = keep * total + new_total, keep * acc + new_acc
            state[c] = new_peak, new_total, new_acc
    for c in range(count):
        rows = slice(c * chunk, (c + 1) * chunk)
        peak, total, acc = state[c]
        att = (acc / total).astype(BF)
        att_out[rows] = att
        log_total = peak + jnp.log(total)
        cot = right_half(own_qc[rows]).astype(F32)
        delta = jnp.sum(att.astype(F32) * cot, axis=1, keepdims=True)
        lanes = lax.broadcasted_iota(jnp.int32, (chunk, 128), 1)
        column = jnp.where(lanes == 0, log_total, delta)
        column_out[rows] = column
        turned = column.T
        for k in range(chunk // 128):
            at = c * (chunk // 128) + k
            for copy in range(NSEC):
                stats[copy, at : at + 1] = turned[0:1, k * 128 : (k + 1) * 128]
                stats[copy, 4 + at : 5 + at] = turned[1:2, k * 128 : (k + 1) * 128]


def queries_kernel(chunk, place, *refs):
    pieces, (feat, att, column, packed, packed_other) = refs[: 2 * NSEC], refs[2 * NSEC :]
    flip, own = place[0], place[1]
    own_qc = part_of(pieces, 0, 1)
    joined = join_query(own_qc, features_at(feat, own))
    near_rows, cot = less_global(joined), right_half(own_qc)
    row_places = places(own, flip, 0)
    count = SEC // chunk
    grads = [None] * count
    for r, offset in enumerate(OFFSETS):
        section = section_at(own, offset)
        kv = part_of(pieces, r, 0)
        kp = join_key(kv, features_at(feat, section))
        for c in range(count):
            rows = slice(c * chunk, (c + 1) * chunk)
            s = dot(joined[rows], kp, NT)
            if r < 3:
                away = row_places[rows] - places(section, flip, 1)
                s = jnp.where(jnp.abs(away) <= HALF, dot(near_rows[rows], kp, NT), s)
            p = jnp.exp(s - column[rows, 0:1])
            ds = p * (dot(cot[rows], kv, NT) - column[rows, 1:2])
            grad = dot(ds.astype(BF), kv)
            grads[c] = grad if r == 0 else grads[c] + grad
    grad = jnp.concatenate(grads, axis=0) if count > 1 else grads[0]
    grad = (grad * (1.0 / math.sqrt(HD))).astype(BF)
    out = jnp.where(low_lanes(SEC), grad, att[...])
    packed[...] = out[:RUN]
    packed_other[...] = out[RUN:]


def keys_kernel(half, place, *refs):
    pieces, (feat, stats, *given, packed, stats_s, sems) = refs[: 2 * NSEC], refs[2 * NSEC :]
    flip, own = place[0], place[1]
    copies = []
    for r, offset in enumerate(OFFSETS):
        at = pl.multiple_of(section_at(own, offset) * 8, 8)
        to = stats_s.at[pl.ds(r * 8, 8)]
        copies.append(pltpu.make_async_copy(stats.at[pl.ds(at, 8)], to, sems.at[r]))
        copies[-1].start()
    own_kv = pieces[half][:RUN]
    joined = join_key(own_kv, features_at(feat, own)[half * RUN : (half + 1) * RUN])
    near_keys, value = less_global(joined), right_half(own_kv)
    key_places = places(own, flip, 0)[half * RUN : (half + 1) * RUN]
    state = None
    for copy in copies:
        copy.wait()
    for r, offset in enumerate(OFFSETS):
        section = section_at(own, offset)
        qc = part_of(pieces, r, 1)
        qp = join_query(qc, features_at(feat, section))
        st = stats_s[r * 8 : r * 8 + 8]
        log_total = jnp.concatenate([st[i : i + 1] for i in range(4)], axis=1)
        delta = jnp.concatenate([st[i : i + 1] for i in range(4, 8)], axis=1)
        s = dot(joined, qp, NT)
        if r < 3:
            away = key_places - places(section, flip, 1)
            s = jnp.where(jnp.abs(away) <= HALF, dot(near_keys, qp, NT), s)
        p = jnp.exp(s - log_total)
        ds = p * (dot(value, qc, NT) - delta)
        both = dot(ds.astype(BF), qc), dot(p.astype(BF), qc)
        state = both if r == 0 else (state[0] + both[0], state[1] + both[1])
    out = jnp.where(low_lanes(RUN), state[0] * (1.0 / math.sqrt(HD)), state[1]).astype(BF)
    if half == 1:
        packed[:RUN] = given[0][...]
        packed[RUN:] = out
    else:
        packed[...] = out


def weights_kernel(tok, tok_other, first, second, sent, out):
    qa = dot(tok[...], first[...], TN) + dot(tok_other[...], sent[:RUN], TN)
    kv = dot(tok[...], second[...], TN) + dot(tok_other[...], sent[RUN:], TN)
    for p in range(16):
        out[p, :64] = kv[p * 64 : (p + 1) * 64].astype(BF)
        upper = qa[p * 32 : (p + 1) * 32, :HD]
        lower = qa[512 + p * 32 : 512 + (p + 1) * 32, :HD]
        out[p, 64:96] = jnp.concatenate([upper, lower], axis=1).astype(BF)


def sum_kernel(parts, out):
    total = parts[0].astype(F32)
    for p in range(1, 16):
        total = total + parts[p].astype(F32)
    total = total.astype(BF)
    for p in range(32):
        out[p] = total


def input_kernel(place, first, second, arrived, wq, wk, wv, att, keep, send):
    swap = place[0] != 0
    core = place[2]
    a, b, c, d = first[...], arrived[:RUN], second[...], arrived[RUN:]
    a, b = jnp.where(swap, b, a), jnp.where(swap, a, b)
    c, d = jnp.where(swap, d, c), jnp.where(swap, c, d)
    dq = jnp.concatenate([a[:, :HD], b[:, :HD]], axis=1)
    att[...] = jnp.concatenate([a[:, HD:], b[:, HD:]], axis=1)
    dk = jnp.concatenate([c[:, :HD], d[:, :HD]], axis=1)
    dv = jnp.concatenate([c[:, HD:], d[:, HD:]], axis=1)
    grad = dot(dq, wq[...], NT) + dot(dk, wk[...], NT) + dot(dv, wv[...], NT)
    for y in range(4):
        low, high = grad[y * 64 : y * 64 + 32], grad[y * 64 + 32 : y * 64 + 64]
        keep[y] = jnp.where(core == 0, low, high)
        send[y] = jnp.where(core == 0, high, low).astype(BF)


def assemble_kernel(parts, gq, gk, gv):
    for p in range(16):
        a, b = parts[2 * p].astype(F32), parts[2 * p + 1].astype(F32)
        low = jnp.concatenate([a[:, :HD], b[:, :HD]], axis=1)
        high = jnp.concatenate([a[:, HD:], b[:, HD:]], axis=1)
        gk[p * 64 : (p + 1) * 64] = low[:64]
        gv[p * 64 : (p + 1) * 64] = high[:64]
        gq[p * 32 : (p + 1) * 32] = low[64:]
        gq[512 + p * 32 : 512 + (p + 1) * 32] = high[64:]


def shift(a, step):
    return lax.ppermute(a, Z, [(i, (i + step) % NSEC) for i in range(NSEC)])


def swap(a):
    return lax.ppermute(a, "xh", [(0, 1), (1, 0)])


def on_device(tokens, wq, wk, wv, cotangent, doc_lengths, global_positions):
    shape = jax.ShapeDtypeStruct
    tok, cot = tokens[0], cotangent[0]
    xh, z, y, core = (lax.axis_index(a) for a in ("xh", Z, "y", "core"))
    place = jnp.stack([xh, z, core]).astype(jnp.int32)
    weight = pltpu.VMEM((1024, 128), BF)
    mine, theirs = call(
        project_kernel,
        (shape((SEC, 128), BF),) * 2,
        (place, tok, wq, wk, wv, cot),
        scratch=(
            pltpu.VMEM((RUN, 1024), BF),
            weight,
            weight,
            weight,
            pltpu.VMEM((RUN, 128), BF),
            pltpu.SemaphoreType.DMA((5,)),
        ),
        flops=6 * 256 * 1024 * 128,
        manual=5,
        limit=64 << 20,
    )
    other = swap(theirs)
    tok_other = swap(tok)
    pairs = SEC * SEC * NSEC
    wide = shape((SEC, 128), F32)

    tie = lax.optimization_barrier
    lower_a, upper_a = [mine, shift(mine, 1)], [mine, shift(mine, -1)]
    late, mine = tie((place, mine))
    feat = call(
        feature_kernel,
        shape((NSEC * SEC, 128), BF),
        (late, doc_lengths, global_positions),
        smem=2,
        limit=FEATURE_LIMIT,
    )
    other, feat = tie((other, feat))
    lower_b, upper_b = [other, shift(other, 1)], [other, shift(other, -1)]
    for x, step in ((lower_a, 1), (upper_a, -1), (lower_b, 1), (upper_b, -1)):
        x.append(shift(x[1], step))
    for x, step in ((lower_a, 1), (upper_a, -1), (lower_b, 1), (upper_b, -1)):
        x.append(shift(x[2], step))
    far = (shift(lower_a[3], 1), shift(upper_b[3], -1))
    pieces = (mine, other)
    for i in (1, 2, 3):
        pieces += (lower_a[i], lower_b[i], upper_a[i], upper_b[i])
    pieces += far
    att_rows, column, stats = call(
        functools.partial(forward_kernel, CHUNK),
        (shape((SEC, 128), BF), wide, shape((NSEC, 8, 128), F32)),
        (place, *pieces, feat),
        flops=2 * 128 * 2 * pairs,
        transcendentals=pairs,
    )
    all_stats = lax.all_to_all(stats, Z, 0, 0, tiled=True).reshape(NSEC * 8, 128)
    half = shape((RUN, 128), BF)
    first, first_sent = call(
        functools.partial(queries_kernel, CHUNK),
        (half, half),
        (place, *pieces, feat, att_rows, column),
        flops=2 * 128 * 3 * pairs,
        transcendentals=pairs,
    )
    all_stats, first, first_sent = tie((all_stats, first, first_sent))

    def keys(half, stats, given, out):
        return call(
            functools.partial(keys_kernel, half),
            out,
            (place, *pieces, feat, stats, *given),
            scratch=(pltpu.VMEM((NSEC * 8, 128), F32), pltpu.SemaphoreType.DMA((NSEC,))),
            flops=2 * 128 * 2 * pairs,
            transcendentals=pairs // 2,
        )

    sent = keys(1, all_stats, (first_sent,), shape((SEC, 128), BF))
    all_stats, sent = tie((all_stats, sent))
    back = swap(sent)
    second = keys(0, all_stats, (), half)
    partial = call(
        weights_kernel,
        shape((16, 96, 128), BF),
        (tok, tok_other, first, second, sent),
        flops=2 * 512 * 1024 * 256,
        smem=0,
    )
    partial, back = tie((partial, back))
    partial = lax.all_to_all(partial, ("b",) + Z, 0, 0, tiled=True)
    att, keep, send = call(
        input_kernel,
        (half, shape((4, 32, 1024), F32), shape((4, 32, 1024), BF)),
        (place, first, second, back, wq, wk, wv),
        flops=6 * 256 * 1024 * 128,
    )
    arrived = lax.ppermute(send, "core", [(0, 1), (1, 0)])
    partial, arrived = tie((partial, arrived))
    total = call(sum_kernel, shape((32, 96, 128), BF), (partial,), smem=0)
    both = keep + arrived.astype(F32)
    share = lax.dynamic_index_in_dim(both, y, 0, False)
    both_bf = both.astype(BF)
    for k in (1, 2, 3):
        out = lax.dynamic_index_in_dim(both_bf, lax.bitwise_xor(y, k), 0, False)
        share = share + lax.ppermute(out, "y", [(i, i ^ k) for i in range(4)]).astype(F32)
    total = lax.all_to_all(total, ("b",) + CTX, 0, 0, tiled=True)
    gq, gk, gv = call(assemble_kernel, (shape((1024, 128), F32),) * 3, (total,), smem=0)
    return att[None], share.astype(BF)[None], gq, gk, gv


def solution(mesh):
    devices = mesh.devices.reshape(2, 2, 2, 2, 2, 4, 2)
    fine = Mesh(devices, ("b",) + CTX + TP)
    in_specs = (
        P("b", CTX, None),
        P(None, TP),
        P(None, TP),
        P(None, TP),
        P("b", CTX, TP),
        P("b", None),
        P("b", None),
    )
    out_specs = (
        P("b", CTX, TP),
        P("b", CTX + TP, None),
        P(None, TP),
        P(None, TP),
        P(None, TP),
    )
    return jax.shard_map(
        on_device, mesh=fine, in_specs=in_specs, out_specs=out_specs, check_vma=False
    )
```

```python
import functools
import math

import jax
import jax.numpy as jnp
from jax import lax
from jax.experimental import pallas as pl
from jax.experimental.pallas import tpu as pltpu
from jax.sharding import Mesh
from jax.sharding import PartitionSpec as P

HALF = 256
HD = 64
RUN = 256
SEC = 512
NSEC = 8
NEG = -1e30
LIMIT = 51 << 20
CHUNK = 512
FEATURE_LIMIT = 64 << 20
BF = jnp.bfloat16
F32 = jnp.float32

Z = ("z2", "z1", "z0")
CTX = Z + ("xh",)
TP = ("y", "core")

OFFSETS = (0, -1, 1, -2, 2, -3, 3, 4)

NN = (((1,), (0,)), ((), ()))
NT = (((1,), (1,)), ((), ()))
TN = (((0,), (0,)), ((), ()))


def dot(a, b, dims=NN):
    return lax.dot_general(a, b, dims, preferred_element_type=F32)


def call(kernel, outs, args, scratch=(), flops=0, transcendentals=0, smem=1, manual=0, limit=None):
    specs = [pl.BlockSpec(memory_space=pltpu.SMEM)] * smem
    specs += [pl.BlockSpec(memory_space=pl.ANY)] * manual
    specs += [pl.BlockSpec(memory_space=pltpu.VMEM)] * (len(args) - smem - manual)
    moved = sum(a.size * a.dtype.itemsize for a in args)
    return pl.pallas_call(
        kernel,
        out_shape=outs,
        in_specs=specs,
        out_specs=jax.tree.map(lambda _: pl.BlockSpec(memory_space=pltpu.VMEM), outs),
        scratch_shapes=list(scratch),
        compiler_params=pltpu.CompilerParams(vmem_limit_bytes=limit or LIMIT),
        cost_estimate=pl.CostEstimate(
            flops=flops, bytes_accessed=moved, transcendentals=transcendentals
        ),
    )(*args)


def low_lanes(rows):
    return lax.broadcasted_iota(jnp.int32, (rows, 128), 1) < HD


def feature_kernel(place, lengths, spots, feat):
    flip = place[0]
    lane = lax.broadcasted_iota(jnp.int32, (RUN, 128), 1)
    last = lane == HD + 8
    lane_row = lax.broadcasted_iota(jnp.int32, (1, 128), 1)
    starts, ends = jnp.zeros((1, 128), jnp.int32), jnp.zeros((1, 128), jnp.int32)
    start = jnp.int32(0)
    for d in range(8):
        end = start + lengths[0, d]
        starts = jnp.where(lane_row == HD + d, start, starts)
        ends = jnp.where(lane_row == HD + d, end, ends)
        start = end

    def one(block, carry):
        half = lax.rem(block, 2)
        run = (block - half) + jnp.where(half == flip, 0, 1)
        pos = run * RUN + lax.broadcasted_iota(jnp.int32, (RUN, RUN), 0)
        hit = jnp.max(jnp.where(pos == spots[...], 1.0, 0.0), axis=1, keepdims=True)
        other = 1.0 - hit
        pos128 = run * RUN + lax.broadcasted_iota(jnp.int32, (RUN, 128), 0)
        member = (pos128 >= starts) & (pos128 < ends)
        row = jnp.where(last, other, jnp.where(member, 1.0, 0.0))
        at = pl.ds(pl.multiple_of(block * RUN, RUN), RUN)
        feat[at, :] = row.astype(BF)
        return carry

    lax.fori_loop(0, 2 * NSEC, one, 0)


def project_kernel(place, tok, wq, wk, wv, cot, mine, theirs, *scratch):
    tok_v, wk_v, wv_v, wq_v, cot_v, sems = scratch
    pairs = ((tok, tok_v), (wk, wk_v), (wv, wv_v), (wq, wq_v), (cot, cot_v))
    copies = [pltpu.make_async_copy(a, b, sems.at[i]) for i, (a, b) in enumerate(pairs)]
    for copy in copies:
        copy.start()
    first = place[0] == 0
    copies[0].wait()
    t = tok_v[...]
    copies[1].wait()
    k = dot(t, wk_v[...]).astype(BF)
    copies[2].wait()
    v = dot(t, wv_v[...]).astype(BF)
    copies[3].wait()
    q = dot(t, wq_v[...]).astype(BF)
    copies[4].wait()
    c = cot_v[...]
    kv0 = jnp.concatenate([k[:, :HD], v[:, :HD]], axis=1)
    kv1 = jnp.concatenate([k[:, HD:], v[:, HD:]], axis=1)
    qc0 = jnp.concatenate([q[:, :HD], c[:, :HD]], axis=1)
    qc1 = jnp.concatenate([q[:, HD:], c[:, HD:]], axis=1)

    @pl.when(first)
    def _():
        mine[:RUN] = kv0
        mine[RUN:] = qc0
        theirs[:RUN] = kv1
        theirs[RUN:] = qc1

    @pl.when(jnp.logical_not(first))
    def _():
        mine[:RUN] = kv1
        mine[RUN:] = qc1
        theirs[:RUN] = kv0
        theirs[RUN:] = qc0


def places(section, flip, along):
    shape = (1, SEC) if along == 1 else (SEC, 1)
    i = lax.broadcasted_iota(jnp.int32, shape, along)
    half = jnp.where(i >= RUN, 1 - flip, flip)
    return section * SEC + half * RUN + lax.bitwise_and(i, RUN - 1)


def section_at(own, offset):
    return lax.rem(own + offset + NSEC, NSEC)


def part_of(pieces, r, part):
    at = slice(part * RUN, (part + 1) * RUN)
    return jnp.concatenate([pieces[2 * r][at], pieces[2 * r + 1][at]], axis=0)


def features_at(feat, section):
    return feat[pl.ds(pl.multiple_of(section * SEC, SEC), SEC), :]


def join_key(kv, feat):
    lane = lax.broadcasted_iota(jnp.int32, kv.shape, 1)
    base = jnp.where(lane < HD + 8, 1.0, 0.0).astype(BF)
    sign = jnp.where(lane == HD + 8, 1.0, jnp.where(lane < HD + 8, -1.0, 0.0)).astype(BF)
    return jnp.where(lane < HD, kv, (base + sign * feat) * jnp.asarray(NEG, BF))


def join_query(qc, feat):
    low = lax.broadcasted_iota(jnp.int32, qc.shape, 1) < HD
    return jnp.where(low, qc * jnp.asarray(1.0 / math.sqrt(HD), BF), feat)


def less_global(joined):
    lane = lax.broadcasted_iota(jnp.int32, joined.shape, 1)
    return jnp.where(lane == HD + 8, jnp.zeros_like(joined), joined)


def right_half(rows):
    low = lax.broadcasted_iota(jnp.int32, rows.shape, 1) < HD
    return jnp.where(low, jnp.zeros_like(rows), rows)


def near_only(own, flip, r, own_places, near, plain):
    if r > 2:
        return plain
    away = own_places - places(section_at(own, OFFSETS[r]), flip, 1)
    return jnp.where(jnp.abs(away) <= HALF, near, plain)


def forward_kernel(place, *refs):
    pieces, (feat, att_out, column_out, stats) = refs[: 2 * NSEC], refs[2 * NSEC :]
    flip, own = place[0], place[1]
    own_qc = part_of(pieces, 0, 1)
    joined = join_query(own_qc, features_at(feat, own))
    near_rows = less_global(joined)
    row_places = places(own, flip, 0)

    def products(r):
        kp = join_key(part_of(pieces, r, 0), features_at(feat, section_at(own, OFFSETS[r])))
        return dot(joined, kp, NT), dot(near_rows, kp, NT) if r < 3 else None

    ahead = products(0)
    for r in range(NSEC):
        plain, near = ahead
        if r + 1 < NSEC:
            ahead = products(r + 1)
        s = near_only(own, flip, r, row_places, near, plain)
        new_peak = jnp.max(s, axis=1, keepdims=True)
        if r > 0:
            new_peak = jnp.maximum(peak, new_peak)
            keep = jnp.exp(peak - new_peak)
        e = jnp.exp(s - new_peak)
        new_total = jnp.sum(e, axis=1, keepdims=True)
        new_acc = dot(e.astype(BF), part_of(pieces, r, 0))
        if r > 0:
            new_total, new_acc = keep * total + new_total, keep * acc + new_acc
        peak, total, acc = new_peak, new_total, new_acc
    att = (acc / total).astype(BF)
    att_out[...] = att
    cot = right_half(own_qc).astype(F32)
    delta = jnp.sum(att.astype(F32) * cot, axis=1, keepdims=True)
    lanes = lax.broadcasted_iota(jnp.int32, (SEC, 128), 1)
    column = jnp.where(lanes == 0, peak + jnp.log(total), delta)
    column_out[...] = column
    turned = column.T
    for k in range(SEC // 128):
        for copy in range(NSEC):
            stats[copy, k : k + 1] = turned[0:1, k * 128 : (k + 1) * 128]
            stats[copy, 4 + k : 5 + k] = turned[1:2, k * 128 : (k + 1) * 128]


def queries_kernel(chunk, place, *refs):
    pieces, (feat, att, column, packed, packed_other) = refs[: 2 * NSEC], refs[2 * NSEC :]
    flip, own = place[0], place[1]
    own_qc = part_of(pieces, 0, 1)
    joined = join_query(own_qc, features_at(feat, own))
    near_rows, cot = less_global(joined), right_half(own_qc)
    row_places = places(own, flip, 0)
    count = SEC // chunk
    grads = [None] * count
    for r, offset in enumerate(OFFSETS):
        section = section_at(own, offset)
        kv = part_of(pieces, r, 0)
        kp = join_key(kv, features_at(feat, section))
        for c in range(count):
            rows = slice(c * chunk, (c + 1) * chunk)
            s = dot(joined[rows], kp, NT)
            if r < 3:
                away = row_places[rows] - places(section, flip, 1)
                s = jnp.where(jnp.abs(away) <= HALF, dot(near_rows[rows], kp, NT), s)
            p = jnp.exp(s - column[rows, 0:1])
            ds = p * (dot(cot[rows], kv, NT) - column[rows, 1:2])
            grad = dot(ds.astype(BF), kv)
            grads[c] = grad if r == 0 else grads[c] + grad
    grad = jnp.concatenate(grads, axis=0) if count > 1 else grads[0]
    grad = (grad * (1.0 / math.sqrt(HD))).astype(BF)
    out = jnp.where(low_lanes(SEC), grad, att[...])
    packed[...] = out[:RUN]
    packed_other[...] = out[RUN:]


def keys_kernel(chunk, place, *refs):
    pieces, (feat, stats, given, packed, sent, stats_s, sems) = refs[: 2 * NSEC], refs[2 * NSEC :]
    flip, own = place[0], place[1]
    copies = []
    for r, offset in enumerate(OFFSETS):
        at = pl.multiple_of(section_at(own, offset) * 8, 8)
        to = stats_s.at[pl.ds(r * 8, 8)]
        copies.append(pltpu.make_async_copy(stats.at[pl.ds(at, 8)], to, sems.at[r]))
        copies[-1].start()
    own_kv = part_of(pieces, 0, 0)
    joined = join_key(own_kv, features_at(feat, own))
    near_keys, value = less_global(joined), right_half(own_kv)
    key_places = places(own, flip, 0)
    count = SEC // chunk
    state = [None] * count
    for copy in copies:
        copy.wait()
    for r, offset in enumerate(OFFSETS):
        section = section_at(own, offset)
        qc = part_of(pieces, r, 1)
        qp = join_query(qc, features_at(feat, section))
        st = stats_s[r * 8 : r * 8 + 8]
        log_total = jnp.concatenate([st[i : i + 1] for i in range(4)], axis=1)
        delta = jnp.concatenate([st[i : i + 1] for i in range(4, 8)], axis=1)
        for c in range(count):
            rows = slice(c * chunk, (c + 1) * chunk)
            s = dot(joined[rows], qp, NT)
            if r < 3:
                away = key_places[rows] - places(section, flip, 1)
                s = jnp.where(jnp.abs(away) <= HALF, dot(near_keys[rows], qp, NT), s)
            p = jnp.exp(s - log_total)
            ds = p * (dot(value[rows], qc, NT) - delta)
            both = dot(ds.astype(BF), qc), dot(p.astype(BF), qc)
            state[c] = both if r == 0 else (state[c][0] + both[0], state[c][1] + both[1])
    key_acc = jnp.concatenate([x[0] for x in state], axis=0) if count > 1 else state[0][0]
    value_acc = jnp.concatenate([x[1] for x in state], axis=0) if count > 1 else state[0][1]
    out = jnp.where(low_lanes(SEC), key_acc * (1.0 / math.sqrt(HD)), value_acc).astype(BF)
    packed[...] = out[:RUN]
    sent[:RUN] = given[...]
    sent[RUN:] = out[RUN:]


def weights_kernel(tok, tok_other, first, second, sent, out):
    qa = dot(tok[...], first[...], TN) + dot(tok_other[...], sent[:RUN], TN)
    kv = dot(tok[...], second[...], TN) + dot(tok_other[...], sent[RUN:], TN)
    for p in range(16):
        out[p, :64] = kv[p * 64 : (p + 1) * 64].astype(BF)
        upper = qa[p * 32 : (p + 1) * 32, :HD]
        lower = qa[512 + p * 32 : 512 + (p + 1) * 32, :HD]
        out[p, 64:96] = jnp.concatenate([upper, lower], axis=1).astype(BF)


def sum_kernel(parts, out):
    total = parts[0].astype(F32)
    for p in range(1, 16):
        total = total + parts[p].astype(F32)
    total = total.astype(BF)
    for p in range(32):
        out[p] = total


def input_kernel(place, first, second, arrived, wq, wk, wv, att, keep, send):
    swap = place[0] != 0
    core = place[2]
    a, b, c, d = first[...], arrived[:RUN], second[...], arrived[RUN:]
    a, b = jnp.where(swap, b, a), jnp.where(swap, a, b)
    c, d = jnp.where(swap, d, c), jnp.where(swap, c, d)
    dq = jnp.concatenate([a[:, :HD], b[:, :HD]], axis=1)
    att[...] = jnp.concatenate([a[:, HD:], b[:, HD:]], axis=1)
    dk = jnp.concatenate([c[:, :HD], d[:, :HD]], axis=1)
    dv = jnp.concatenate([c[:, HD:], d[:, HD:]], axis=1)
    grad = dot(dq, wq[...], NT) + dot(dk, wk[...], NT) + dot(dv, wv[...], NT)
    for y in range(4):
        low, high = grad[y * 64 : y * 64 + 32], grad[y * 64 + 32 : y * 64 + 64]
        keep[y] = jnp.where(core == 0, low, high)
        send[y] = jnp.where(core == 0, high, low).astype(BF)


def assemble_kernel(parts, gq, gk, gv):
    for p in range(16):
        a, b = parts[2 * p].astype(F32), parts[2 * p + 1].astype(F32)
        low = jnp.concatenate([a[:, :HD], b[:, :HD]], axis=1)
        high = jnp.concatenate([a[:, HD:], b[:, HD:]], axis=1)
        gk[p * 64 : (p + 1) * 64] = low[:64]
        gv[p * 64 : (p + 1) * 64] = high[:64]
        gq[p * 32 : (p + 1) * 32] = low[64:]
        gq[512 + p * 32 : 512 + (p + 1) * 32] = high[64:]


def shift(a, step):
    return lax.ppermute(a, Z, [(i, (i + step) % NSEC) for i in range(NSEC)])


def swap(a):
    return lax.ppermute(a, "xh", [(0, 1), (1, 0)])


def on_device(tokens, wq, wk, wv, cotangent, doc_lengths, global_positions):
    shape = jax.ShapeDtypeStruct
    tok, cot = tokens[0], cotangent[0]
    xh, z, y, core = (lax.axis_index(a) for a in ("xh", Z, "y", "core"))
    place = jnp.stack([xh, z, core]).astype(jnp.int32)
    weight = pltpu.VMEM((1024, 128), BF)
    mine, theirs = call(
        project_kernel,
        (shape((SEC, 128), BF),) * 2,
        (place, tok, wq, wk, wv, cot),
        scratch=(
            pltpu.VMEM((RUN, 1024), BF),
            weight,
            weight,
            weight,
            pltpu.VMEM((RUN, 128), BF),
            pltpu.SemaphoreType.DMA((5,)),
        ),
        flops=6 * 256 * 1024 * 128,
        manual=5,
        limit=64 << 20,
    )
    other = swap(theirs)
    tok_other = swap(tok)
    pairs = SEC * SEC * NSEC
    wide = shape((SEC, 128), F32)

    tie = lax.optimization_barrier
    lower_a, upper_a = [mine, shift(mine, 1)], [mine, shift(mine, -1)]
    late, mine = tie((place, mine))
    feat = call(
        feature_kernel,
        shape((NSEC * SEC, 128), BF),
        (late, doc_lengths, global_positions),
        smem=2,
        limit=FEATURE_LIMIT,
    )
    other, feat, lower_a[1], upper_a[1] = tie((other, feat, lower_a[1], upper_a[1]))
    lower_b, upper_b = [other, shift(other, 1)], [other, shift(other, -1)]
    for x, step in ((lower_a, 1), (upper_a, -1), (lower_b, 1), (upper_b, -1)):
        x.append(shift(x[1], step))
    for x, step in ((lower_a, 1), (upper_a, -1), (lower_b, 1), (upper_b, -1)):
        x.append(shift(x[2], step))
    far = (shift(lower_a[3], 1), shift(upper_b[3], -1))
    pieces = (mine, other)
    for i in (1, 2, 3):
        pieces += (lower_a[i], lower_b[i], upper_a[i], upper_b[i])
    pieces += far
    att_rows, column, stats = call(
        forward_kernel,
        (shape((SEC, 128), BF), wide, shape((NSEC, 8, 128), F32)),
        (place, *pieces, feat),
        flops=2 * 128 * 2 * pairs,
        transcendentals=pairs,
    )
    all_stats = lax.all_to_all(stats, Z, 0, 0, tiled=True).reshape(NSEC * 8, 128)
    half = shape((RUN, 128), BF)
    first, first_sent = call(
        functools.partial(queries_kernel, CHUNK),
        (half, half),
        (place, *pieces, feat, att_rows, column),
        flops=2 * 128 * 3 * pairs,
        transcendentals=pairs,
    )
    all_stats, first, first_sent = tie((all_stats, first, first_sent))
    second, sent = call(
        functools.partial(keys_kernel, CHUNK),
        (half, shape((SEC, 128), BF)),
        (place, *pieces, feat, all_stats, first_sent),
        scratch=(pltpu.VMEM((NSEC * 8, 128), F32), pltpu.SemaphoreType.DMA((NSEC,))),
        flops=2 * 128 * 4 * pairs,
        transcendentals=pairs,
    )
    back = swap(sent)
    partial = call(
        weights_kernel,
        shape((16, 96, 128), BF),
        (tok, tok_other, first, second, sent),
        flops=2 * 512 * 1024 * 256,
        smem=0,
    )
    partial = lax.all_to_all(partial, ("b",) + Z, 0, 0, tiled=True)
    att, keep, send = call(
        input_kernel,
        (half, shape((4, 32, 1024), F32), shape((4, 32, 1024), BF)),
        (place, first, second, back, wq, wk, wv),
        flops=6 * 256 * 1024 * 128,
    )
    partial, send = tie((partial, send))
    arrived = lax.ppermute(send, "core", [(0, 1), (1, 0)])
    total = call(sum_kernel, shape((32, 96, 128), BF), (partial,), smem=0)
    both = keep + arrived.astype(F32)
    share = lax.dynamic_index_in_dim(both, y, 0, False)
    both_bf = both.astype(BF)
    for k in (1, 2, 3):
        out = lax.dynamic_index_in_dim(both_bf, lax.bitwise_xor(y, k), 0, False)
        share = share + lax.ppermute(out, "y", [(i, i ^ k) for i in range(4)]).astype(F32)
    total = lax.all_to_all(total, ("b",) + CTX, 0, 0, tiled=True)
    gq, gk, gv = call(assemble_kernel, (shape((1024, 128), F32),) * 3, (total,), smem=0)
    return att[None], share.astype(BF)[None], gq, gk, gv


def solution(mesh):
    devices = mesh.devices.reshape(2, 2, 2, 2, 2, 4, 2)
    fine = Mesh(devices, ("b",) + CTX + TP)
    in_specs = (
        P("b", CTX, None),
        P(None, TP),
        P(None, TP),
        P(None, TP),
        P("b", CTX, TP),
        P("b", None),
        P("b", None),
    )
    out_specs = (
        P("b", CTX, TP),
        P("b", CTX + TP, None),
        P(None, TP),
        P(None, TP),
        P(None, TP),
    )
    return jax.shard_map(
        on_device, mesh=fine, in_specs=in_specs, out_specs=out_specs, check_vma=False
    )
```

```python
import functools
import math

import jax
import jax.numpy as jnp
from jax import lax
from jax.experimental import pallas as pl
from jax.experimental.pallas import tpu as pltpu
from jax.sharding import Mesh
from jax.sharding import PartitionSpec as P

HALF = 256
HD = 64
RUN = 256
SEC = 512
NSEC = 8
NEG = -1e30
LIMIT = 51 << 20
CHUNK = 512
SPLIT = 7
FEATURE_LIMIT = 64 << 20
BF = jnp.bfloat16
F32 = jnp.float32

Z = ("z2", "z1", "z0")
CTX = Z + ("xh",)
TP = ("y", "core")

OFFSETS = (0, -1, 1, -2, 2, -3, 3, 4)

NN = (((1,), (0,)), ((), ()))
NT = (((1,), (1,)), ((), ()))
TN = (((0,), (0,)), ((), ()))


def dot(a, b, dims=NN):
    return lax.dot_general(a, b, dims, preferred_element_type=F32)


def call(kernel, outs, args, scratch=(), flops=0, transcendentals=0, smem=1, manual=0, limit=None):
    specs = [pl.BlockSpec(memory_space=pltpu.SMEM)] * smem
    specs += [pl.BlockSpec(memory_space=pl.ANY)] * manual
    specs += [pl.BlockSpec(memory_space=pltpu.VMEM)] * (len(args) - smem - manual)
    moved = sum(a.size * a.dtype.itemsize for a in args)
    return pl.pallas_call(
        kernel,
        out_shape=outs,
        in_specs=specs,
        out_specs=jax.tree.map(lambda _: pl.BlockSpec(memory_space=pltpu.VMEM), outs),
        scratch_shapes=list(scratch),
        compiler_params=pltpu.CompilerParams(vmem_limit_bytes=limit or LIMIT),
        cost_estimate=pl.CostEstimate(
            flops=flops, bytes_accessed=moved, transcendentals=transcendentals
        ),
    )(*args)


def low_lanes(rows):
    return lax.broadcasted_iota(jnp.int32, (rows, 128), 1) < HD


def feature_kernel(place, lengths, spots, feat):
    flip = place[0]
    lane = lax.broadcasted_iota(jnp.int32, (RUN, 128), 1)
    last = lane == HD + 8
    lane_row = lax.broadcasted_iota(jnp.int32, (1, 128), 1)
    starts, ends = jnp.zeros((1, 128), jnp.int32), jnp.zeros((1, 128), jnp.int32)
    start = jnp.int32(0)
    for d in range(8):
        end = start + lengths[0, d]
        starts = jnp.where(lane_row == HD + d, start, starts)
        ends = jnp.where(lane_row == HD + d, end, ends)
        start = end

    def one(block, carry):
        half = lax.rem(block, 2)
        run = (block - half) + jnp.where(half == flip, 0, 1)
        pos = run * RUN + lax.broadcasted_iota(jnp.int32, (RUN, RUN), 0)
        hit = jnp.max(jnp.where(pos == spots[...], 1.0, 0.0), axis=1, keepdims=True)
        other = 1.0 - hit
        pos128 = run * RUN + lax.broadcasted_iota(jnp.int32, (RUN, 128), 0)
        member = (pos128 >= starts) & (pos128 < ends)
        row = jnp.where(last, other, jnp.where(member, 1.0, 0.0))
        at = pl.ds(pl.multiple_of(block * RUN, RUN), RUN)
        feat[at, :] = row.astype(BF)
        return carry

    lax.fori_loop(0, 2 * NSEC, one, 0)


def project_kernel(tok, wq, wk, wv, cot, mine, theirs, *scratch):
    tok_v, wk_v, wv_v, wq_v, cot_v, sems = scratch
    pairs = ((tok, tok_v), (wk, wk_v), (wv, wv_v), (wq, wq_v), (cot, cot_v))
    copies = [pltpu.make_async_copy(a, b, sems.at[i]) for i, (a, b) in enumerate(pairs)]
    for copy in copies:
        copy.start()
    first = lax.axis_index("xh") == 0
    copies[0].wait()
    t = tok_v[...]
    copies[1].wait()
    k = dot(t, wk_v[...]).astype(BF)
    copies[2].wait()
    v = dot(t, wv_v[...]).astype(BF)
    copies[3].wait()
    q = dot(t, wq_v[...]).astype(BF)
    copies[4].wait()
    c = cot_v[...]
    kv0 = jnp.concatenate([k[:, :HD], v[:, :HD]], axis=1)
    kv1 = jnp.concatenate([k[:, HD:], v[:, HD:]], axis=1)
    qc0 = jnp.concatenate([q[:, :HD], c[:, :HD]], axis=1)
    qc1 = jnp.concatenate([q[:, HD:], c[:, HD:]], axis=1)

    @pl.when(first)
    def _():
        mine[:RUN] = kv0
        mine[RUN:] = qc0
        theirs[:RUN] = kv1
        theirs[RUN:] = qc1

    @pl.when(jnp.logical_not(first))
    def _():
        mine[:RUN] = kv1
        mine[RUN:] = qc1
        theirs[:RUN] = kv0
        theirs[RUN:] = qc0


def places(section, flip, along):
    shape = (1, SEC) if along == 1 else (SEC, 1)
    i = lax.broadcasted_iota(jnp.int32, shape, along)
    half = jnp.where(i >= RUN, 1 - flip, flip)
    return section * SEC + half * RUN + lax.bitwise_and(i, RUN - 1)


def section_at(own, offset):
    return lax.rem(own + offset + NSEC, NSEC)


def part_of(pieces, r, part):
    at = slice(part * RUN, (part + 1) * RUN)
    return jnp.concatenate([pieces[2 * r][at], pieces[2 * r + 1][at]], axis=0)


def features_at(feat, section):
    return feat[pl.ds(pl.multiple_of(section * SEC, SEC), SEC), :]


def join_key(kv, feat):
    lane = lax.broadcasted_iota(jnp.int32, kv.shape, 1)
    base = jnp.where(lane < HD + 8, 1.0, 0.0).astype(BF)
    sign = jnp.where(lane == HD + 8, 1.0, jnp.where(lane < HD + 8, -1.0, 0.0)).astype(BF)
    return jnp.where(lane < HD, kv, (base + sign * feat) * jnp.asarray(NEG, BF))


def join_query(qc, feat):
    low = lax.broadcasted_iota(jnp.int32, qc.shape, 1) < HD
    return jnp.where(low, qc * jnp.asarray(1.0 / math.sqrt(HD), BF), feat)


def less_global(joined):
    lane = lax.broadcasted_iota(jnp.int32, joined.shape, 1)
    return jnp.where(lane == HD + 8, jnp.zeros_like(joined), joined)


def right_half(rows):
    low = lax.broadcasted_iota(jnp.int32, rows.shape, 1) < HD
    return jnp.where(low, jnp.zeros_like(rows), rows)


def near_only(own, flip, r, own_places, near, plain):
    if r > 2:
        return plain
    away = own_places - places(section_at(own, OFFSETS[r]), flip, 1)
    return jnp.where(jnp.abs(away) <= HALF, near, plain)


def forward_kernel(lo, hi, place, own_a, own_b, feat, *refs):
    pieces, refs = refs[: 2 * (hi - lo)], list(refs[2 * (hi - lo) :])
    flip, own = place[0], place[1]
    own_qc = part_of((own_a, own_b), 0, 1)
    joined = join_query(own_qc, features_at(feat, own))
    near_rows = less_global(joined)
    row_places = places(own, flip, 0)
    lanes = lax.broadcasted_iota(jnp.int32, (SEC, 128), 1)
    if lo > 0:
        acc_in, peak_in = refs.pop(0), refs.pop(0)
        peak, total, acc = peak_in[:, 0:1], peak_in[:, 1:2], acc_in[...]

    def products(r):
        kv = part_of(pieces, r - lo, 0)
        kp = join_key(kv, features_at(feat, section_at(own, OFFSETS[r])))
        return dot(joined, kp, NT), dot(near_rows, kp, NT) if r < 3 else None

    ahead = products(lo)
    for r in range(lo, hi):
        plain, near = ahead
        if r + 1 < hi:
            ahead = products(r + 1)
        s = near_only(own, flip, r, row_places, near, plain)
        new_peak = jnp.max(s, axis=1, keepdims=True)
        if r > 0:
            new_peak = jnp.maximum(peak, new_peak)
            keep = jnp.exp(peak - new_peak)
        e = jnp.exp(s - new_peak)
        new_total = jnp.sum(e, axis=1, keepdims=True)
        new_acc = dot(e.astype(BF), part_of(pieces, r - lo, 0))
        if r > 0:
            new_total, new_acc = keep * total + new_total, keep * acc + new_acc
        peak, total, acc = new_peak, new_total, new_acc
    if hi < NSEC:
        acc_out, peak_out = refs
        acc_out[...] = acc
        peak_out[...] = jnp.where(lanes == 0, peak, total)
        return
    att_out, column_out, stats = refs
    att = (acc / total).astype(BF)
    att_out[...] = att
    cot = right_half(own_qc).astype(F32)
    delta = jnp.sum(att.astype(F32) * cot, axis=1, keepdims=True)
    column = jnp.where(lanes == 0, peak + jnp.log(total), delta)
    column_out[...] = column
    turned = column.T
    for k in range(SEC // 128):
        for copy in range(NSEC):
            stats[copy, k : k + 1] = turned[0:1, k * 128 : (k + 1) * 128]
            stats[copy, 4 + k : 5 + k] = turned[1:2, k * 128 : (k + 1) * 128]


def queries_kernel(chunk, place, *refs):
    pieces, (feat, att, column, packed, packed_other) = refs[: 2 * NSEC], refs[2 * NSEC :]
    flip, own = place[0], place[1]
    own_qc = part_of(pieces, 0, 1)
    joined = join_query(own_qc, features_at(feat, own))
    near_rows, cot = less_global(joined), right_half(own_qc)
    row_places = places(own, flip, 0)
    count = SEC // chunk
    grads = [None] * count
    for r, offset in enumerate(OFFSETS):
        section = section_at(own, offset)
        kv = part_of(pieces, r, 0)
        kp = join_key(kv, features_at(feat, section))
        for c in range(count):
            rows = slice(c * chunk, (c + 1) * chunk)
            s = dot(joined[rows], kp, NT)
            if r < 3:
                away = row_places[rows] - places(section, flip, 1)
                s = jnp.where(jnp.abs(away) <= HALF, dot(near_rows[rows], kp, NT), s)
            p = jnp.exp(s - column[rows, 0:1])
            ds = p * (dot(cot[rows], kv, NT) - column[rows, 1:2])
            grad = dot(ds.astype(BF), kv)
            grads[c] = grad if r == 0 else grads[c] + grad
    grad = jnp.concatenate(grads, axis=0) if count > 1 else grads[0]
    grad = (grad * (1.0 / math.sqrt(HD))).astype(BF)
    out = jnp.where(low_lanes(SEC), grad, att[...])
    packed[...] = out[:RUN]
    packed_other[...] = out[RUN:]


def keys_kernel(chunk, place, *refs):
    pieces, (feat, stats, given, packed, sent, stats_s, sems) = refs[: 2 * NSEC], refs[2 * NSEC :]
    flip, own = place[0], place[1]
    copies = []
    for r, offset in enumerate(OFFSETS):
        at = pl.multiple_of(section_at(own, offset) * 8, 8)
        to = stats_s.at[pl.ds(r * 8, 8)]
        copies.append(pltpu.make_async_copy(stats.at[pl.ds(at, 8)], to, sems.at[r]))
        copies[-1].start()
    own_kv = part_of(pieces, 0, 0)
    joined = join_key(own_kv, features_at(feat, own))
    near_keys, value = less_global(joined), right_half(own_kv)
    key_places = places(own, flip, 0)
    count = SEC // chunk
    state = [None] * count
    for copy in copies:
        copy.wait()
    for r, offset in enumerate(OFFSETS):
        section = section_at(own, offset)
        qc = part_of(pieces, r, 1)
        qp = join_query(qc, features_at(feat, section))
        st = stats_s[r * 8 : r * 8 + 8]
        log_total = jnp.concatenate([st[i : i + 1] for i in range(4)], axis=1)
        delta = jnp.concatenate([st[i : i + 1] for i in range(4, 8)], axis=1)
        for c in range(count):
            rows = slice(c * chunk, (c + 1) * chunk)
            s = dot(joined[rows], qp, NT)
            if r < 3:
                away = key_places[rows] - places(section, flip, 1)
                s = jnp.where(jnp.abs(away) <= HALF, dot(near_keys[rows], qp, NT), s)
            p = jnp.exp(s - log_total)
            ds = p * (dot(value[rows], qc, NT) - delta)
            both = dot(ds.astype(BF), qc), dot(p.astype(BF), qc)
            state[c] = both if r == 0 else (state[c][0] + both[0], state[c][1] + both[1])
    key_acc = jnp.concatenate([x[0] for x in state], axis=0) if count > 1 else state[0][0]
    value_acc = jnp.concatenate([x[1] for x in state], axis=0) if count > 1 else state[0][1]
    out = jnp.where(low_lanes(SEC), key_acc * (1.0 / math.sqrt(HD)), value_acc).astype(BF)
    packed[...] = out[:RUN]
    sent[:RUN] = given[...]
    sent[RUN:] = out[RUN:]


def weights_kernel(tok, tok_other, first, second, sent, out):
    qa = dot(tok[...], first[...], TN) + dot(tok_other[...], sent[:RUN], TN)
    kv = dot(tok[...], second[...], TN) + dot(tok_other[...], sent[RUN:], TN)
    for p in range(16):
        out[p, :64] = kv[p * 64 : (p + 1) * 64].astype(BF)
        upper = qa[p * 32 : (p + 1) * 32, :HD]
        lower = qa[512 + p * 32 : 512 + (p + 1) * 32, :HD]
        out[p, 64:96] = jnp.concatenate([upper, lower], axis=1).astype(BF)


def sum_kernel(parts, out):
    total = parts[0].astype(F32)
    for p in range(1, 16):
        total = total + parts[p].astype(F32)
    total = total.astype(BF)
    for p in range(32):
        out[p] = total


def input_kernel(place, first, second, arrived, wq, wk, wv, att, keep, send):
    swap = place[0] != 0
    core = place[2]
    a, b, c, d = first[...], arrived[:RUN], second[...], arrived[RUN:]
    a, b = jnp.where(swap, b, a), jnp.where(swap, a, b)
    c, d = jnp.where(swap, d, c), jnp.where(swap, c, d)
    dq = jnp.concatenate([a[:, :HD], b[:, :HD]], axis=1)
    att[...] = jnp.concatenate([a[:, HD:], b[:, HD:]], axis=1)
    dk = jnp.concatenate([c[:, :HD], d[:, :HD]], axis=1)
    dv = jnp.concatenate([c[:, HD:], d[:, HD:]], axis=1)
    grad = dot(dq, wq[...], NT) + dot(dk, wk[...], NT) + dot(dv, wv[...], NT)
    for y in range(4):
        low, high = grad[y * 64 : y * 64 + 32], grad[y * 64 + 32 : y * 64 + 64]
        keep[y] = jnp.where(core == 0, low, high)
        send[y] = jnp.where(core == 0, high, low).astype(BF)


def assemble_kernel(parts, gq, gk, gv):
    for p in range(16):
        a, b = parts[2 * p].astype(F32), parts[2 * p + 1].astype(F32)
        low = jnp.concatenate([a[:, :HD], b[:, :HD]], axis=1)
        high = jnp.concatenate([a[:, HD:], b[:, HD:]], axis=1)
        gk[p * 64 : (p + 1) * 64] = low[:64]
        gv[p * 64 : (p + 1) * 64] = high[:64]
        gq[p * 32 : (p + 1) * 32] = low[64:]
        gq[512 + p * 32 : 512 + (p + 1) * 32] = high[64:]


def shift(a, step):
    return lax.ppermute(a, Z, [(i, (i + step) % NSEC) for i in range(NSEC)])


def swap(a):
    return lax.ppermute(a, "xh", [(0, 1), (1, 0)])


def on_device(tokens, wq, wk, wv, cotangent, doc_lengths, global_positions):
    shape = jax.ShapeDtypeStruct
    tok, cot = tokens[0], cotangent[0]
    xh, z, y, core = (lax.axis_index(a) for a in ("xh", Z, "y", "core"))
    place = jnp.stack([xh, z, core]).astype(jnp.int32)
    weight = pltpu.VMEM((1024, 128), BF)
    mine, theirs = call(
        project_kernel,
        (shape((SEC, 128), BF),) * 2,
        (tok, wq, wk, wv, cot),
        scratch=(
            pltpu.VMEM((RUN, 1024), BF),
            weight,
            weight,
            weight,
            pltpu.VMEM((RUN, 128), BF),
            pltpu.SemaphoreType.DMA((5,)),
        ),
        flops=6 * 256 * 1024 * 128,
        smem=0,
        manual=5,
        limit=64 << 20,
    )
    other = swap(theirs)
    tok_other = swap(tok)
    pairs = SEC * SEC * NSEC
    wide = shape((SEC, 128), F32)

    tie = lax.optimization_barrier
    lower_a, upper_a = [mine, shift(mine, 1)], [mine, shift(mine, -1)]
    late, mine = tie((place, mine))
    feat = call(
        feature_kernel,
        shape((NSEC * SEC, 128), BF),
        (late, doc_lengths, global_positions),
        smem=2,
        limit=FEATURE_LIMIT,
    )
    other, feat, lower_a[1], upper_a[1] = tie((other, feat, lower_a[1], upper_a[1]))
    lower_b, upper_b = [other, shift(other, 1)], [other, shift(other, -1)]
    for x, step in ((lower_a, 1), (upper_a, -1), (lower_b, 1), (upper_b, -1)):
        x.append(shift(x[1], step))
    for x, step in ((lower_a, 1), (upper_a, -1), (lower_b, 1), (upper_b, -1)):
        x.append(shift(x[2], step))
    far = (shift(lower_a[3], 1), shift(upper_b[3], -1))
    pieces = (mine, other)
    for i in (1, 2, 3):
        pieces += (lower_a[i], lower_b[i], upper_a[i], upper_b[i])
    pieces += far
    state = call(
        functools.partial(forward_kernel, 0, SPLIT),
        (wide, wide),
        (place, mine, other, feat, *pieces[: 2 * SPLIT]),
        flops=2 * 128 * 2 * pairs * SPLIT // NSEC,
        transcendentals=pairs * SPLIT // NSEC,
    )
    tok_other, *state = tie((tok_other, *state))
    att_rows, column, stats = call(
        functools.partial(forward_kernel, SPLIT, NSEC),
        (shape((SEC, 128), BF), wide, shape((NSEC, 8, 128), F32)),
        (place, mine, other, feat, *pieces[2 * SPLIT :], *state),
        flops=2 * 128 * 2 * pairs * (NSEC - SPLIT) // NSEC,
        transcendentals=pairs * (NSEC - SPLIT) // NSEC,
    )
    all_stats = lax.all_to_all(stats, Z, 0, 0, tiled=True).reshape(NSEC * 8, 128)
    half = shape((RUN, 128), BF)
    first, first_sent = call(
        functools.partial(queries_kernel, CHUNK),
        (half, half),
        (place, *pieces, feat, att_rows, column),
        flops=2 * 128 * 3 * pairs,
        transcendentals=pairs,
    )
    all_stats, first, first_sent = tie((all_stats, first, first_sent))
    second, sent = call(
        functools.partial(keys_kernel, CHUNK),
        (half, shape((SEC, 128), BF)),
        (place, *pieces, feat, all_stats, first_sent),
        scratch=(pltpu.VMEM((NSEC * 8, 128), F32), pltpu.SemaphoreType.DMA((NSEC,))),
        flops=2 * 128 * 4 * pairs,
        transcendentals=pairs,
    )
    back = swap(sent)
    partial = call(
        weights_kernel,
        shape((16, 96, 128), BF),
        (tok, tok_other, first, second, sent),
        flops=2 * 512 * 1024 * 256,
        smem=0,
    )
    partial = lax.all_to_all(partial, ("b",) + Z, 0, 0, tiled=True)
    att, keep, send = call(
        input_kernel,
        (half, shape((4, 32, 1024), F32), shape((4, 32, 1024), BF)),
        (place, first, second, back, wq, wk, wv),
        flops=6 * 256 * 1024 * 128,
    )
    partial, send = tie((partial, send))
    arrived = lax.ppermute(send, "core", [(0, 1), (1, 0)])
    total = call(sum_kernel, shape((32, 96, 128), BF), (partial,), smem=0)
    both = keep + arrived.astype(F32)
    share = lax.dynamic_index_in_dim(both, y, 0, False)
    both_bf = both.astype(BF)
    for k in (1, 2, 3):
        out = lax.dynamic_index_in_dim(both_bf, lax.bitwise_xor(y, k), 0, False)
        share = share + lax.ppermute(out, "y", [(i, i ^ k) for i in range(4)]).astype(F32)
    total = lax.all_to_all(total, ("b",) + CTX, 0, 0, tiled=True)
    gq, gk, gv = call(assemble_kernel, (shape((1024, 128), F32),) * 3, (total,), smem=0)
    return att[None], share.astype(BF)[None], gq, gk, gv


def solution(mesh):
    devices = mesh.devices.reshape(2, 2, 2, 2, 2, 4, 2)
    fine = Mesh(devices, ("b",) + CTX + TP)
    in_specs = (
        P("b", CTX, None),
        P(None, TP),
        P(None, TP),
        P(None, TP),
        P("b", CTX, TP),
        P("b", None),
        P("b", None),
    )
    out_specs = (
        P("b", CTX, TP),
        P("b", CTX + TP, None),
        P(None, TP),
        P(None, TP),
        P(None, TP),
    )
    return jax.shard_map(
        on_device, mesh=fine, in_specs=in_specs, out_specs=out_specs, check_vma=False
    )
```

```python
import functools
import math

import jax
import jax.numpy as jnp
from jax import lax
from jax.experimental import pallas as pl
from jax.experimental.pallas import tpu as pltpu
from jax.sharding import Mesh
from jax.sharding import PartitionSpec as P

HALF = 256
HD = 64
RUN = 256
SEC = 512
NSEC = 8
NEG = -1e30
LIMIT = 51 << 20
CHUNK = 512
FEATURE_LIMIT = 64 << 20
BF = jnp.bfloat16
F32 = jnp.float32

Z = ("z2", "z1", "z0")
CTX = Z + ("xh",)
TP = ("y", "core")

OFFSETS = (0, -1, 1, -2, 2, -3, 3, 4)

NN = (((1,), (0,)), ((), ()))
NT = (((1,), (1,)), ((), ()))
TN = (((0,), (0,)), ((), ()))


def dot(a, b, dims=NN):
    return lax.dot_general(a, b, dims, preferred_element_type=F32)


def call(kernel, outs, args, scratch=(), flops=0, transcendentals=0, smem=1, manual=0, limit=None):
    specs = [pl.BlockSpec(memory_space=pltpu.SMEM)] * smem
    specs += [pl.BlockSpec(memory_space=pl.ANY)] * manual
    specs += [pl.BlockSpec(memory_space=pltpu.VMEM)] * (len(args) - smem - manual)
    moved = sum(a.size * a.dtype.itemsize for a in args)
    return pl.pallas_call(
        kernel,
        out_shape=outs,
        in_specs=specs,
        out_specs=jax.tree.map(lambda _: pl.BlockSpec(memory_space=pltpu.VMEM), outs),
        scratch_shapes=list(scratch),
        compiler_params=pltpu.CompilerParams(vmem_limit_bytes=limit or LIMIT),
        cost_estimate=pl.CostEstimate(
            flops=flops, bytes_accessed=moved, transcendentals=transcendentals
        ),
    )(*args)


def low_lanes(rows):
    return lax.broadcasted_iota(jnp.int32, (rows, 128), 1) < HD


def feature_kernel(place, lengths, spots, feat):
    flip = place[0]
    lane = lax.broadcasted_iota(jnp.int32, (RUN, 128), 1)
    last = lane == HD + 8
    lane_row = lax.broadcasted_iota(jnp.int32, (1, 128), 1)
    starts, ends = jnp.zeros((1, 128), jnp.int32), jnp.zeros((1, 128), jnp.int32)
    start = jnp.int32(0)
    for d in range(8):
        end = start + lengths[0, d]
        starts = jnp.where(lane_row == HD + d, start, starts)
        ends = jnp.where(lane_row == HD + d, end, ends)
        start = end

    def one(block, carry):
        half = lax.rem(block, 2)
        run = (block - half) + jnp.where(half == flip, 0, 1)
        pos = run * RUN + lax.broadcasted_iota(jnp.int32, (RUN, RUN), 0)
        hit = jnp.max(jnp.where(pos == spots[...], 1.0, 0.0), axis=1, keepdims=True)
        other = 1.0 - hit
        pos128 = run * RUN + lax.broadcasted_iota(jnp.int32, (RUN, 128), 0)
        member = (pos128 >= starts) & (pos128 < ends)
        row = jnp.where(last, other, jnp.where(member, 1.0, 0.0))
        at = pl.ds(pl.multiple_of(block * RUN, RUN), RUN)
        feat[at, :] = row.astype(BF)
        return carry

    lax.fori_loop(0, 2 * NSEC, one, 0)


def project_kernel(tok, wq, wk, wv, cot, mine, theirs, *scratch):
    tok_v, wk_v, wv_v, wq_v, cot_v, sems = scratch
    pairs = ((tok, tok_v), (wk, wk_v), (wv, wv_v), (wq, wq_v), (cot, cot_v))
    copies = [pltpu.make_async_copy(a, b, sems.at[i]) for i, (a, b) in enumerate(pairs)]
    for copy in copies:
        copy.start()
    first = lax.axis_index("xh") == 0
    copies[0].wait()
    t = tok_v[...]
    copies[1].wait()
    k = dot(t, wk_v[...]).astype(BF)
    copies[2].wait()
    v = dot(t, wv_v[...]).astype(BF)
    copies[3].wait()
    q = dot(t, wq_v[...]).astype(BF)
    copies[4].wait()
    c = cot_v[...]
    kv0 = jnp.concatenate([k[:, :HD], v[:, :HD]], axis=1)
    kv1 = jnp.concatenate([k[:, HD:], v[:, HD:]], axis=1)
    qc0 = jnp.concatenate([q[:, :HD], c[:, :HD]], axis=1)
    qc1 = jnp.concatenate([q[:, HD:], c[:, HD:]], axis=1)

    @pl.when(first)
    def _():
        mine[:RUN] = kv0
        mine[RUN:] = qc0
        theirs[:RUN] = kv1
        theirs[RUN:] = qc1

    @pl.when(jnp.logical_not(first))
    def _():
        mine[:RUN] = kv1
        mine[RUN:] = qc1
        theirs[:RUN] = kv0
        theirs[RUN:] = qc0


def places(section, flip, along):
    shape = (1, SEC) if along == 1 else (SEC, 1)
    i = lax.broadcasted_iota(jnp.int32, shape, along)
    half = jnp.where(i >= RUN, 1 - flip, flip)
    return section * SEC + half * RUN + lax.bitwise_and(i, RUN - 1)


def section_at(own, offset):
    return lax.rem(own + offset + NSEC, NSEC)


def part_of(pieces, r, part):
    at = slice(part * RUN, (part + 1) * RUN)
    return jnp.concatenate([pieces[2 * r][at], pieces[2 * r + 1][at]], axis=0)


def features_at(feat, section):
    return feat[pl.ds(pl.multiple_of(section * SEC, SEC), SEC), :]


def join_key(kv, feat):
    lane = lax.broadcasted_iota(jnp.int32, kv.shape, 1)
    base = jnp.where(lane < HD + 8, 1.0, 0.0).astype(BF)
    sign = jnp.where(lane == HD + 8, 1.0, jnp.where(lane < HD + 8, -1.0, 0.0)).astype(BF)
    return jnp.where(lane < HD, kv, (base + sign * feat) * jnp.asarray(NEG, BF))


def join_query(qc, feat):
    low = lax.broadcasted_iota(jnp.int32, qc.shape, 1) < HD
    return jnp.where(low, qc * jnp.asarray(1.0 / math.sqrt(HD), BF), feat)


def less_global(joined):
    lane = lax.broadcasted_iota(jnp.int32, joined.shape, 1)
    return jnp.where(lane == HD + 8, jnp.zeros_like(joined), joined)


def right_half(rows):
    low = lax.broadcasted_iota(jnp.int32, rows.shape, 1) < HD
    return jnp.where(low, jnp.zeros_like(rows), rows)


def near_only(own, flip, r, own_places, near, plain):
    if r > 2:
        return plain
    away = own_places - places(section_at(own, OFFSETS[r]), flip, 1)
    return jnp.where(jnp.abs(away) <= HALF, near, plain)


def forward_kernel(place, *refs):
    pieces, (feat, att_out, column_out, stats) = refs[: 2 * NSEC], refs[2 * NSEC :]
    flip, own = place[0], place[1]
    own_qc = part_of(pieces, 0, 1)
    joined = join_query(own_qc, features_at(feat, own))
    near_rows = less_global(joined)
    row_places = places(own, flip, 0)

    def products(r):
        kp = join_key(part_of(pieces, r, 0), features_at(feat, section_at(own, OFFSETS[r])))
        return dot(joined, kp, NT), dot(near_rows, kp, NT) if r < 3 else None

    ahead = products(0)
    for r in range(NSEC):
        plain, near = ahead
        if r + 1 < NSEC:
            ahead = products(r + 1)
        s = near_only(own, flip, r, row_places, near, plain)
        new_peak = jnp.max(s, axis=1, keepdims=True)
        if r > 0:
            new_peak = jnp.maximum(peak, new_peak)
            keep = jnp.exp(peak - new_peak)
        e = jnp.exp(s - new_peak)
        new_total = jnp.sum(e, axis=1, keepdims=True)
        new_acc = dot(e.astype(BF), part_of(pieces, r, 0))
        if r > 0:
            new_total, new_acc = keep * total + new_total, keep * acc + new_acc
        peak, total, acc = new_peak, new_total, new_acc
    att = (acc / total).astype(BF)
    att_out[...] = att
    cot = right_half(own_qc).astype(F32)
    delta = jnp.sum(att.astype(F32) * cot, axis=1, keepdims=True)
    lanes = lax.broadcasted_iota(jnp.int32, (SEC, 128), 1)
    column = jnp.where(lanes == 0, peak + jnp.log(total), delta)
    column_out[...] = column
    turned = column.T
    for k in range(SEC // 128):
        for copy in range(NSEC):
            stats[copy, k : k + 1] = turned[0:1, k * 128 : (k + 1) * 128]
            stats[copy, 4 + k : 5 + k] = turned[1:2, k * 128 : (k + 1) * 128]


def queries_kernel(chunk, place, *refs):
    pieces, (feat, att, column, packed, packed_other) = refs[: 2 * NSEC], refs[2 * NSEC :]
    flip, own = place[0], place[1]
    own_qc = part_of(pieces, 0, 1)
    joined = join_query(own_qc, features_at(feat, own))
    near_rows, cot = less_global(joined), right_half(own_qc)
    row_places = places(own, flip, 0)
    count = SEC // chunk
    grads = [None] * count
    for r, offset in enumerate(OFFSETS):
        section = section_at(own, offset)
        kv = part_of(pieces, r, 0)
        kp = join_key(kv, features_at(feat, section))
        for c in range(count):
            rows = slice(c * chunk, (c + 1) * chunk)
            s = dot(joined[rows], kp, NT)
            if r < 3:
                away = row_places[rows] - places(section, flip, 1)
                s = jnp.where(jnp.abs(away) <= HALF, dot(near_rows[rows], kp, NT), s)
            p = jnp.exp(s - column[rows, 0:1])
            ds = p * (dot(cot[rows], kv, NT) - column[rows, 1:2])
            grad = dot(ds.astype(BF), kv)
            grads[c] = grad if r == 0 else grads[c] + grad
    grad = jnp.concatenate(grads, axis=0) if count > 1 else grads[0]
    grad = (grad * (1.0 / math.sqrt(HD))).astype(BF)
    out = jnp.where(low_lanes(SEC), grad, att[...])
    packed[...] = out[:RUN]
    packed_other[...] = out[RUN:]


def keys_kernel(chunk, place, *refs):
    pieces, (feat, stats, given, packed, sent, stats_s, sems) = refs[: 2 * NSEC], refs[2 * NSEC :]
    flip, own = place[0], place[1]
    copies = []
    for r, offset in enumerate(OFFSETS):
        at = pl.multiple_of(section_at(own, offset) * 8, 8)
        to = stats_s.at[pl.ds(r * 8, 8)]
        copies.append(pltpu.make_async_copy(stats.at[pl.ds(at, 8)], to, sems.at[r]))
        copies[-1].start()
    own_kv = part_of(pieces, 0, 0)
    joined = join_key(own_kv, features_at(feat, own))
    near_keys, value = less_global(joined), right_half(own_kv)
    key_places = places(own, flip, 0)
    count = SEC // chunk
    state = [None] * count
    for copy in copies:
        copy.wait()
    for r, offset in enumerate(OFFSETS):
        section = section_at(own, offset)
        qc = part_of(pieces, r, 1)
        qp = join_query(qc, features_at(feat, section))
        st = stats_s[r * 8 : r * 8 + 8]
        log_total = jnp.concatenate([st[i : i + 1] for i in range(4)], axis=1)
        delta = jnp.concatenate([st[i : i + 1] for i in range(4, 8)], axis=1)
        for c in range(count):
            rows = slice(c * chunk, (c + 1) * chunk)
            s = dot(joined[rows], qp, NT)
            if r < 3:
                away = key_places[rows] - places(section, flip, 1)
                s = jnp.where(jnp.abs(away) <= HALF, dot(near_keys[rows], qp, NT), s)
            p = jnp.exp(s - log_total)
            ds = p * (dot(value[rows], qc, NT) - delta)
            both = dot(ds.astype(BF), qc), dot(p.astype(BF), qc)
            state[c] = both if r == 0 else (state[c][0] + both[0], state[c][1] + both[1])
    key_acc = jnp.concatenate([x[0] for x in state], axis=0) if count > 1 else state[0][0]
    value_acc = jnp.concatenate([x[1] for x in state], axis=0) if count > 1 else state[0][1]
    out = jnp.where(low_lanes(SEC), key_acc * (1.0 / math.sqrt(HD)), value_acc).astype(BF)
    packed[...] = out[:RUN]
    sent[:RUN] = given[...]
    sent[RUN:] = out[RUN:]


def weights_kernel(tok, tok_other, first, second, sent, out):
    qa = dot(tok[...], first[...], TN) + dot(tok_other[...], sent[:RUN], TN)
    kv = dot(tok[...], second[...], TN) + dot(tok_other[...], sent[RUN:], TN)
    for p in range(16):
        out[p, :64] = kv[p * 64 : (p + 1) * 64].astype(BF)
        upper = qa[p * 32 : (p + 1) * 32, :HD]
        lower = qa[512 + p * 32 : 512 + (p + 1) * 32, :HD]
        out[p, 64:96] = jnp.concatenate([upper, lower], axis=1).astype(BF)


def sum_kernel(parts, out):
    total = parts[0].astype(F32)
    for p in range(1, 16):
        total = total + parts[p].astype(F32)
    total = total.astype(BF)
    for p in range(32):
        out[p] = total


def input_kernel(place, first, second, arrived, wq, wk, wv, att, keep, send):
    swap = place[0] != 0
    core = place[2]
    a, b, c, d = first[...], arrived[:RUN], second[...], arrived[RUN:]
    a, b = jnp.where(swap, b, a), jnp.where(swap, a, b)
    c, d = jnp.where(swap, d, c), jnp.where(swap, c, d)
    dq = jnp.concatenate([a[:, :HD], b[:, :HD]], axis=1)
    att[...] = jnp.concatenate([a[:, HD:], b[:, HD:]], axis=1)
    dk = jnp.concatenate([c[:, :HD], d[:, :HD]], axis=1)
    dv = jnp.concatenate([c[:, HD:], d[:, HD:]], axis=1)
    grad = dot(dq, wq[...], NT) + dot(dk, wk[...], NT) + dot(dv, wv[...], NT)
    for y in range(4):
        low, high = grad[y * 64 : y * 64 + 32], grad[y * 64 + 32 : y * 64 + 64]
        keep[y] = jnp.where(core == 0, low, high)
        send[y] = jnp.where(core == 0, high, low).astype(BF)


def assemble_kernel(parts, gq, gk, gv):
    for p in range(16):
        a, b = parts[2 * p].astype(F32), parts[2 * p + 1].astype(F32)
        low = jnp.concatenate([a[:, :HD], b[:, :HD]], axis=1)
        high = jnp.concatenate([a[:, HD:], b[:, HD:]], axis=1)
        gk[p * 64 : (p + 1) * 64] = low[:64]
        gv[p * 64 : (p + 1) * 64] = high[:64]
        gq[p * 32 : (p + 1) * 32] = low[64:]
        gq[512 + p * 32 : 512 + (p + 1) * 32] = high[64:]


def shift(a, step):
    return lax.ppermute(a, Z, [(i, (i + step) % NSEC) for i in range(NSEC)])


def swap(a):
    return lax.ppermute(a, "xh", [(0, 1), (1, 0)])


def on_device(tokens, wq, wk, wv, cotangent, doc_lengths, global_positions):
    shape = jax.ShapeDtypeStruct
    tok, cot = tokens[0], cotangent[0]
    xh, z, y, core = (lax.axis_index(a) for a in ("xh", Z, "y", "core"))
    place = jnp.stack([xh, z, core]).astype(jnp.int32)
    weight = pltpu.VMEM((1024, 128), BF)
    mine, theirs = call(
        project_kernel,
        (shape((SEC, 128), BF),) * 2,
        (tok, wq, wk, wv, cot),
        scratch=(
            pltpu.VMEM((RUN, 1024), BF),
            weight,
            weight,
            weight,
            pltpu.VMEM((RUN, 128), BF),
            pltpu.SemaphoreType.DMA((5,)),
        ),
        flops=6 * 256 * 1024 * 128,
        smem=0,
        manual=5,
        limit=64 << 20,
    )
    other = swap(theirs)
    tok_other = swap(tok)
    pairs = SEC * SEC * NSEC
    wide = shape((SEC, 128), F32)

    tie = lax.optimization_barrier
    lower_a, upper_a = [mine, shift(mine, 1)], [mine, shift(mine, -1)]
    late, mine = tie((place, mine))
    feat = call(
        feature_kernel,
        shape((NSEC * SEC, 128), BF),
        (late, doc_lengths, global_positions),
        smem=2,
        limit=FEATURE_LIMIT,
    )
    other, feat, lower_a[1], upper_a[1] = tie((other, feat, lower_a[1], upper_a[1]))
    lower_b, upper_b = [other, shift(other, 1)], [other, shift(other, -1)]
    for x, step in ((lower_a, 1), (upper_a, -1), (lower_b, 1), (upper_b, -1)):
        x.append(shift(x[1], step))
    for x, step in ((lower_a, 1), (upper_a, -1), (lower_b, 1), (upper_b, -1)):
        x.append(shift(x[2], step))
    far = (shift(lower_a[3], 1), shift(upper_b[3], -1))
    pieces = (mine, other)
    for i in (1, 2, 3):
        pieces += (lower_a[i], lower_b[i], upper_a[i], upper_b[i])
    pieces += far
    tok_other, feat = tie((tok_other, feat))
    att_rows, column, stats = call(
        forward_kernel,
        (shape((SEC, 128), BF), wide, shape((NSEC, 8, 128), F32)),
        (place, *pieces, feat),
        flops=2 * 128 * 2 * pairs,
        transcendentals=pairs,
    )
    all_stats = lax.all_to_all(stats, Z, 0, 0, tiled=True).reshape(NSEC * 8, 128)
    half = shape((RUN, 128), BF)
    first, first_sent = call(
        functools.partial(queries_kernel, CHUNK),
        (half, half),
        (place, *pieces, feat, att_rows, column),
        flops=2 * 128 * 3 * pairs,
        transcendentals=pairs,
    )
    all_stats, first, first_sent = tie((all_stats, first, first_sent))
    second, sent = call(
        functools.partial(keys_kernel, CHUNK),
        (half, shape((SEC, 128), BF)),
        (place, *pieces, feat, all_stats, first_sent),
        scratch=(pltpu.VMEM((NSEC * 8, 128), F32), pltpu.SemaphoreType.DMA((NSEC,))),
        flops=2 * 128 * 4 * pairs,
        transcendentals=pairs,
    )
    back = swap(sent)
    partial = call(
        weights_kernel,
        shape((16, 96, 128), BF),
        (tok, tok_other, first, second, sent),
        flops=2 * 512 * 1024 * 256,
        smem=0,
    )
    partial = lax.all_to_all(partial, ("b",) + Z, 0, 0, tiled=True)
    att, keep, send = call(
        input_kernel,
        (half, shape((4, 32, 1024), F32), shape((4, 32, 1024), BF)),
        (place, first, second, back, wq, wk, wv),
        flops=6 * 256 * 1024 * 128,
    )
    partial, send = tie((partial, send))
    arrived = lax.ppermute(send, "core", [(0, 1), (1, 0)])
    total = call(sum_kernel, shape((32, 96, 128), BF), (partial,), smem=0)
    both = keep + arrived.astype(F32)
    share = lax.dynamic_index_in_dim(both, y, 0, False)
    both_bf = both.astype(BF)
    for k in (1, 2, 3):
        out = lax.dynamic_index_in_dim(both_bf, lax.bitwise_xor(y, k), 0, False)
        share = share + lax.ppermute(out, "y", [(i, i ^ k) for i in range(4)]).astype(F32)
    total = lax.all_to_all(total, ("b",) + CTX, 0, 0, tiled=True)
    gq, gk, gv = call(assemble_kernel, (shape((1024, 128), F32),) * 3, (total,), smem=0)
    return att[None], share.astype(BF)[None], gq, gk, gv


def solution(mesh):
    devices = mesh.devices.reshape(2, 2, 2, 2, 2, 4, 2)
    fine = Mesh(devices, ("b",) + CTX + TP)
    in_specs = (
        P("b", CTX, None),
        P(None, TP),
        P(None, TP),
        P(None, TP),
        P("b", CTX, TP),
        P("b", None),
        P("b", None),
    )
    out_specs = (
        P("b", CTX, TP),
        P("b", CTX + TP, None),
        P(None, TP),
        P(None, TP),
        P(None, TP),
    )
    return jax.shard_map(
        on_device, mesh=fine, in_specs=in_specs, out_specs=out_specs, check_vma=False
    )
```

```python
import functools
import math

import jax
import jax.numpy as jnp
from jax import lax
from jax.experimental import pallas as pl
from jax.experimental.pallas import tpu as pltpu
from jax.sharding import Mesh
from jax.sharding import PartitionSpec as P

HALF = 256
HD = 64
RUN = 256
SEC = 512
NSEC = 8
NEG = -1e30
LIMIT = 51 << 20
CHUNK = 512
FEATURE_LIMIT = 64 << 20
BF = jnp.bfloat16
F32 = jnp.float32

Z = ("z2", "z1", "z0")
CTX = Z + ("xh",)
TP = ("y", "core")

OFFSETS = (0, -1, 1, -2, 2, -3, 3, 4)

NN = (((1,), (0,)), ((), ()))
NT = (((1,), (1,)), ((), ()))
TN = (((0,), (0,)), ((), ()))


def dot(a, b, dims=NN):
    return lax.dot_general(a, b, dims, preferred_element_type=F32)


def call(kernel, outs, args, scratch=(), flops=0, transcendentals=0, smem=1, manual=0, limit=None):
    specs = [pl.BlockSpec(memory_space=pltpu.SMEM)] * smem
    specs += [pl.BlockSpec(memory_space=pl.ANY)] * manual
    specs += [pl.BlockSpec(memory_space=pltpu.VMEM)] * (len(args) - smem - manual)
    moved = sum(a.size * a.dtype.itemsize for a in args)
    return pl.pallas_call(
        kernel,
        out_shape=outs,
        in_specs=specs,
        out_specs=jax.tree.map(lambda _: pl.BlockSpec(memory_space=pltpu.VMEM), outs),
        scratch_shapes=list(scratch),
        compiler_params=pltpu.CompilerParams(vmem_limit_bytes=limit or LIMIT),
        cost_estimate=pl.CostEstimate(
            flops=flops, bytes_accessed=moved, transcendentals=transcendentals
        ),
    )(*args)


def low_lanes(rows):
    return lax.broadcasted_iota(jnp.int32, (rows, 128), 1) < HD


def feature_kernel(place, lengths, spots, feat):
    flip = place[0]
    lane = lax.broadcasted_iota(jnp.int32, (RUN, 128), 1)
    last = lane == HD + 8
    lane_row = lax.broadcasted_iota(jnp.int32, (1, 128), 1)
    starts, ends = jnp.zeros((1, 128), jnp.int32), jnp.zeros((1, 128), jnp.int32)
    start = jnp.int32(0)
    for d in range(8):
        end = start + lengths[0, d]
        starts = jnp.where(lane_row == HD + d, start, starts)
        ends = jnp.where(lane_row == HD + d, end, ends)
        start = end

    def one(block, carry):
        half = lax.rem(block, 2)
        run = (block - half) + jnp.where(half == flip, 0, 1)
        pos = run * RUN + lax.broadcasted_iota(jnp.int32, (RUN, RUN), 0)
        hit = jnp.max(jnp.where(pos == spots[...], 1.0, 0.0), axis=1, keepdims=True)
        other = 1.0 - hit
        pos128 = run * RUN + lax.broadcasted_iota(jnp.int32, (RUN, 128), 0)
        member = (pos128 >= starts) & (pos128 < ends)
        row = jnp.where(last, other, jnp.where(member, 1.0, 0.0))
        at = pl.ds(pl.multiple_of(block * RUN, RUN), RUN)
        feat[at, :] = row.astype(BF)
        return carry

    lax.fori_loop(0, 2 * NSEC, one, 0)


def project_kernel(tok, wq, wk, wv, cot, mine, theirs, *scratch):
    tok_v, wk_v, wv_v, wq_v, cot_v, sems = scratch
    pairs = ((tok, tok_v), (wk, wk_v), (wv, wv_v), (wq, wq_v), (cot, cot_v))
    copies = [pltpu.make_async_copy(a, b, sems.at[i]) for i, (a, b) in enumerate(pairs)]
    for copy in copies:
        copy.start()
    first = lax.axis_index("xh") == 0
    copies[0].wait()
    t = tok_v[...]
    copies[1].wait()
    k = dot(t, wk_v[...]).astype(BF)
    copies[2].wait()
    v = dot(t, wv_v[...]).astype(BF)
    copies[3].wait()
    q = dot(t, wq_v[...]).astype(BF)
    copies[4].wait()
    c = cot_v[...]
    kv0 = jnp.concatenate([k[:, :HD], v[:, :HD]], axis=1)
    kv1 = jnp.concatenate([k[:, HD:], v[:, HD:]], axis=1)
    qc0 = jnp.concatenate([q[:, :HD], c[:, :HD]], axis=1)
    qc1 = jnp.concatenate([q[:, HD:], c[:, HD:]], axis=1)

    @pl.when(first)
    def _():
        mine[:RUN] = kv0
        mine[RUN:] = qc0
        theirs[:RUN] = kv1
        theirs[RUN:] = qc1

    @pl.when(jnp.logical_not(first))
    def _():
        mine[:RUN] = kv1
        mine[RUN:] = qc1
        theirs[:RUN] = kv0
        theirs[RUN:] = qc0


def places(section, flip, along):
    shape = (1, SEC) if along == 1 else (SEC, 1)
    i = lax.broadcasted_iota(jnp.int32, shape, along)
    half = jnp.where(i >= RUN, 1 - flip, flip)
    return section * SEC + half * RUN + lax.bitwise_and(i, RUN - 1)


def section_at(own, offset):
    return lax.rem(own + offset + NSEC, NSEC)


def part_of(pieces, r, part):
    at = slice(part * RUN, (part + 1) * RUN)
    return jnp.concatenate([pieces[2 * r][at], pieces[2 * r + 1][at]], axis=0)


def features_at(feat, section):
    return feat[pl.ds(pl.multiple_of(section * SEC, SEC), SEC), :]


def join_key(kv, feat):
    lane = lax.broadcasted_iota(jnp.int32, kv.shape, 1)
    base = jnp.where(lane < HD + 8, 1.0, 0.0).astype(BF)
    sign = jnp.where(lane == HD + 8, 1.0, jnp.where(lane < HD + 8, -1.0, 0.0)).astype(BF)
    return jnp.where(lane < HD, kv, (base + sign * feat) * jnp.asarray(NEG, BF))


def join_query(qc, feat):
    low = lax.broadcasted_iota(jnp.int32, qc.shape, 1) < HD
    return jnp.where(low, qc * jnp.asarray(1.0 / math.sqrt(HD), BF), feat)


def less_global(joined):
    lane = lax.broadcasted_iota(jnp.int32, joined.shape, 1)
    return jnp.where(lane == HD + 8, jnp.zeros_like(joined), joined)


def right_half(rows):
    low = lax.broadcasted_iota(jnp.int32, rows.shape, 1) < HD
    return jnp.where(low, jnp.zeros_like(rows), rows)


def near_only(own, flip, r, own_places, near, plain):
    if r > 2:
        return plain
    away = own_places - places(section_at(own, OFFSETS[r]), flip, 1)
    return jnp.where(jnp.abs(away) <= HALF, near, plain)


def forward_kernel(place, *refs):
    pieces, (feat, att_out, column_out, stats) = refs[: 2 * NSEC], refs[2 * NSEC :]
    flip, own = place[0], place[1]
    own_qc = part_of(pieces, 0, 1)
    joined = join_query(own_qc, features_at(feat, own))
    near_rows = less_global(joined)
    row_places = places(own, flip, 0)

    def products(r):
        kp = join_key(part_of(pieces, r, 0), features_at(feat, section_at(own, OFFSETS[r])))
        return dot(joined, kp, NT), dot(near_rows, kp, NT) if r < 3 else None

    ahead = products(0)
    for r in range(NSEC):
        plain, near = ahead
        if r + 1 < NSEC:
            ahead = products(r + 1)
        s = near_only(own, flip, r, row_places, near, plain)
        new_peak = jnp.max(s, axis=1, keepdims=True)
        if r > 0:
            new_peak = jnp.maximum(peak, new_peak)
            keep = jnp.exp(peak - new_peak)
        e = jnp.exp(s - new_peak)
        new_total = jnp.sum(e, axis=1, keepdims=True)
        new_acc = dot(e.astype(BF), part_of(pieces, r, 0))
        if r > 0:
            new_total, new_acc = keep * total + new_total, keep * acc + new_acc
        peak, total, acc = new_peak, new_total, new_acc
    att = (acc / total).astype(BF)
    att_out[...] = att
    cot = right_half(own_qc).astype(F32)
    delta = jnp.sum(att.astype(F32) * cot, axis=1, keepdims=True)
    lanes = lax.broadcasted_iota(jnp.int32, (SEC, 128), 1)
    column = jnp.where(lanes == 0, peak + jnp.log(total), delta)
    column_out[...] = column
    turned = column.T
    for k in range(SEC // 128):
        for copy in range(NSEC):
            stats[copy, k : k + 1] = turned[0:1, k * 128 : (k + 1) * 128]
            stats[copy, 4 + k : 5 + k] = turned[1:2, k * 128 : (k + 1) * 128]


def queries_kernel(chunk, place, *refs):
    pieces, (feat, att, column, packed, packed_other) = refs[: 2 * NSEC], refs[2 * NSEC :]
    flip, own = place[0], place[1]
    own_qc = part_of(pieces, 0, 1)
    joined = join_query(own_qc, features_at(feat, own))
    near_rows, cot = less_global(joined), right_half(own_qc)
    row_places = places(own, flip, 0)
    count = SEC // chunk
    grads = [None] * count
    for r, offset in enumerate(OFFSETS):
        section = section_at(own, offset)
        kv = part_of(pieces, r, 0)
        kp = join_key(kv, features_at(feat, section))
        for c in range(count):
            rows = slice(c * chunk, (c + 1) * chunk)
            s = dot(joined[rows], kp, NT)
            if r < 3:
                away = row_places[rows] - places(section, flip, 1)
                s = jnp.where(jnp.abs(away) <= HALF, dot(near_rows[rows], kp, NT), s)
            p = jnp.exp(s - column[rows, 0:1])
            ds = p * (dot(cot[rows], kv, NT) - column[rows, 1:2])
            grad = dot(ds.astype(BF), kv)
            grads[c] = grad if r == 0 else grads[c] + grad
    grad = jnp.concatenate(grads, axis=0) if count > 1 else grads[0]
    grad = (grad * (1.0 / math.sqrt(HD))).astype(BF)
    out = jnp.where(low_lanes(SEC), grad, att[...])
    packed[...] = out[:RUN]
    packed_other[...] = out[RUN:]


def keys_kernel(chunk, place, *refs):
    pieces, (feat, stats, given, packed, sent, stats_s, sems) = refs[: 2 * NSEC], refs[2 * NSEC :]
    flip, own = place[0], place[1]
    copies = []
    for r, offset in enumerate(OFFSETS):
        at = pl.multiple_of(section_at(own, offset) * 8, 8)
        to = stats_s.at[pl.ds(r * 8, 8)]
        copies.append(pltpu.make_async_copy(stats.at[pl.ds(at, 8)], to, sems.at[r]))
        copies[-1].start()
    own_kv = part_of(pieces, 0, 0)
    joined = join_key(own_kv, features_at(feat, own))
    near_keys, value = less_global(joined), right_half(own_kv)
    key_places = places(own, flip, 0)
    count = SEC // chunk
    state = [None] * count
    for copy in copies:
        copy.wait()
    for r, offset in enumerate(OFFSETS):
        section = section_at(own, offset)
        qc = part_of(pieces, r, 1)
        qp = join_query(qc, features_at(feat, section))
        st = stats_s[r * 8 : r * 8 + 8]
        log_total = jnp.concatenate([st[i : i + 1] for i in range(4)], axis=1)
        delta = jnp.concatenate([st[i : i + 1] for i in range(4, 8)], axis=1)
        for c in range(count):
            rows = slice(c * chunk, (c + 1) * chunk)
            s = dot(joined[rows], qp, NT)
            if r < 3:
                away = key_places[rows] - places(section, flip, 1)
                s = jnp.where(jnp.abs(away) <= HALF, dot(near_keys[rows], qp, NT), s)
            p = jnp.exp(s - log_total)
            ds = p * (dot(value[rows], qc, NT) - delta)
            both = dot(ds.astype(BF), qc), dot(p.astype(BF), qc)
            state[c] = both if r == 0 else (state[c][0] + both[0], state[c][1] + both[1])
    key_acc = jnp.concatenate([x[0] for x in state], axis=0) if count > 1 else state[0][0]
    value_acc = jnp.concatenate([x[1] for x in state], axis=0) if count > 1 else state[0][1]
    out = jnp.where(low_lanes(SEC), key_acc * (1.0 / math.sqrt(HD)), value_acc).astype(BF)
    packed[...] = out[:RUN]
    sent[:RUN] = given[...]
    sent[RUN:] = out[RUN:]


def weights_kernel(tok, tok_other, first, second, sent, out):
    qa = dot(tok[...], first[...], TN) + dot(tok_other[...], sent[:RUN], TN)
    kv = dot(tok[...], second[...], TN) + dot(tok_other[...], sent[RUN:], TN)
    for p in range(16):
        out[p, :64] = kv[p * 64 : (p + 1) * 64].astype(BF)
        upper = qa[p * 32 : (p + 1) * 32, :HD]
        lower = qa[512 + p * 32 : 512 + (p + 1) * 32, :HD]
        out[p, 64:96] = jnp.concatenate([upper, lower], axis=1).astype(BF)


def sum_kernel(parts, out):
    total = parts[0].astype(F32)
    for p in range(1, 16):
        total = total + parts[p].astype(F32)
    total = total.astype(BF)
    for p in range(32):
        out[p] = total


def input_kernel(place, first, second, arrived, wq, wk, wv, att, keep, send):
    swap = place[0] != 0
    core = place[2]
    a, b, c, d = first[...], arrived[:RUN], second[...], arrived[RUN:]
    a, b = jnp.where(swap, b, a), jnp.where(swap, a, b)
    c, d = jnp.where(swap, d, c), jnp.where(swap, c, d)
    dq = jnp.concatenate([a[:, :HD], b[:, :HD]], axis=1)
    att[...] = jnp.concatenate([a[:, HD:], b[:, HD:]], axis=1)
    dk = jnp.concatenate([c[:, :HD], d[:, :HD]], axis=1)
    dv = jnp.concatenate([c[:, HD:], d[:, HD:]], axis=1)
    grad = dot(dq, wq[...], NT) + dot(dk, wk[...], NT) + dot(dv, wv[...], NT)
    for y in range(4):
        low, high = grad[y * 64 : y * 64 + 32], grad[y * 64 + 32 : y * 64 + 64]
        keep[y] = jnp.where(core == 0, low, high)
        send[y] = jnp.where(core == 0, high, low).astype(BF)


def assemble_kernel(parts, gq, gk, gv):
    for p in range(16):
        a, b = parts[2 * p].astype(F32), parts[2 * p + 1].astype(F32)
        low = jnp.concatenate([a[:, :HD], b[:, :HD]], axis=1)
        high = jnp.concatenate([a[:, HD:], b[:, HD:]], axis=1)
        gk[p * 64 : (p + 1) * 64] = low[:64]
        gv[p * 64 : (p + 1) * 64] = high[:64]
        gq[p * 32 : (p + 1) * 32] = low[64:]
        gq[512 + p * 32 : 512 + (p + 1) * 32] = high[64:]


def shift(a, step):
    return lax.ppermute(a, Z, [(i, (i + step) % NSEC) for i in range(NSEC)])


def swap(a):
    return lax.ppermute(a, "xh", [(0, 1), (1, 0)])


def on_device(tokens, wq, wk, wv, cotangent, doc_lengths, global_positions):
    shape = jax.ShapeDtypeStruct
    tok, cot = tokens[0], cotangent[0]
    xh, z, y, core = (lax.axis_index(a) for a in ("xh", Z, "y", "core"))
    place = jnp.stack([xh, z, core]).astype(jnp.int32)
    weight = pltpu.VMEM((1024, 128), BF)
    mine, theirs = call(
        project_kernel,
        (shape((SEC, 128), BF),) * 2,
        (tok, wq, wk, wv, cot),
        scratch=(
            pltpu.VMEM((RUN, 1024), BF),
            weight,
            weight,
            weight,
            pltpu.VMEM((RUN, 128), BF),
            pltpu.SemaphoreType.DMA((5,)),
        ),
        flops=6 * 256 * 1024 * 128,
        smem=0,
        manual=5,
        limit=64 << 20,
    )
    other = swap(theirs)
    tok_other = swap(tok)
    pairs = SEC * SEC * NSEC
    wide = shape((SEC, 128), F32)

    tie = lax.optimization_barrier
    lower_a, upper_a = [mine, shift(mine, 1)], [mine, shift(mine, -1)]
    late, mine = tie((place, mine))
    feat = call(
        feature_kernel,
        shape((NSEC * SEC, 128), BF),
        (late, doc_lengths, global_positions),
        smem=2,
        limit=FEATURE_LIMIT,
    )
    other, feat, lower_a[1], upper_a[1] = tie((other, feat, lower_a[1], upper_a[1]))
    lower_b, upper_b = [other, shift(other, 1)], [other, shift(other, -1)]
    for x, step in ((lower_a, 1), (upper_a, -1), (lower_b, 1), (upper_b, -1)):
        x.append(shift(x[1], step))
    for x, step in ((lower_a, 1), (upper_a, -1), (lower_b, 1), (upper_b, -1)):
        x.append(shift(x[2], step))
    far = (shift(lower_a[3], 1), shift(upper_b[3], -1))
    pieces = (mine, other)
    for i in (1, 2, 3):
        pieces += (lower_a[i], lower_b[i], upper_a[i], upper_b[i])
    pieces += far
    att_rows, column, stats = call(
        forward_kernel,
        (shape((SEC, 128), BF), wide, shape((NSEC, 8, 128), F32)),
        (place, *pieces, feat),
        flops=2 * 128 * 2 * pairs,
        transcendentals=pairs,
    )
    all_stats = lax.all_to_all(stats, Z, 0, 0, tiled=True).reshape(NSEC * 8, 128)
    half = shape((RUN, 128), BF)
    first, first_sent = call(
        functools.partial(queries_kernel, CHUNK),
        (half, half),
        (place, *pieces, feat, att_rows, column),
        flops=2 * 128 * 3 * pairs,
        transcendentals=pairs,
    )
    all_stats, first, first_sent = tie((all_stats, first, first_sent))
    second, sent = call(
        functools.partial(keys_kernel, CHUNK),
        (half, shape((SEC, 128), BF)),
        (place, *pieces, feat, all_stats, first_sent),
        scratch=(pltpu.VMEM((NSEC * 8, 128), F32), pltpu.SemaphoreType.DMA((NSEC,))),
        flops=2 * 128 * 4 * pairs,
        transcendentals=pairs,
    )
    back = swap(sent)
    partial = call(
        weights_kernel,
        shape((16, 96, 128), BF),
        (tok, tok_other, first, second, sent),
        flops=2 * 512 * 1024 * 256,
        smem=0,
    )
    partial = lax.all_to_all(partial, ("b",) + Z, 0, 0, tiled=True)
    att, keep, send = call(
        input_kernel,
        (half, shape((4, 32, 1024), F32), shape((4, 32, 1024), BF)),
        (place, first, second, back, wq, wk, wv),
        flops=6 * 256 * 1024 * 128,
    )
    partial, send = tie((partial, send))
    arrived = lax.ppermute(send, "core", [(0, 1), (1, 0)])
    total = call(sum_kernel, shape((32, 96, 128), BF), (partial,), smem=0)
    both = keep + arrived.astype(F32)
    share = lax.dynamic_index_in_dim(both, y, 0, False)
    both_bf = both.astype(BF)
    for k in (1, 2, 3):
        out = lax.dynamic_index_in_dim(both_bf, lax.bitwise_xor(y, k), 0, False)
        share = share + lax.ppermute(out, "y", [(i, i ^ k) for i in range(4)]).astype(F32)
    total = lax.all_to_all(total, ("b",) + CTX, 0, 0, tiled=True)
    gq, gk, gv = call(assemble_kernel, (shape((1024, 128), F32),) * 3, (total,), smem=0)
    return att[None], share.astype(BF)[None], gq, gk, gv


def solution(mesh):
    devices = mesh.devices.reshape(2, 2, 2, 2, 2, 4, 2)
    fine = Mesh(devices, ("b",) + CTX + TP)
    in_specs = (
        P("b", CTX, None),
        P(None, TP),
        P(None, TP),
        P(None, TP),
        P("b", CTX, TP),
        P("b", None),
        P("b", None),
    )
    out_specs = (
        P("b", CTX, TP),
        P("b", CTX + TP, None),
        P(None, TP),
        P(None, TP),
        P(None, TP),
    )
    return jax.shard_map(
        on_device, mesh=fine, in_specs=in_specs, out_specs=out_specs, check_vma=False
    )
```

```python
import functools
import math

import jax
import jax.numpy as jnp
from jax import lax
from jax.experimental import pallas as pl
from jax.experimental.pallas import tpu as pltpu
from jax.sharding import Mesh
from jax.sharding import PartitionSpec as P

HALF = 256
HD = 64
RUN = 256
SEC = 512
NSEC = 8
NEG = -1e30
LIMIT = 51 << 20
CHUNK = 512
FEATURE_LIMIT = 63 << 20
BF = jnp.bfloat16
F32 = jnp.float32

Z = ("z2", "z1", "z0")
CTX = Z + ("xh",)
TP = ("y", "core")

OFFSETS = (0, -1, 1, -2, 2, -3, 3, 4)

NN = (((1,), (0,)), ((), ()))
NT = (((1,), (1,)), ((), ()))
TN = (((0,), (0,)), ((), ()))


def dot(a, b, dims=NN):
    return lax.dot_general(a, b, dims, preferred_element_type=F32)


def call(kernel, outs, args, scratch=(), flops=0, transcendentals=0, smem=1, manual=0, limit=None):
    specs = [pl.BlockSpec(memory_space=pltpu.SMEM)] * smem
    specs += [pl.BlockSpec(memory_space=pl.ANY)] * manual
    specs += [pl.BlockSpec(memory_space=pltpu.VMEM)] * (len(args) - smem - manual)
    moved = sum(a.size * a.dtype.itemsize for a in args)
    return pl.pallas_call(
        kernel,
        out_shape=outs,
        in_specs=specs,
        out_specs=jax.tree.map(lambda _: pl.BlockSpec(memory_space=pltpu.VMEM), outs),
        scratch_shapes=list(scratch),
        compiler_params=pltpu.CompilerParams(vmem_limit_bytes=limit or LIMIT),
        cost_estimate=pl.CostEstimate(
            flops=flops, bytes_accessed=moved, transcendentals=transcendentals
        ),
    )(*args)


def low_lanes(rows):
    return lax.broadcasted_iota(jnp.int32, (rows, 128), 1) < HD


def feature_kernel(place, lengths, spots, feat):
    flip = place[0]
    lane = lax.broadcasted_iota(jnp.int32, (RUN, 128), 1)
    last = lane == HD + 8
    lane_row = lax.broadcasted_iota(jnp.int32, (1, 128), 1)
    starts, ends = jnp.zeros((1, 128), jnp.int32), jnp.zeros((1, 128), jnp.int32)
    start = jnp.int32(0)
    for d in range(8):
        end = start + lengths[0, d]
        starts = jnp.where(lane_row == HD + d, start, starts)
        ends = jnp.where(lane_row == HD + d, end, ends)
        start = end

    def one(block, carry):
        half = lax.rem(block, 2)
        run = (block - half) + jnp.where(half == flip, 0, 1)
        pos = run * RUN + lax.broadcasted_iota(jnp.int32, (RUN, RUN), 0)
        hit = jnp.max(jnp.where(pos == spots[...], 1.0, 0.0), axis=1, keepdims=True)
        other = 1.0 - hit
        pos128 = run * RUN + lax.broadcasted_iota(jnp.int32, (RUN, 128), 0)
        member = (pos128 >= starts) & (pos128 < ends)
        row = jnp.where(last, other, jnp.where(member, 1.0, 0.0))
        at = pl.ds(pl.multiple_of(block * RUN, RUN), RUN)
        feat[at, :] = row.astype(BF)
        return carry

    lax.fori_loop(0, 2 * NSEC, one, 0)


def project_kernel(tok, wq, wk, wv, cot, mine, theirs, *scratch):
    tok_v, wk_v, wv_v, wq_v, cot_v, sems = scratch
    pairs = ((tok, tok_v), (wk, wk_v), (wv, wv_v), (wq, wq_v), (cot, cot_v))
    copies = [pltpu.make_async_copy(a, b, sems.at[i]) for i, (a, b) in enumerate(pairs)]
    for copy in copies:
        copy.start()
    first = lax.axis_index("xh") == 0
    copies[0].wait()
    t = tok_v[...]
    copies[1].wait()
    k = dot(t, wk_v[...]).astype(BF)
    copies[2].wait()
    v = dot(t, wv_v[...]).astype(BF)
    copies[3].wait()
    q = dot(t, wq_v[...]).astype(BF)
    copies[4].wait()
    c = cot_v[...]
    kv0 = jnp.concatenate([k[:, :HD], v[:, :HD]], axis=1)
    kv1 = jnp.concatenate([k[:, HD:], v[:, HD:]], axis=1)
    qc0 = jnp.concatenate([q[:, :HD], c[:, :HD]], axis=1)
    qc1 = jnp.concatenate([q[:, HD:], c[:, HD:]], axis=1)

    @pl.when(first)
    def _():
        mine[:RUN] = kv0
        mine[RUN:] = qc0
        theirs[:RUN] = kv1
        theirs[RUN:] = qc1

    @pl.when(jnp.logical_not(first))
    def _():
        mine[:RUN] = kv1
        mine[RUN:] = qc1
        theirs[:RUN] = kv0
        theirs[RUN:] = qc0


def places(section, flip, along):
    shape = (1, SEC) if along == 1 else (SEC, 1)
    i = lax.broadcasted_iota(jnp.int32, shape, along)
    half = jnp.where(i >= RUN, 1 - flip, flip)
    return section * SEC + half * RUN + lax.bitwise_and(i, RUN - 1)


def section_at(own, offset):
    return lax.rem(own + offset + NSEC, NSEC)


def part_of(pieces, r, part):
    at = slice(part * RUN, (part + 1) * RUN)
    return jnp.concatenate([pieces[2 * r][at], pieces[2 * r + 1][at]], axis=0)


def features_at(feat, section):
    return feat[pl.ds(pl.multiple_of(section * SEC, SEC), SEC), :]


def join_key(kv, feat):
    lane = lax.broadcasted_iota(jnp.int32, kv.shape, 1)
    base = jnp.where(lane < HD + 8, 1.0, 0.0).astype(BF)
    sign = jnp.where(lane == HD + 8, 1.0, jnp.where(lane < HD + 8, -1.0, 0.0)).astype(BF)
    return jnp.where(lane < HD, kv, (base + sign * feat) * jnp.asarray(NEG, BF))


def join_query(qc, feat):
    low = lax.broadcasted_iota(jnp.int32, qc.shape, 1) < HD
    return jnp.where(low, qc * jnp.asarray(1.0 / math.sqrt(HD), BF), feat)


def less_global(joined):
    lane = lax.broadcasted_iota(jnp.int32, joined.shape, 1)
    return jnp.where(lane == HD + 8, jnp.zeros_like(joined), joined)


def right_half(rows):
    low = lax.broadcasted_iota(jnp.int32, rows.shape, 1) < HD
    return jnp.where(low, jnp.zeros_like(rows), rows)


def near_only(own, flip, r, own_places, near, plain):
    if r > 2:
        return plain
    away = own_places - places(section_at(own, OFFSETS[r]), flip, 1)
    return jnp.where(jnp.abs(away) <= HALF, near, plain)


def forward_kernel(place, *refs):
    pieces, (feat, att_out, column_out, stats) = refs[: 2 * NSEC], refs[2 * NSEC :]
    flip, own = place[0], place[1]
    own_qc = part_of(pieces, 0, 1)
    joined = join_query(own_qc, features_at(feat, own))
    near_rows = less_global(joined)
    row_places = places(own, flip, 0)

    def products(r):
        kp = join_key(part_of(pieces, r, 0), features_at(feat, section_at(own, OFFSETS[r])))
        return dot(joined, kp, NT), dot(near_rows, kp, NT) if r < 3 else None

    ahead = products(0)
    for r in range(NSEC):
        plain, near = ahead
        if r + 1 < NSEC:
            ahead = products(r + 1)
        s = near_only(own, flip, r, row_places, near, plain)
        new_peak = jnp.max(s, axis=1, keepdims=True)
        if r > 0:
            new_peak = jnp.maximum(peak, new_peak)
            keep = jnp.exp(peak - new_peak)
        e = jnp.exp(s - new_peak)
        new_total = jnp.sum(e, axis=1, keepdims=True)
        new_acc = dot(e.astype(BF), part_of(pieces, r, 0))
        if r > 0:
            new_total, new_acc = keep * total + new_total, keep * acc + new_acc
        peak, total, acc = new_peak, new_total, new_acc
    att = (acc / total).astype(BF)
    att_out[...] = att
    cot = right_half(own_qc).astype(F32)
    delta = jnp.sum(att.astype(F32) * cot, axis=1, keepdims=True)
    lanes = lax.broadcasted_iota(jnp.int32, (SEC, 128), 1)
    column = jnp.where(lanes == 0, peak + jnp.log(total), delta)
    column_out[...] = column
    turned = column.T
    for k in range(SEC // 128):
        for copy in range(NSEC):
            stats[copy, k : k + 1] = turned[0:1, k * 128 : (k + 1) * 128]
            stats[copy, 4 + k : 5 + k] = turned[1:2, k * 128 : (k + 1) * 128]


def queries_kernel(chunk, place, *refs):
    pieces, (feat, att, column, packed, packed_other) = refs[: 2 * NSEC], refs[2 * NSEC :]
    flip, own = place[0], place[1]
    own_qc = part_of(pieces, 0, 1)
    joined = join_query(own_qc, features_at(feat, own))
    near_rows, cot = less_global(joined), right_half(own_qc)
    row_places = places(own, flip, 0)
    count = SEC // chunk
    grads = [None] * count
    for r, offset in enumerate(OFFSETS):
        section = section_at(own, offset)
        kv = part_of(pieces, r, 0)
        kp = join_key(kv, features_at(feat, section))
        for c in range(count):
            rows = slice(c * chunk, (c + 1) * chunk)
            s = dot(joined[rows], kp, NT)
            if r < 3:
                away = row_places[rows] - places(section, flip, 1)
                s = jnp.where(jnp.abs(away) <= HALF, dot(near_rows[rows], kp, NT), s)
            p = jnp.exp(s - column[rows, 0:1])
            ds = p * (dot(cot[rows], kv, NT) - column[rows, 1:2])
            grad = dot(ds.astype(BF), kv)
            grads[c] = grad if r == 0 else grads[c] + grad
    grad = jnp.concatenate(grads, axis=0) if count > 1 else grads[0]
    grad = (grad * (1.0 / math.sqrt(HD))).astype(BF)
    out = jnp.where(low_lanes(SEC), grad, att[...])
    packed[...] = out[:RUN]
    packed_other[...] = out[RUN:]


def keys_kernel(chunk, place, *refs):
    pieces, (feat, stats, given, packed, sent, stats_s, sems) = refs[: 2 * NSEC], refs[2 * NSEC :]
    flip, own = place[0], place[1]
    copies = []
    for r, offset in enumerate(OFFSETS):
        at = pl.multiple_of(section_at(own, offset) * 8, 8)
        to = stats_s.at[pl.ds(r * 8, 8)]
        copies.append(pltpu.make_async_copy(stats.at[pl.ds(at, 8)], to, sems.at[r]))
        copies[-1].start()
    own_kv = part_of(pieces, 0, 0)
    joined = join_key(own_kv, features_at(feat, own))
    near_keys, value = less_global(joined), right_half(own_kv)
    key_places = places(own, flip, 0)
    count = SEC // chunk
    state = [None] * count
    for copy in copies:
        copy.wait()
    for r, offset in enumerate(OFFSETS):
        section = section_at(own, offset)
        qc = part_of(pieces, r, 1)
        qp = join_query(qc, features_at(feat, section))
        st = stats_s[r * 8 : r * 8 + 8]
        log_total = jnp.concatenate([st[i : i + 1] for i in range(4)], axis=1)
        delta = jnp.concatenate([st[i : i + 1] for i in range(4, 8)], axis=1)
        for c in range(count):
            rows = slice(c * chunk, (c + 1) * chunk)
            s = dot(joined[rows], qp, NT)
            if r < 3:
                away = key_places[rows] - places(section, flip, 1)
                s = jnp.where(jnp.abs(away) <= HALF, dot(near_keys[rows], qp, NT), s)
            p = jnp.exp(s - log_total)
            ds = p * (dot(value[rows], qc, NT) - delta)
            both = dot(ds.astype(BF), qc), dot(p.astype(BF), qc)
            state[c] = both if r == 0 else (state[c][0] + both[0], state[c][1] + both[1])
    key_acc = jnp.concatenate([x[0] for x in state], axis=0) if count > 1 else state[0][0]
    value_acc = jnp.concatenate([x[1] for x in state], axis=0) if count > 1 else state[0][1]
    out = jnp.where(low_lanes(SEC), key_acc * (1.0 / math.sqrt(HD)), value_acc).astype(BF)
    packed[...] = out[:RUN]
    sent[:RUN] = given[...]
    sent[RUN:] = out[RUN:]


def weights_kernel(tok, tok_other, first, second, sent, out):
    qa = dot(tok[...], first[...], TN) + dot(tok_other[...], sent[:RUN], TN)
    kv = dot(tok[...], second[...], TN) + dot(tok_other[...], sent[RUN:], TN)
    for p in range(16):
        out[p, :64] = kv[p * 64 : (p + 1) * 64].astype(BF)
        upper = qa[p * 32 : (p + 1) * 32, :HD]
        lower = qa[512 + p * 32 : 512 + (p + 1) * 32, :HD]
        out[p, 64:96] = jnp.concatenate([upper, lower], axis=1).astype(BF)


def sum_kernel(parts, out):
    total = parts[0].astype(F32)
    for p in range(1, 16):
        total = total + parts[p].astype(F32)
    total = total.astype(BF)
    for p in range(32):
        out[p] = total


def input_kernel(place, first, second, arrived, wq, wk, wv, att, keep, send):
    swap = place[0] != 0
    core = place[2]
    a, b, c, d = first[...], arrived[:RUN], second[...], arrived[RUN:]
    a, b = jnp.where(swap, b, a), jnp.where(swap, a, b)
    c, d = jnp.where(swap, d, c), jnp.where(swap, c, d)
    dq = jnp.concatenate([a[:, :HD], b[:, :HD]], axis=1)
    att[...] = jnp.concatenate([a[:, HD:], b[:, HD:]], axis=1)
    dk = jnp.concatenate([c[:, :HD], d[:, :HD]], axis=1)
    dv = jnp.concatenate([c[:, HD:], d[:, HD:]], axis=1)
    grad = dot(dq, wq[...], NT) + dot(dk, wk[...], NT) + dot(dv, wv[...], NT)
    for y in range(4):
        low, high = grad[y * 64 : y * 64 + 32], grad[y * 64 + 32 : y * 64 + 64]
        keep[y] = jnp.where(core == 0, low, high)
        send[y] = jnp.where(core == 0, high, low).astype(BF)


def assemble_kernel(parts, gq, gk, gv):
    for p in range(16):
        a, b = parts[2 * p].astype(F32), parts[2 * p + 1].astype(F32)
        low = jnp.concatenate([a[:, :HD], b[:, :HD]], axis=1)
        high = jnp.concatenate([a[:, HD:], b[:, HD:]], axis=1)
        gk[p * 64 : (p + 1) * 64] = low[:64]
        gv[p * 64 : (p + 1) * 64] = high[:64]
        gq[p * 32 : (p + 1) * 32] = low[64:]
        gq[512 + p * 32 : 512 + (p + 1) * 32] = high[64:]


def shift(a, step):
    return lax.ppermute(a, Z, [(i, (i + step) % NSEC) for i in range(NSEC)])


def swap(a):
    return lax.ppermute(a, "xh", [(0, 1), (1, 0)])


def on_device(tokens, wq, wk, wv, cotangent, doc_lengths, global_positions):
    shape = jax.ShapeDtypeStruct
    tok, cot = tokens[0], cotangent[0]
    xh, z, y, core = (lax.axis_index(a) for a in ("xh", Z, "y", "core"))
    place = jnp.stack([xh, z, core]).astype(jnp.int32)
    weight = pltpu.VMEM((1024, 128), BF)
    mine, theirs = call(
        project_kernel,
        (shape((SEC, 128), BF),) * 2,
        (tok, wq, wk, wv, cot),
        scratch=(
            pltpu.VMEM((RUN, 1024), BF),
            weight,
            weight,
            weight,
            pltpu.VMEM((RUN, 128), BF),
            pltpu.SemaphoreType.DMA((5,)),
        ),
        flops=6 * 256 * 1024 * 128,
        smem=0,
        manual=5,
        limit=63 << 20,
    )
    other = swap(theirs)
    tok_other = swap(tok)
    pairs = SEC * SEC * NSEC
    wide = shape((SEC, 128), F32)

    tie = lax.optimization_barrier
    lower_a, upper_a = [mine, shift(mine, 1)], [mine, shift(mine, -1)]
    late, mine = tie((place, mine))
    feat = call(
        feature_kernel,
        shape((NSEC * SEC, 128), BF),
        (late, doc_lengths, global_positions),
        smem=2,
        limit=FEATURE_LIMIT,
    )
    other, feat, lower_a[1], upper_a[1] = tie((other, feat, lower_a[1], upper_a[1]))
    lower_b, upper_b = [other, shift(other, 1)], [other, shift(other, -1)]
    for x, step in ((lower_a, 1), (upper_a, -1), (lower_b, 1), (upper_b, -1)):
        x.append(shift(x[1], step))
    for x, step in ((lower_a, 1), (upper_a, -1), (lower_b, 1), (upper_b, -1)):
        x.append(shift(x[2], step))
    far = (shift(lower_a[3], 1), shift(upper_b[3], -1))
    pieces = (mine, other)
    for i in (1, 2, 3):
        pieces += (lower_a[i], lower_b[i], upper_a[i], upper_b[i])
    pieces += far
    att_rows, column, stats = call(
        forward_kernel,
        (shape((SEC, 128), BF), wide, shape((NSEC, 8, 128), F32)),
        (place, *pieces, feat),
        flops=2 * 128 * 2 * pairs,
        transcendentals=pairs,
    )
    all_stats = lax.all_to_all(stats, Z, 0, 0, tiled=True).reshape(NSEC * 8, 128)
    half = shape((RUN, 128), BF)
    first, first_sent = call(
        functools.partial(queries_kernel, CHUNK),
        (half, half),
        (place, *pieces, feat, att_rows, column),
        flops=2 * 128 * 3 * pairs,
        transcendentals=pairs,
    )
    all_stats, first, first_sent = tie((all_stats, first, first_sent))
    second, sent = call(
        functools.partial(keys_kernel, CHUNK),
        (half, shape((SEC, 128), BF)),
        (place, *pieces, feat, all_stats, first_sent),
        scratch=(pltpu.VMEM((NSEC * 8, 128), F32), pltpu.SemaphoreType.DMA((NSEC,))),
        flops=2 * 128 * 4 * pairs,
        transcendentals=pairs,
    )
    back = swap(sent)
    partial = call(
        weights_kernel,
        shape((16, 96, 128), BF),
        (tok, tok_other, first, second, sent),
        flops=2 * 512 * 1024 * 256,
        smem=0,
    )
    partial = lax.all_to_all(partial, ("b",) + Z, 0, 0, tiled=True)
    att, keep, send = call(
        input_kernel,
        (half, shape((4, 32, 1024), F32), shape((4, 32, 1024), BF)),
        (place, first, second, back, wq, wk, wv),
        flops=6 * 256 * 1024 * 128,
    )
    partial, send = tie((partial, send))
    arrived = lax.ppermute(send, "core", [(0, 1), (1, 0)])
    total = call(sum_kernel, shape((32, 96, 128), BF), (partial,), smem=0)
    both = keep + arrived.astype(F32)
    share = lax.dynamic_index_in_dim(both, y, 0, False)
    both_bf = both.astype(BF)
    for k in (1, 2, 3):
        out = lax.dynamic_index_in_dim(both_bf, lax.bitwise_xor(y, k), 0, False)
        share = share + lax.ppermute(out, "y", [(i, i ^ k) for i in range(4)]).astype(F32)
    total = lax.all_to_all(total, ("b",) + CTX, 0, 0, tiled=True)
    gq, gk, gv = call(assemble_kernel, (shape((1024, 128), F32),) * 3, (total,), smem=0)
    return att[None], share.astype(BF)[None], gq, gk, gv


def solution(mesh):
    devices = mesh.devices.reshape(2, 2, 2, 2, 2, 4, 2)
    fine = Mesh(devices, ("b",) + CTX + TP)
    in_specs = (
        P("b", CTX, None),
        P(None, TP),
        P(None, TP),
        P(None, TP),
        P("b", CTX, TP),
        P("b", None),
        P("b", None),
    )
    out_specs = (
        P("b", CTX, TP),
        P("b", CTX + TP, None),
        P(None, TP),
        P(None, TP),
        P(None, TP),
    )
    return jax.shard_map(
        on_device, mesh=fine, in_specs=in_specs, out_specs=out_specs, check_vma=False
    )
```
